32 devices in a mesh: seq: 2 (over x), expert: 4 (over y, core), mp: 4 (over z).
Axes of the slice: x: 2, y: 2, z: 4, core: 2. Of those that a mesh axis runs over, the one named last changes fastest.
Arguments:
- tokens: bfloat16 [256, 6144], P(('seq', 'expert', 'mp')), may hold values from -6 to 6
- out_grad: bfloat16 [256, 6144], P(('seq', 'expert', 'mp')), may hold values from -3 to 3
- kept_mask: int32 [256], P(('seq', 'expert', 'mp')), may hold values 0 or 1
- routes: int32 [256, 2], P(('seq', 'expert', 'mp')), may hold values from 0 to 3, all different within a row; in each aligned block of 8 rows (0 to 7, 8 to 15, ...) at most 4 rows name the same one
- router: bfloat16 [6144, 4], replicated, may hold values from -0.078125 to 0.078125
- gate_weight: bfloat16 [4, 6144, 8192], P('expert', None, ('seq', 'mp')), may hold values from -0.078125 to 0.078125
- up_weight: bfloat16 [4, 6144, 8192], P('expert', None, ('seq', 'mp')), may hold values from -0.078125 to 0.078125
- down_weight: bfloat16 [4, 8192, 6144], P('expert', ('seq', 'mp')), may hold values from -0.0625 to 0.0625
Outputs:
- d_tokens: bfloat16 [256, 6144], P(('seq', 'expert', 'mp'))
- gate_grad: float32 [256, 2], P(('seq', 'expert', 'mp'))
The draws below stay inside these ranges and needn't reach their ends.
Inputs may be any that keep to these rules, and one draw needn't show every extreme that they name: `routes`: among the 8 rows of one device, at most 4 name any one expert, and in every draw some expert is named by exactly 4 rows of some device.
All inputs are finite; a program needn't handle non-finite values. No bound on the sum of `kept_mask` on one device may be relied on, other than what follows from the above.
Results may differ from the reference program's by a relative error of at most 0.02.
Values may be sent and summed in bfloat16 or wider, within the bound.
No kernel may reach another device: no remote copies, remote signals or barrier semaphores. Data moves between devices by JAX's collectives and lax.ppermute only.
A program may use at most 128 MiB of HBM per device.

```python
import math
import jax
import jax.numpy as jnp
import numpy as np
from jax import lax

D = 6144
FF = 8192
TOK_DEV = 8
EXPERTS = 4
TOKENS = 256
CAP = 4
N_SEQ = 2
N_MP = 4


def with_ends(result, key, smallest, high):
    spot = [jax.random.randint(jax.random.fold_in(key, axis), (), 0, length) for axis, length in enumerate(result.shape)]
    longest = result.shape.index(max(result.shape))
    next_to = spot[:longest] + [(spot[longest] + 1) % result.shape[longest]] + spot[longest + 1:]
    return result.at[tuple(spot)].set(smallest).at[tuple(next_to)].set(high)


def steps_of(own_key, dims, shards, smallest, largest):
    factor_of = 1.0
    for dim, shards_of in shards:
        steps = jax.random.uniform(jax.random.fold_in(jax.random.fold_in(own_key, 6), dim), (shards_of,), jnp.float32, smallest / len(shards), largest / len(shards))
        factor_of = factor_of * jnp.repeat(jnp.exp(steps), dims[dim] // shards_of).reshape((-1,) + (1,) * (len(dims) - 1 - dim))
    return factor_of


def deal_out(rng, own, number, rows, number_of, top, most, slope):
    ranking = jax.random.permutation(rng, number_of)
    crowded, usual = shares(number_of, rows * top, most, slope, True), shares(number_of, rows * top, most, slope, False)
    places = jnp.arange(number_of)

    def named(tallies, offset_by):
        used = int((tallies > 0).sum())
        fixed = max(1, used // 4)
        passed = fixed + (places - fixed + offset_by * (used - fixed)) % max(1, number_of - fixed)
        return jnp.zeros((number_of,), jnp.int32).at[ranking[jnp.where(places < fixed, places, passed)]].set(jnp.asarray(tallies, jnp.int32))

    tallies = jnp.where(number % 4 == 0, named(crowded, number // 4), named(usual, number - number // 4 - 1))
    mixed = jax.random.permutation(jax.random.fold_in(own, 3), number_of)
    giver, receiver = mixed[0:number_of // 2 * 2:2], mixed[1:number_of // 2 * 2:2]
    room = jnp.minimum(tallies[giver] - 1, most - tallies[receiver]) // 2
    room = jnp.where((giver == ranking[0]) | (receiver == ranking[0]) | (tallies[receiver] == 0), 0, jnp.maximum(room, 0))
    passed = jax.random.randint(jax.random.fold_in(own, 4), (number_of // 2,), 0, 1 << 20) % (room + 1)
    tallies = tallies.at[giver].add(-passed).at[receiver].add(passed)
    members = jnp.searchsorted(jnp.cumsum(tallies), jnp.arange(rows * top), side="right").astype(jnp.int32)
    table = members.reshape(top, rows).T
    table = table[jax.random.permutation(jax.random.fold_in(own, 1), rows)]
    offset_by = jax.random.randint(jax.random.fold_in(own, 2), (rows, 1), 0, top)
    return jnp.take_along_axis(table, (jnp.arange(top)[None, :] + offset_by) % top, axis=1)


def shares(amount, total, limit, slope, full):
    portions = [(1 << 20) // math.isqrt(standing ** slope) + 1 for standing in range(1, amount + 1)]
    largest = limit if full else min(limit, max(-(-total // amount), total * portions[0] // sum(portions)))
    least = 1 if total - largest >= amount - 1 else 0
    holding, surplus = [largest] + [least] * (amount - 1), total - largest - least * (amount - 1)
    while surplus > 0:
        free = [i for i in range(1, amount) if holding[i] < largest] or [i for i in range(1, amount) if holding[i] < limit]
        pool, remaining = sum([portions[i] for i in free]), surplus
        for i in free:
            addition = min(limit - holding[i], max(1, remaining * portions[i] // pool), surplus)
            holding[i] = holding[i] + addition
            surplus = surplus - addition
    return np.array(holding)


def noise(rng, dims, scale, bound, shards=(), kind=jnp.bfloat16):
    gain = steps_of(rng, dims, shards, -0.22, 0.18) if shards else 1.0
    entries = jax.random.normal(rng, dims, jnp.float32) * scale * gain
    return jnp.minimum(jnp.maximum(entries, -bound), bound).astype(kind)


def setup_inputs(seed: int = 0) -> dict:
    key_list = jax.random.split(jax.random.key(seed), 9)
    tokens = noise(key_list[0], (TOKENS, D), 1.0, 6.0, ((0, 32),))
    out_grad = noise(key_list[1], (TOKENS, D), 0.5, 3.0, ((0, 32),))
    kept_mask = with_ends((jax.random.randint(key_list[2], (TOKENS,), 0, 5) < 4).astype(jnp.int32), jax.random.fold_in(key_list[2], 1), 0, 1)
    routes_keys = jax.random.split(jax.random.fold_in(key_list[3], 1), TOKENS // TOK_DEV)
    routes_turns = jax.random.permutation(jax.random.fold_in(key_list[3], 3), TOKENS // TOK_DEV)
    routes = jax.vmap(lambda own, number: deal_out(jax.random.fold_in(key_list[3], 2), own, number, TOK_DEV, EXPERTS, 2, CAP, 1))(routes_keys, routes_turns).reshape((TOKENS, 2))
    router = noise(key_list[4], (D, EXPERTS), D ** -0.5, 0.078125)
    gate_weight = noise(key_list[5], (EXPERTS, D, FF), D ** -0.5, 0.078125, ((0, 4), (2, 8)))
    up_weight = noise(key_list[6], (EXPERTS, D, FF), D ** -0.5, 0.078125, ((0, 4), (2, 8)))
    down_weight = noise(key_list[7], (EXPERTS, FF, D), FF ** -0.5, 0.0625, ((0, 4), (1, 8)))
    return dict(tokens=tokens, out_grad=out_grad, kept_mask=kept_mask, routes=routes, router=router, gate_weight=gate_weight, up_weight=up_weight, down_weight=down_weight)


def expert_pass(token_rows, grad_rows, gate_rows, gate_mat, up_mat, down_mat):
    pre_gate = jnp.dot(token_rows, gate_mat, preferred_element_type=jnp.float32)
    pre_up = jnp.dot(token_rows, up_mat, preferred_element_type=jnp.float32)
    sigma = jax.nn.sigmoid(pre_gate)
    act = pre_gate * sigma
    hidden = act * pre_up
    grad_hidden = jnp.dot(grad_rows, down_mat.T, preferred_element_type=jnp.float32)
    gate_dot = jnp.sum(grad_hidden * hidden, axis=1)
    scaled = gate_rows.astype(jnp.float32)[:, None] * grad_hidden
    grad_gate = (scaled * pre_up * sigma * (1.0 + pre_gate * (1.0 - sigma))).astype(jnp.bfloat16)
    grad_up = (scaled * act).astype(jnp.bfloat16)
    blocks = N_SEQ * N_MP
    width = FF // blocks

    def add_block(total, block_index):
        start = (block_index * width).astype(jnp.int32)
        left_gate = lax.dynamic_slice_in_dim(grad_gate, start, width, 1)
        left_up = lax.dynamic_slice_in_dim(grad_up, start, width, 1)
        right_gate = lax.dynamic_slice_in_dim(gate_mat, start, width, 1)
        right_up = lax.dynamic_slice_in_dim(up_mat, start, width, 1)
        part = jnp.dot(left_gate, right_gate.T, preferred_element_type=jnp.float32)
        part = part + jnp.dot(left_up, right_up.T, preferred_element_type=jnp.float32)
        rounded = lax.optimization_barrier(part.astype(jnp.bfloat16))
        return total + rounded.astype(jnp.float32), None

    start_total = jnp.zeros((token_rows.shape[0], token_rows.shape[1]), jnp.float32)
    expert_grad, _ = lax.scan(add_block, start_total, jnp.arange(blocks, dtype=jnp.int32))
    return expert_grad, gate_dot


def reference(tokens, out_grad, kept_mask, routes, router, gate_weight, up_weight, down_weight):
    logits = jnp.dot(tokens, router, preferred_element_type=jnp.float32)
    first_id = routes[:, 0].astype(jnp.int32)
    second_id = routes[:, 1].astype(jnp.int32)
    first_logit = jnp.take_along_axis(logits, first_id[:, None], axis=1)[:, 0]
    second_logit = jnp.take_along_axis(logits, second_id[:, None], axis=1)[:, 0]
    gate_first = jax.nn.sigmoid(first_logit - second_logit)
    gate_second = jax.nn.sigmoid(second_logit - first_logit)
    keep_rows = kept_mask.astype(jnp.float32)
    most_rows = (TOKENS // TOK_DEV) * CAP

    def per_expert(carry, inputs):
        grad_total, dot_total = carry
        expert_id, gate_mat, up_mat, down_mat = inputs
        hit = (kept_mask == 1) & ((first_id == expert_id) | (second_id == expert_id))
        hit = hit.astype(jnp.int32)
        order = jnp.argsort(1 - hit, stable=True)[:most_rows].astype(jnp.int32)
        live = hit[order].astype(jnp.float32)
        gate_rows = jnp.where(first_id == expert_id, gate_first, gate_second).astype(jnp.bfloat16)[order]
        expert_grad, gate_dot = expert_pass(tokens[order], out_grad[order], gate_rows, gate_mat, up_mat, down_mat)
        grad_total = grad_total.at[order].add(expert_grad * live[:, None])
        dot_total = dot_total.at[order, expert_id].add(gate_dot * live)
        return (grad_total, dot_total), None

    start = (jnp.zeros((TOKENS, D), jnp.float32), jnp.zeros((TOKENS, EXPERTS), jnp.float32))
    (grad_total, dot_total), _ = lax.scan(per_expert, start, (jnp.arange(EXPERTS, dtype=jnp.int32), gate_weight, up_weight, down_weight))
    dot_first = jnp.take_along_axis(dot_total, first_id[:, None], axis=1)[:, 0]
    dot_second = jnp.take_along_axis(dot_total, second_id[:, None], axis=1)[:, 0]
    product = gate_first * gate_second * keep_rows
    grad_first = product * (dot_first - dot_second)
    grad_second = product * (dot_second - dot_first)
    columns = lax.broadcasted_iota(jnp.int32, (TOKENS, EXPERTS), 1)
    first_hot = (first_id[:, None] == columns).astype(jnp.float32)
    second_hot = (second_id[:, None] == columns).astype(jnp.float32)
    logit_grad = first_hot * grad_first[:, None] + second_hot * grad_second[:, None]
    router_term = jnp.dot(logit_grad, router.astype(jnp.float32).T, precision=lax.Precision.HIGHEST)
    d_tokens = ((grad_total + router_term) * keep_rows[:, None]).astype(jnp.bfloat16)
    gate_grad = jnp.stack([grad_first, grad_second], axis=1)
    return d_tokens, gate_grad
```

```python
import jax
import jax.numpy as jnp
from jax import lax
from jax.sharding import PartitionSpec as P


def routed_plan(tokens, out_grad, kept_mask, routes, router, gate_weight, up_weight, down_weight):
    row_count = tokens.shape[0]
    width = tokens.shape[1]
    expert_count = lax.axis_size("expert")
    capacity = max(3 * row_count // 8, 2 * row_count // expert_count)
    logits = jnp.dot(tokens, router, preferred_element_type=jnp.float32)
    columns = lax.broadcasted_iota(jnp.int32, (row_count, expert_count), 1)
    first_hot = (routes[:, 0:1] == columns).astype(jnp.float32)
    second_hot = (routes[:, 1:2] == columns).astype(jnp.float32)
    first_logit = jnp.sum(logits * first_hot, axis=1)
    second_logit = jnp.sum(logits * second_hot, axis=1)
    gate_first = jax.nn.sigmoid(first_logit - second_logit)
    gate_second = jax.nn.sigmoid(second_logit - first_logit)
    keep_rows = kept_mask.astype(jnp.float32)
    chosen = ((first_hot + second_hot) * keep_rows[:, None]).astype(jnp.int32)
    position = jnp.cumsum(chosen, axis=0) - 1
    slot_iota = lax.broadcasted_iota(jnp.int32, (row_count, expert_count, capacity), 2)
    select_mask = (chosen[:, :, None] == 1) & (position[:, :, None] == slot_iota)
    select_bf = select_mask.astype(jnp.bfloat16)
    select_full = select_mask.astype(jnp.float32)
    token_send = jnp.einsum(
        "tec,td->ecd", select_bf, tokens, preferred_element_type=jnp.float32
    ).astype(jnp.bfloat16)
    grad_send = jnp.einsum(
        "tec,td->ecd", select_bf, out_grad, preferred_element_type=jnp.float32
    ).astype(jnp.bfloat16)
    gate_table = first_hot * gate_first[:, None] + second_hot * gate_second[:, None]
    gate_send = jnp.einsum(
        "tec,te->ec", select_full, gate_table, precision=lax.Precision.HIGHEST
    ).astype(jnp.bfloat16)
    token_recv, grad_recv, gate_recv = (
        lax.all_to_all(token_send, "expert", split_axis=0, concat_axis=0, tiled=True),
        lax.all_to_all(grad_send, "expert", split_axis=0, concat_axis=0, tiled=True),
        lax.all_to_all(gate_send, "expert", split_axis=0, concat_axis=0, tiled=True),
    )
    token_all, grad_all, gate_all = (
        lax.all_gather(token_recv, ("seq", "mp"), axis=0, tiled=True),
        lax.all_gather(grad_recv, ("seq", "mp"), axis=0, tiled=True),
        lax.all_gather(gate_recv, ("seq", "mp"), axis=0, tiled=True),
    )
    token_all = token_all.reshape(-1, width)
    grad_all = grad_all.reshape(-1, width)
    gate_all = gate_all.reshape(-1)
    gate_local = gate_weight[0]
    up_local = up_weight[0]
    down_local = down_weight[0]
    pre_gate = jnp.dot(token_all, gate_local, preferred_element_type=jnp.float32)
    pre_up = jnp.dot(token_all, up_local, preferred_element_type=jnp.float32)
    sigma = jax.nn.sigmoid(pre_gate)
    act = pre_gate * sigma
    hidden = act * pre_up
    grad_hidden = jnp.dot(grad_all, down_local.T, preferred_element_type=jnp.float32)
    gate_dot = jnp.sum(grad_hidden * hidden, axis=1)
    scaled = gate_all.astype(jnp.float32)[:, None] * grad_hidden
    grad_gate = (scaled * pre_up * sigma * (1.0 + pre_gate * (1.0 - sigma))).astype(jnp.bfloat16)
    grad_up = (scaled * act).astype(jnp.bfloat16)
    expert_grad = jnp.dot(grad_gate, gate_local.T, preferred_element_type=jnp.float32)
    expert_grad = expert_grad + jnp.dot(grad_up, up_local.T, preferred_element_type=jnp.float32)
    grad_own = lax.psum_scatter(
        expert_grad.astype(jnp.bfloat16), ("seq", "mp"), scatter_dimension=0, tiled=True
    ).astype(jnp.float32)
    dot_own = lax.psum_scatter(gate_dot, ("seq", "mp"), scatter_dimension=0, tiled=True)
    grad_back, dot_back = (
        lax.all_to_all(
            grad_own.reshape(expert_count, capacity, width).astype(jnp.bfloat16),
            "expert",
            split_axis=0,
            concat_axis=0,
            tiled=True,
        ).astype(jnp.float32),
        lax.all_to_all(
            dot_own.reshape(expert_count, capacity).astype(jnp.bfloat16),
            "expert",
            split_axis=0,
            concat_axis=0,
            tiled=True,
        ).astype(jnp.float32),
    )
    expert_sum = jnp.einsum("tec,ecd->td", select_full, grad_back, precision=lax.Precision.HIGHEST)
    dot_table = jnp.einsum("tec,ec->te", select_full, dot_back, precision=lax.Precision.HIGHEST)
    dot_first = jnp.sum(dot_table * first_hot, axis=1)
    dot_second = jnp.sum(dot_table * second_hot, axis=1)
    product = gate_first * gate_second * keep_rows
    grad_first = product * (dot_first - dot_second)
    grad_second = product * (dot_second - dot_first)
    logit_grad = first_hot * grad_first[:, None] + second_hot * grad_second[:, None]
    router_term = jnp.dot(logit_grad, router.astype(jnp.float32).T, precision=lax.Precision.HIGHEST)
    d_tokens = ((expert_sum + router_term) * keep_rows[:, None]).astype(jnp.bfloat16)
    gate_grad = jnp.stack([grad_first, grad_second], axis=1)
    return (d_tokens, gate_grad)

def shift(value, axis, step):
    size = lax.axis_size(axis)
    return lax.ppermute(value, axis, [((i + step) % size, i) for i in range(size)])


def swap(value, axis, bit):
    return lax.ppermute(value, axis, [(i ^ bit, i) for i in range(lax.axis_size(axis))])


def swap_x(value):
    return swap(value, "seq", 1)


def swap_y(value):
    return swap(value, "expert", 2)


def swap_core(value):
    return swap(value, "expert", 1)


def gather(rows):
    columns = rows.shape[1] // 256 * 128
    z_rows = jnp.concatenate([rows] + [shift(rows, "mp", k) for k in range(1, lax.axis_size("mp"))], axis=0)
    halves = []
    for half, first, second in ((z_rows[:, :columns], swap_x, swap_y), (z_rows[:, columns:], swap_y, swap_x)):
        near = first(half)
        far = second(jnp.concatenate([half, near], axis=0))
        far = jnp.split(far, 2, axis=0)
        blocks = [half, near] + far if first is swap_x else [half, far[0], near, far[1]]
        mine = jnp.concatenate(blocks, axis=0)
        halves.append(jnp.concatenate([mine, swap_core(mine)], axis=0))
    return halves


def scatter_half(partial, first, second):
    rows = partial.shape[0] // 2
    total = partial[:rows].astype(jnp.float32) + swap_core(partial[rows:]).astype(jnp.float32)
    own, by_x, by_y, by_both = jnp.split(total, 4, axis=0)
    near, far = (by_x, [by_y, by_both]) if first is swap_x else (by_y, [by_x, by_both])
    rest = second(jnp.concatenate(far, axis=0).astype(jnp.bfloat16)).astype(jnp.float32)
    rest_own, rest_near = jnp.split(rest, 2, axis=0)
    return own + rest_own + first((near + rest_near).astype(jnp.bfloat16)).astype(jnp.float32)


def scatter_z(total):
    size = lax.axis_size("mp")
    rows = total.shape[0] // size
    result = total[:rows]
    for k in range(1, size):
        result = result + shift(total[k * rows:(k + 1) * rows].astype(jnp.bfloat16), "mp", size - k).astype(jnp.float32)
    return result


def gathered_plan(tokens, out_grad, kept_mask, routes, router, gate_weight, up_weight, down_weight):
    row_count, width = tokens.shape
    expert_count = lax.axis_size("expert")
    columns = lax.broadcasted_iota(jnp.int32, (row_count, expert_count), 1)
    first_hot = (routes[:, 0:1] == columns).astype(jnp.float32)
    second_hot = (routes[:, 1:2] == columns).astype(jnp.float32)
    keep_rows = kept_mask.astype(jnp.float32)
    token_halves = gather(tokens)
    logits = jnp.dot(tokens, router, preferred_element_type=jnp.float32)
    first_logit = jnp.sum(logits * first_hot, axis=1)
    second_logit = jnp.sum(logits * second_hot, axis=1)
    gate_first = jax.nn.sigmoid(first_logit - second_logit)
    gate_second = jax.nn.sigmoid(second_logit - first_logit)
    gate_table = (first_hot * gate_first[:, None] + second_hot * gate_second[:, None]) * keep_rows[:, None]
    gate_table = jnp.pad(gate_table.astype(jnp.bfloat16), ((0, 0), (0, 256 - expert_count)))
    grad_halves = gather(jnp.concatenate([gate_table, out_grad], axis=1))
    half = width // 2
    expert = lax.axis_index("expert")
    first_grad = grad_halves[0][:, 256:]
    gates = grad_halves[0][:, :expert_count].astype(jnp.float32)
    gate_all = jnp.sum(jnp.where(lax.broadcasted_iota(jnp.int32, gates.shape, 1) == expert, gates, 0.0), axis=1)
    second_grad = grad_halves[1]
    gate_local, up_local, down_local = gate_weight[0], up_weight[0], down_weight[0]

    def dot(a, b):
        return jnp.dot(a, b, preferred_element_type=jnp.float32)

    token_all = jnp.concatenate(token_halves, axis=1)
    grad_all = jnp.concatenate([first_grad, second_grad], axis=1)
    pre_gate = dot(token_all, gate_local)
    pre_up = dot(token_all, up_local)
    sigma = jax.nn.sigmoid(pre_gate)
    act = pre_gate * sigma
    hidden = act * pre_up
    grad_hidden = dot(grad_all, down_local.T)
    gate_dot = jnp.sum(grad_hidden * hidden, axis=1)
    scaled = gate_all[:, None] * grad_hidden
    grad_gate = (scaled * pre_up * sigma * (1.0 + pre_gate * (1.0 - sigma))).astype(jnp.bfloat16)
    grad_up = (scaled * act).astype(jnp.bfloat16)
    dots = jnp.where(lax.broadcasted_iota(jnp.int32, (gate_dot.shape[0], 128), 1) == expert, gate_dot[:, None], 0.0)
    low = dot(grad_gate, gate_local[:half].T) + dot(grad_up, up_local[:half].T)
    high = dot(grad_gate, gate_local[half:].T) + dot(grad_up, up_local[half:].T)
    low = scatter_half(jnp.concatenate([low.astype(jnp.bfloat16), dots.astype(jnp.bfloat16)], axis=1), swap_x, swap_y)
    high = scatter_half(high.astype(jnp.bfloat16), swap_y, swap_x)
    total = scatter_z(jnp.concatenate([low, high], axis=1))
    expert_sum = jnp.concatenate([total[:, :half], total[:, half + 128:]], axis=1)
    dot_table = total[:, half:half + expert_count]
    dot_first = jnp.sum(dot_table * first_hot, axis=1)
    dot_second = jnp.sum(dot_table * second_hot, axis=1)
    product = gate_first * gate_second * keep_rows
    grad_first = product * (dot_first - dot_second)
    grad_second = product * (dot_second - dot_first)
    logit_grad = first_hot * grad_first[:, None] + second_hot * grad_second[:, None]
    router_term = jnp.dot(logit_grad, router.astype(jnp.float32).T, precision=lax.Precision.HIGHEST)
    d_tokens = ((expert_sum + router_term) * keep_rows[:, None]).astype(jnp.bfloat16)
    gate_grad = jnp.stack([grad_first, grad_second], axis=1)
    return (d_tokens, gate_grad)


def solution(mesh):
    gathers = mesh.shape["seq"] == 2 and mesh.shape["expert"] == 4
    return jax.shard_map(
        gathered_plan if gathers else routed_plan,
        mesh=mesh,
        in_specs=(
            P(("seq", "expert", "mp"), None),
            P(("seq", "expert", "mp"), None),
            P(("seq", "expert", "mp")),
            P(("seq", "expert", "mp"), None),
            P(),
            P("expert", None, ("seq", "mp")),
            P("expert", None, ("seq", "mp")),
            P("expert", ("seq", "mp"), None),
        ),
        out_specs=(P(("seq", "expert", "mp"), None), P(("seq", "expert", "mp"), None)),
        check_vma=False,
    )
```

```python
import jax
import jax.numpy as jnp
from jax import lax
from jax.sharding import PartitionSpec as P


def routed_plan(tokens, out_grad, kept_mask, routes, router, gate_weight, up_weight, down_weight):
    row_count = tokens.shape[0]
    width = tokens.shape[1]
    expert_count = lax.axis_size("expert")
    capacity = max(3 * row_count // 8, 2 * row_count // expert_count)
    logits = jnp.dot(tokens, router, preferred_element_type=jnp.float32)
    columns = lax.broadcasted_iota(jnp.int32, (row_count, expert_count), 1)
    first_hot = (routes[:, 0:1] == columns).astype(jnp.float32)
    second_hot = (routes[:, 1:2] == columns).astype(jnp.float32)
    first_logit = jnp.sum(logits * first_hot, axis=1)
    second_logit = jnp.sum(logits * second_hot, axis=1)
    gate_first = jax.nn.sigmoid(first_logit - second_logit)
    gate_second = jax.nn.sigmoid(second_logit - first_logit)
    keep_rows = kept_mask.astype(jnp.float32)
    chosen = ((first_hot + second_hot) * keep_rows[:, None]).astype(jnp.int32)
    position = jnp.cumsum(chosen, axis=0) - 1
    slot_iota = lax.broadcasted_iota(jnp.int32, (row_count, expert_count, capacity), 2)
    select_mask = (chosen[:, :, None] == 1) & (position[:, :, None] == slot_iota)
    select_bf = select_mask.astype(jnp.bfloat16)
    select_full = select_mask.astype(jnp.float32)
    token_send = jnp.einsum(
        "tec,td->ecd", select_bf, tokens, preferred_element_type=jnp.float32
    ).astype(jnp.bfloat16)
    grad_send = jnp.einsum(
        "tec,td->ecd", select_bf, out_grad, preferred_element_type=jnp.float32
    ).astype(jnp.bfloat16)
    gate_table = first_hot * gate_first[:, None] + second_hot * gate_second[:, None]
    gate_send = jnp.einsum(
        "tec,te->ec", select_full, gate_table, precision=lax.Precision.HIGHEST
    ).astype(jnp.bfloat16)
    token_recv, grad_recv, gate_recv = (
        lax.all_to_all(token_send, "expert", split_axis=0, concat_axis=0, tiled=True),
        lax.all_to_all(grad_send, "expert", split_axis=0, concat_axis=0, tiled=True),
        lax.all_to_all(gate_send, "expert", split_axis=0, concat_axis=0, tiled=True),
    )
    token_all, grad_all, gate_all = (
        lax.all_gather(token_recv, ("seq", "mp"), axis=0, tiled=True),
        lax.all_gather(grad_recv, ("seq", "mp"), axis=0, tiled=True),
        lax.all_gather(gate_recv, ("seq", "mp"), axis=0, tiled=True),
    )
    token_all = token_all.reshape(-1, width)
    grad_all = grad_all.reshape(-1, width)
    gate_all = gate_all.reshape(-1)
    gate_local = gate_weight[0]
    up_local = up_weight[0]
    down_local = down_weight[0]
    pre_gate = jnp.dot(token_all, gate_local, preferred_element_type=jnp.float32)
    pre_up = jnp.dot(token_all, up_local, preferred_element_type=jnp.float32)
    sigma = jax.nn.sigmoid(pre_gate)
    act = pre_gate * sigma
    hidden = act * pre_up
    grad_hidden = jnp.dot(grad_all, down_local.T, preferred_element_type=jnp.float32)
    gate_dot = jnp.sum(grad_hidden * hidden, axis=1)
    scaled = gate_all.astype(jnp.float32)[:, None] * grad_hidden
    grad_gate = (scaled * pre_up * sigma * (1.0 + pre_gate * (1.0 - sigma))).astype(jnp.bfloat16)
    grad_up = (scaled * act).astype(jnp.bfloat16)
    expert_grad = jnp.dot(grad_gate, gate_local.T, preferred_element_type=jnp.float32)
    expert_grad = expert_grad + jnp.dot(grad_up, up_local.T, preferred_element_type=jnp.float32)
    grad_own = lax.psum_scatter(
        expert_grad.astype(jnp.bfloat16), ("seq", "mp"), scatter_dimension=0, tiled=True
    ).astype(jnp.float32)
    dot_own = lax.psum_scatter(gate_dot, ("seq", "mp"), scatter_dimension=0, tiled=True)
    grad_back, dot_back = (
        lax.all_to_all(
            grad_own.reshape(expert_count, capacity, width).astype(jnp.bfloat16),
            "expert",
            split_axis=0,
            concat_axis=0,
            tiled=True,
        ).astype(jnp.float32),
        lax.all_to_all(
            dot_own.reshape(expert_count, capacity).astype(jnp.bfloat16),
            "expert",
            split_axis=0,
            concat_axis=0,
            tiled=True,
        ).astype(jnp.float32),
    )
    expert_sum = jnp.einsum("tec,ecd->td", select_full, grad_back, precision=lax.Precision.HIGHEST)
    dot_table = jnp.einsum("tec,ec->te", select_full, dot_back, precision=lax.Precision.HIGHEST)
    dot_first = jnp.sum(dot_table * first_hot, axis=1)
    dot_second = jnp.sum(dot_table * second_hot, axis=1)
    product = gate_first * gate_second * keep_rows
    grad_first = product * (dot_first - dot_second)
    grad_second = product * (dot_second - dot_first)
    logit_grad = first_hot * grad_first[:, None] + second_hot * grad_second[:, None]
    router_term = jnp.dot(logit_grad, router.astype(jnp.float32).T, precision=lax.Precision.HIGHEST)
    d_tokens = ((expert_sum + router_term) * keep_rows[:, None]).astype(jnp.bfloat16)
    gate_grad = jnp.stack([grad_first, grad_second], axis=1)
    return (d_tokens, gate_grad)

def shift(value, axis, step):
    size = lax.axis_size(axis)
    return lax.ppermute(value, axis, [((i + step) % size, i) for i in range(size)])


def swap(value, axis, bit):
    return lax.ppermute(value, axis, [(i ^ bit, i) for i in range(lax.axis_size(axis))])


def swap_x(value):
    return swap(value, "seq", 1)


def swap_y(value):
    return swap(value, "expert", 2)


def swap_core(value):
    return swap(value, "expert", 1)


def gather_z(rows):
    return [rows] + [shift(rows, "mp", k) for k in range(1, lax.axis_size("mp"))]


def gather_rest(z_rows):
    z_rows = jnp.concatenate(z_rows, axis=0)
    columns = z_rows.shape[1] // 256 * 128
    halves = []
    for half, first, second in ((z_rows[:, :columns], swap_x, swap_y), (z_rows[:, columns:], swap_y, swap_x)):
        near = first(half)
        far = second(jnp.concatenate([half, near], axis=0))
        far = jnp.split(far, 2, axis=0)
        blocks = [half, near] + far if first is swap_x else [half, far[0], near, far[1]]
        mine = jnp.concatenate(blocks, axis=0)
        halves.append(jnp.concatenate([mine, swap_core(mine)], axis=0))
    return halves


def scatter_half(partial, first, second):
    rows = partial.shape[0] // 2
    total = partial[:rows].astype(jnp.float32) + swap_core(partial[rows:]).astype(jnp.float32)
    own, by_x, by_y, by_both = jnp.split(total, 4, axis=0)
    near, far = (by_x, [by_y, by_both]) if first is swap_x else (by_y, [by_x, by_both])
    rest = second(jnp.concatenate(far, axis=0).astype(jnp.bfloat16)).astype(jnp.float32)
    rest_own, rest_near = jnp.split(rest, 2, axis=0)
    return own + rest_own + first((near + rest_near).astype(jnp.bfloat16)).astype(jnp.float32)


def scatter_z(total):
    size = lax.axis_size("mp")
    rows = total.shape[0] // size
    result = total[:rows]
    for k in range(1, size):
        result = result + shift(total[k * rows:(k + 1) * rows].astype(jnp.bfloat16), "mp", size - k).astype(jnp.float32)
    return result


def gathered_plan(tokens, out_grad, kept_mask, routes, router, gate_weight, up_weight, down_weight):
    row_count, width = tokens.shape
    expert_count = lax.axis_size("expert")
    columns = lax.broadcasted_iota(jnp.int32, (row_count, expert_count), 1)
    first_hot = (routes[:, 0:1] == columns).astype(jnp.float32)
    second_hot = (routes[:, 1:2] == columns).astype(jnp.float32)
    keep_rows = kept_mask.astype(jnp.float32)
    token_z = gather_z(tokens)
    logits = jnp.dot(tokens, router, preferred_element_type=jnp.float32)
    first_logit = jnp.sum(logits * first_hot, axis=1)
    second_logit = jnp.sum(logits * second_hot, axis=1)
    gate_first = jax.nn.sigmoid(first_logit - second_logit)
    gate_second = jax.nn.sigmoid(second_logit - first_logit)
    gate_table = (first_hot * gate_first[:, None] + second_hot * gate_second[:, None]) * keep_rows[:, None]
    gate_table = jnp.pad(gate_table.astype(jnp.bfloat16), ((0, 0), (0, 256 - expert_count)))
    grad_rows, token_z[1] = lax.optimization_barrier((jnp.concatenate([gate_table, out_grad], axis=1), token_z[1]))
    grad_z = gather_z(grad_rows)
    token_halves = gather_rest(token_z)
    grad_halves = gather_rest(grad_z)
    half = width // 2
    expert = lax.axis_index("expert")
    first_grad = grad_halves[0][:, 256:]
    gates = grad_halves[0][:, :expert_count].astype(jnp.float32)
    gate_all = jnp.sum(jnp.where(lax.broadcasted_iota(jnp.int32, gates.shape, 1) == expert, gates, 0.0), axis=1)
    second_grad = grad_halves[1]
    gate_local, up_local, down_local = gate_weight[0], up_weight[0], down_weight[0]

    def dot(a, b):
        return jnp.dot(a, b, preferred_element_type=jnp.float32)

    token_all = jnp.concatenate(token_halves, axis=1)
    grad_all = jnp.concatenate([first_grad, second_grad], axis=1)
    pre_gate = dot(token_all, gate_local)
    pre_up = dot(token_all, up_local)
    sigma = jax.nn.sigmoid(pre_gate)
    act = pre_gate * sigma
    hidden = act * pre_up
    grad_hidden = dot(grad_all, down_local.T)
    gate_dot = jnp.sum(grad_hidden * hidden, axis=1)
    scaled = gate_all[:, None] * grad_hidden
    grad_gate = (scaled * pre_up * sigma * (1.0 + pre_gate * (1.0 - sigma))).astype(jnp.bfloat16)
    grad_up = (scaled * act).astype(jnp.bfloat16)
    dots = jnp.where(lax.broadcasted_iota(jnp.int32, (gate_dot.shape[0], 128), 1) == expert, gate_dot[:, None], 0.0)
    low = dot(grad_gate, gate_local[:half].T) + dot(grad_up, up_local[:half].T)
    low = jnp.concatenate([low.astype(jnp.bfloat16), dots.astype(jnp.bfloat16)], axis=1)
    low, grad_gate, grad_up = lax.optimization_barrier((low, grad_gate, grad_up))
    high = dot(grad_gate, gate_local[half:].T) + dot(grad_up, up_local[half:].T)
    low = scatter_z(scatter_half(low, swap_x, swap_y))
    high = scatter_z(scatter_half(high.astype(jnp.bfloat16), swap_y, swap_x))
    expert_sum = jnp.concatenate([low[:, :half], high], axis=1)
    dot_table = low[:, half:half + expert_count]
    dot_first = jnp.sum(dot_table * first_hot, axis=1)
    dot_second = jnp.sum(dot_table * second_hot, axis=1)
    product = gate_first * gate_second * keep_rows
    grad_first = product * (dot_first - dot_second)
    grad_second = product * (dot_second - dot_first)
    logit_grad = first_hot * grad_first[:, None] + second_hot * grad_second[:, None]
    router_term = jnp.dot(logit_grad, router.astype(jnp.float32).T, precision=lax.Precision.HIGHEST)
    d_tokens = ((expert_sum + router_term) * keep_rows[:, None]).astype(jnp.bfloat16)
    gate_grad = jnp.stack([grad_first, grad_second], axis=1)
    return (d_tokens, gate_grad)


def solution(mesh):
    gathers = mesh.shape["seq"] == 2 and mesh.shape["expert"] == 4
    return jax.shard_map(
        gathered_plan if gathers else routed_plan,
        mesh=mesh,
        in_specs=(
            P(("seq", "expert", "mp"), None),
            P(("seq", "expert", "mp"), None),
            P(("seq", "expert", "mp")),
            P(("seq", "expert", "mp"), None),
            P(),
            P("expert", None, ("seq", "mp")),
            P("expert", None, ("seq", "mp")),
            P("expert", ("seq", "mp"), None),
        ),
        out_specs=(P(("seq", "expert", "mp"), None), P(("seq", "expert", "mp"), None)),
        check_vma=False,
    )
```

```python
import functools
import math

import jax
import jax.numpy as jnp
from jax import lax
from jax.experimental import pallas as pl
from jax.experimental.pallas import tpu as pltpu
from jax.sharding import PartitionSpec as P

TOKEN_PART = 512
HIDDEN_PART = 256
COLUMN_PART = 512
TOKEN_VMEM = 16 * 2 ** 20
GRAD_VMEM = 20 * 2 ** 20
OUTPUT_VMEM = 16 * 2 ** 20


def routed_plan(tokens, out_grad, kept_mask, routes, router, gate_weight, up_weight, down_weight):
    row_count = tokens.shape[0]
    width = tokens.shape[1]
    expert_count = lax.axis_size("expert")
    capacity = max(3 * row_count // 8, 2 * row_count // expert_count)
    logits = jnp.dot(tokens, router, preferred_element_type=jnp.float32)
    columns = lax.broadcasted_iota(jnp.int32, (row_count, expert_count), 1)
    first_hot = (routes[:, 0:1] == columns).astype(jnp.float32)
    second_hot = (routes[:, 1:2] == columns).astype(jnp.float32)
    first_logit = jnp.sum(logits * first_hot, axis=1)
    second_logit = jnp.sum(logits * second_hot, axis=1)
    gate_first = jax.nn.sigmoid(first_logit - second_logit)
    gate_second = jax.nn.sigmoid(second_logit - first_logit)
    keep_rows = kept_mask.astype(jnp.float32)
    chosen = ((first_hot + second_hot) * keep_rows[:, None]).astype(jnp.int32)
    position = jnp.cumsum(chosen, axis=0) - 1
    slot_iota = lax.broadcasted_iota(jnp.int32, (row_count, expert_count, capacity), 2)
    select_mask = (chosen[:, :, None] == 1) & (position[:, :, None] == slot_iota)
    select_bf = select_mask.astype(jnp.bfloat16)
    select_full = select_mask.astype(jnp.float32)
    token_send = jnp.einsum(
        "tec,td->ecd", select_bf, tokens, preferred_element_type=jnp.float32
    ).astype(jnp.bfloat16)
    grad_send = jnp.einsum(
        "tec,td->ecd", select_bf, out_grad, preferred_element_type=jnp.float32
    ).astype(jnp.bfloat16)
    gate_table = first_hot * gate_first[:, None] + second_hot * gate_second[:, None]
    gate_send = jnp.einsum(
        "tec,te->ec", select_full, gate_table, precision=lax.Precision.HIGHEST
    ).astype(jnp.bfloat16)
    token_recv, grad_recv, gate_recv = (
        lax.all_to_all(token_send, "expert", split_axis=0, concat_axis=0, tiled=True),
        lax.all_to_all(grad_send, "expert", split_axis=0, concat_axis=0, tiled=True),
        lax.all_to_all(gate_send, "expert", split_axis=0, concat_axis=0, tiled=True),
    )
    token_all, grad_all, gate_all = (
        lax.all_gather(token_recv, ("seq", "mp"), axis=0, tiled=True),
        lax.all_gather(grad_recv, ("seq", "mp"), axis=0, tiled=True),
        lax.all_gather(gate_recv, ("seq", "mp"), axis=0, tiled=True),
    )
    token_all = token_all.reshape(-1, width)
    grad_all = grad_all.reshape(-1, width)
    gate_all = gate_all.reshape(-1)
    gate_local = gate_weight[0]
    up_local = up_weight[0]
    down_local = down_weight[0]
    pre_gate = jnp.dot(token_all, gate_local, preferred_element_type=jnp.float32)
    pre_up = jnp.dot(token_all, up_local, preferred_element_type=jnp.float32)
    sigma = jax.nn.sigmoid(pre_gate)
    act = pre_gate * sigma
    hidden = act * pre_up
    grad_hidden = jnp.dot(grad_all, down_local.T, preferred_element_type=jnp.float32)
    gate_dot = jnp.sum(grad_hidden * hidden, axis=1)
    scaled = gate_all.astype(jnp.float32)[:, None] * grad_hidden
    grad_gate = (scaled * pre_up * sigma * (1.0 + pre_gate * (1.0 - sigma))).astype(jnp.bfloat16)
    grad_up = (scaled * act).astype(jnp.bfloat16)
    expert_grad = jnp.dot(grad_gate, gate_local.T, preferred_element_type=jnp.float32)
    expert_grad = expert_grad + jnp.dot(grad_up, up_local.T, preferred_element_type=jnp.float32)
    grad_own = lax.psum_scatter(
        expert_grad.astype(jnp.bfloat16), ("seq", "mp"), scatter_dimension=0, tiled=True
    ).astype(jnp.float32)
    dot_own = lax.psum_scatter(gate_dot, ("seq", "mp"), scatter_dimension=0, tiled=True)
    grad_back, dot_back = (
        lax.all_to_all(
            grad_own.reshape(expert_count, capacity, width).astype(jnp.bfloat16),
            "expert",
            split_axis=0,
            concat_axis=0,
            tiled=True,
        ).astype(jnp.float32),
        lax.all_to_all(
            dot_own.reshape(expert_count, capacity).astype(jnp.bfloat16),
            "expert",
            split_axis=0,
            concat_axis=0,
            tiled=True,
        ).astype(jnp.float32),
    )
    expert_sum = jnp.einsum("tec,ecd->td", select_full, grad_back, precision=lax.Precision.HIGHEST)
    dot_table = jnp.einsum("tec,ec->te", select_full, dot_back, precision=lax.Precision.HIGHEST)
    dot_first = jnp.sum(dot_table * first_hot, axis=1)
    dot_second = jnp.sum(dot_table * second_hot, axis=1)
    product = gate_first * gate_second * keep_rows
    grad_first = product * (dot_first - dot_second)
    grad_second = product * (dot_second - dot_first)
    logit_grad = first_hot * grad_first[:, None] + second_hot * grad_second[:, None]
    router_term = jnp.dot(logit_grad, router.astype(jnp.float32).T, precision=lax.Precision.HIGHEST)
    d_tokens = ((expert_sum + router_term) * keep_rows[:, None]).astype(jnp.bfloat16)
    gate_grad = jnp.stack([grad_first, grad_second], axis=1)
    return (d_tokens, gate_grad)

def shift(value, axis, step):
    size = lax.axis_size(axis)
    return lax.ppermute(value, axis, [((i + step) % size, i) for i in range(size)])


def swap(value, axis, bit):
    return lax.ppermute(value, axis, [(i ^ bit, i) for i in range(lax.axis_size(axis))])


def swap_x(value):
    return swap(value, "seq", 1)


def swap_y(value):
    return swap(value, "expert", 2)


def swap_core(value):
    return swap(value, "expert", 1)


def gather_z(rows):
    return [rows] + [shift(rows, "mp", k) for k in range(1, lax.axis_size("mp"))]


def gather_near(z_rows, cut):
    rows = jnp.concatenate(z_rows, axis=0)
    low, high = rows[:, :cut], rows[:, cut:]
    return [low, swap_x(low)], [high, swap_y(high)]


def gather_far(low, high):
    return swap_y(jnp.concatenate(low, axis=0)), swap_x(jnp.concatenate(high, axis=0))


def gather_core(low, low_far, high, high_far):
    high_far = jnp.split(high_far, 2, axis=0)
    low = jnp.concatenate(low + [low_far], axis=0)
    high = jnp.concatenate([high[0], high_far[0], high[1], high_far[1]], axis=0)
    return tuple(jnp.concatenate([mine, swap_core(mine)], axis=0) for mine in (low, high))


def scatter_half(kept, sent, first, second):
    total = kept + swap_core(sent).astype(jnp.float32)
    own, by_x, by_y, by_both = jnp.split(total, 4, axis=0)
    near, far = (by_x, [by_y, by_both]) if first is swap_x else (by_y, [by_x, by_both])
    rest = second(jnp.concatenate(far, axis=0).astype(jnp.bfloat16)).astype(jnp.float32)
    rest_own, rest_near = jnp.split(rest, 2, axis=0)
    return own + rest_own + first((near + rest_near).astype(jnp.bfloat16)).astype(jnp.float32)


def scatter_z(total):
    size = lax.axis_size("mp")
    rows = total.shape[0] // size
    result = total[:rows]
    for k in range(1, size):
        result = result + shift(total[k * rows:(k + 1) * rows].astype(jnp.bfloat16), "mp", size - k).astype(jnp.float32)
    return result


def product(a, b, b_dim):
    return lax.dot_general(a, b, (((1,), (b_dim,)), ((), ())), preferred_element_type=jnp.float32)


def part_of(length, wanted):
    return math.gcd(length, wanted)


def token_kernel(low, high, gate_weight, up_weight, pre_gate, pre_up, gate_copy, up_copy, gate_sems, up_sems):
    half = low.shape[1]
    depth = part_of(half, TOKEN_PART)
    steps = half // depth

    def copies(index):
        rows = pl.ds(pl.multiple_of(index * depth, depth), depth)
        return (
            pltpu.make_async_copy(gate_weight.at[0, rows], gate_copy.at[rows], gate_sems.at[index]),
            pltpu.make_async_copy(up_weight.at[0, rows], up_copy.at[rows], up_sems.at[index]),
        )

    @pl.loop(0, 2 * steps)
    def _(index):
        for copy in copies(index):
            copy.start()

    pre_gate[...] = jnp.zeros_like(pre_gate)
    pre_up[...] = jnp.zeros_like(pre_up)
    for first, part in ((0, low), (steps, high)):

        @pl.loop(0, steps)
        def _(step):
            for copy in copies(first + step):
                copy.wait()
            rows = pl.ds(pl.multiple_of((first + step) * depth, depth), depth)
            values = part[:, pl.ds(pl.multiple_of(step * depth, depth), depth)]
            pre_gate[...] += product(values, gate_copy[rows, :], 0)
            pre_up[...] += product(values, up_copy[rows, :], 0)


def multiply_tokens(low, high, gate_weight, up_weight):
    rows, half = low.shape
    width, hidden = gate_weight.shape[1:]
    steps = width // part_of(half, TOKEN_PART)
    return pl.pallas_call(
        token_kernel,
        out_shape=(
            pltpu.VMEM((rows, hidden), jnp.float32),
            pltpu.VMEM((rows, hidden), jnp.float32),
            pltpu.VMEM((width, hidden), jnp.bfloat16),
            pltpu.VMEM((width, hidden), jnp.bfloat16),
        ),
        in_specs=[pl.BlockSpec(memory_space=pltpu.VMEM)] * 2 + [pl.BlockSpec(memory_space=pl.ANY)] * 2,
        out_specs=(pl.BlockSpec(memory_space=pltpu.VMEM),) * 4,
        scratch_shapes=[pltpu.SemaphoreType.DMA((steps,)), pltpu.SemaphoreType.DMA((steps,))],
        compiler_params=pltpu.CompilerParams(vmem_limit_bytes=TOKEN_VMEM),
        cost_estimate=pl.CostEstimate(
            flops=4 * rows * width * hidden, bytes_accessed=4 * width * hidden, transcendentals=0
        ),
    )(low, high, gate_weight, up_weight)


def grad_kernel(
    expert, low, high, pre_gate, pre_up, down_weight, grad_gate, grad_up, dots, gate_rows, dot_sums, down, down_sems
):
    table = low.shape[1] - high.shape[1]
    half = high.shape[1]
    hidden = down.shape[0]
    depth = part_of(hidden, HIDDEN_PART)
    steps = hidden // depth

    def copy_of(index):
        rows = pl.ds(pl.multiple_of(index * depth, depth), depth)
        return pltpu.make_async_copy(down_weight.at[0, rows], down.at[rows], down_sems.at[index])

    @pl.loop(0, steps)
    def _(index):
        copy_of(index).start()

    lanes = lax.broadcasted_iota(jnp.int32, (low.shape[0], table), 1)
    gate_rows[...] = jnp.sum(
        jnp.where(lanes == expert[0], low[:, :table].astype(jnp.float32), 0.0), axis=1, keepdims=True
    )
    dot_sums[...] = jnp.zeros_like(dot_sums)

    @pl.loop(0, steps)
    def _(step):
        copy_of(step).wait()
        span = pl.ds(pl.multiple_of(step * depth, depth), depth)
        grad_hidden = product(low[:, table:], down[span, :half], 1) + product(high[...], down[span, half:], 1)
        gates = pre_gate[:, span]
        ups = pre_up[:, span]
        sigma = jax.nn.sigmoid(gates)
        act = gates * sigma
        dot_sums[...] += jnp.sum(grad_hidden * (act * ups), axis=1, keepdims=True)
        scaled = gate_rows[...] * grad_hidden
        grad_gate[:, span] = (scaled * ups * sigma * (1.0 + gates * (1.0 - sigma))).astype(jnp.bfloat16)
        grad_up[:, span] = (scaled * act).astype(jnp.bfloat16)

    dots[...] = jnp.where(lanes == expert[0], dot_sums[...], 0.0).astype(jnp.bfloat16)


def multiply_grads(expert, low, high, pre_gate, pre_up, down_weight):
    rows, hidden = pre_gate.shape
    width = down_weight.shape[2]
    table = low.shape[1] - high.shape[1]
    return pl.pallas_call(
        grad_kernel,
        out_shape=(
            pltpu.VMEM((rows, hidden), jnp.bfloat16),
            pltpu.VMEM((rows, hidden), jnp.bfloat16),
            pltpu.VMEM((rows, table), jnp.bfloat16),
        ),
        in_specs=[pl.BlockSpec(memory_space=pltpu.SMEM)]
        + [pl.BlockSpec(memory_space=pltpu.VMEM)] * 4
        + [pl.BlockSpec(memory_space=pl.ANY)],
        out_specs=(pl.BlockSpec(memory_space=pltpu.VMEM),) * 3,
        scratch_shapes=[
            pltpu.VMEM((rows, 1), jnp.float32),
            pltpu.VMEM((rows, 1), jnp.float32),
            pltpu.VMEM((hidden, width), jnp.bfloat16),
            pltpu.SemaphoreType.DMA((hidden // part_of(hidden, HIDDEN_PART),)),
        ],
        compiler_params=pltpu.CompilerParams(vmem_limit_bytes=GRAD_VMEM),
        cost_estimate=pl.CostEstimate(
            flops=2 * rows * width * hidden, bytes_accessed=2 * width * hidden, transcendentals=rows * hidden
        ),
    )(expert, low, high, pre_gate, pre_up, down_weight)


def output_kernel(first, grad_gate, grad_up, gate_copy, up_copy, *refs):
    dots, kept, sent = refs if len(refs) == 3 else (None,) + refs
    rows = kept.shape[0]
    columns = kept.shape[1] - (0 if dots is None else dots.shape[1])
    part = part_of(columns, COLUMN_PART)

    @pl.loop(0, columns // part)
    def _(step):
        span = pl.ds(pl.multiple_of(first + step * part, part), part)
        place = pl.ds(pl.multiple_of(step * part, part), part)
        result = product(grad_gate[...], gate_copy[span, :], 1) + product(grad_up[...], up_copy[span, :], 1)
        kept[:, place] = result[:rows]
        sent[:, place] = result[rows:].astype(jnp.bfloat16)

    if dots is not None:
        kept[:, columns:] = dots[:rows, :].astype(jnp.float32)
        sent[:, columns:] = dots[rows:, :]


def multiply_outputs(first, columns, grad_gate, grad_up, gate_copy, up_copy, *dots):
    rows, hidden = grad_gate.shape
    total = columns + sum(value.shape[1] for value in dots)
    return pl.pallas_call(
        functools.partial(output_kernel, first),
        out_shape=(
            pltpu.VMEM((rows // 2, total), jnp.float32),
            pltpu.VMEM((rows // 2, total), jnp.bfloat16),
        ),
        in_specs=[pl.BlockSpec(memory_space=pltpu.VMEM)] * (4 + len(dots)),
        out_specs=(pl.BlockSpec(memory_space=pltpu.VMEM),) * 2,
        compiler_params=pltpu.CompilerParams(vmem_limit_bytes=OUTPUT_VMEM),
        cost_estimate=pl.CostEstimate(
            flops=4 * rows * columns * hidden, bytes_accessed=4 * rows * columns, transcendentals=0
        ),
    )(grad_gate, grad_up, gate_copy, up_copy, *dots)


def gathered_plan(tokens, out_grad, kept_mask, routes, router, gate_weight, up_weight, down_weight):
    row_count, width = tokens.shape
    expert_count = lax.axis_size("expert")
    columns = lax.broadcasted_iota(jnp.int32, (row_count, expert_count), 1)
    first_hot = (routes[:, 0:1] == columns).astype(jnp.float32)
    second_hot = (routes[:, 1:2] == columns).astype(jnp.float32)
    keep_rows = kept_mask.astype(jnp.float32)
    half = width // 2
    table = 128
    token_z = gather_z(tokens)
    logits = jnp.dot(tokens, router, preferred_element_type=jnp.float32)
    first_logit = jnp.sum(logits * first_hot, axis=1)
    second_logit = jnp.sum(logits * second_hot, axis=1)
    gate_first = jax.nn.sigmoid(first_logit - second_logit)
    gate_second = jax.nn.sigmoid(second_logit - first_logit)
    gate_table = (first_hot * gate_first[:, None] + second_hot * gate_second[:, None]) * keep_rows[:, None]
    gate_table = jnp.pad(gate_table.astype(jnp.bfloat16), ((0, 0), (0, table - expert_count)))
    grad_rows, token_z[1] = lax.optimization_barrier((jnp.concatenate([gate_table, out_grad], axis=1), token_z[1]))
    grad_z = gather_z(grad_rows)
    token_near = gather_near(token_z, half)
    token_far = gather_far(*token_near)
    grad_z, token_far = lax.optimization_barrier((grad_z, token_far))
    grad_near = gather_near(grad_z, half + table)
    token_halves = gather_core(token_near[0], token_far[0], token_near[1], token_far[1])
    grad_far = gather_far(*grad_near)
    pre_gate, pre_up, gate_copy, up_copy = multiply_tokens(*token_halves, gate_weight, up_weight)
    grad_far, pre_gate = lax.optimization_barrier((grad_far, pre_gate))
    grad_halves = gather_core(grad_near[0], grad_far[0], grad_near[1], grad_far[1])
    expert = lax.axis_index("expert").astype(jnp.int32).reshape(1)
    grad_gate, grad_up, dots = multiply_grads(expert, *grad_halves, pre_gate, pre_up, down_weight)
    kept, sent = multiply_outputs(0, half, grad_gate, grad_up, gate_copy, up_copy, dots)
    sent, grad_gate = lax.optimization_barrier((sent, grad_gate))
    low = scatter_z(scatter_half(kept, sent, swap_x, swap_y))
    kept, sent = multiply_outputs(half, half, grad_gate, grad_up, gate_copy, up_copy)
    high = scatter_z(scatter_half(kept, sent, swap_y, swap_x))
    expert_sum = jnp.concatenate([low[:, :half], high], axis=1)
    dot_table = low[:, half:half + expert_count]
    dot_first = jnp.sum(dot_table * first_hot, axis=1)
    dot_second = jnp.sum(dot_table * second_hot, axis=1)
    product = gate_first * gate_second * keep_rows
    grad_first = product * (dot_first - dot_second)
    grad_second = product * (dot_second - dot_first)
    logit_grad = first_hot * grad_first[:, None] + second_hot * grad_second[:, None]
    router_term = jnp.dot(logit_grad, router.astype(jnp.float32).T, precision=lax.Precision.HIGHEST)
    d_tokens = ((expert_sum + router_term) * keep_rows[:, None]).astype(jnp.bfloat16)
    gate_grad = jnp.stack([grad_first, grad_second], axis=1)
    return (d_tokens, gate_grad)


def solution(mesh):
    gathers = mesh.shape["seq"] == 2 and mesh.shape["expert"] == 4
    return jax.shard_map(
        gathered_plan if gathers else routed_plan,
        mesh=mesh,
        in_specs=(
            P(("seq", "expert", "mp"), None),
            P(("seq", "expert", "mp"), None),
            P(("seq", "expert", "mp")),
            P(("seq", "expert", "mp"), None),
            P(),
            P("expert", None, ("seq", "mp")),
            P("expert", None, ("seq", "mp")),
            P("expert", ("seq", "mp"), None),
        ),
        out_specs=(P(("seq", "expert", "mp"), None), P(("seq", "expert", "mp"), None)),
        check_vma=False,
    )
```

```python
import functools
import math

import jax
import jax.numpy as jnp
from jax import lax
from jax.experimental import pallas as pl
from jax.experimental.pallas import tpu as pltpu
from jax.sharding import PartitionSpec as P

TOKEN_PART = 512
HIDDEN_PART = 256
COLUMN_PART = 512
TOKEN_VMEM = 16 * 2 ** 20
GRAD_VMEM = 20 * 2 ** 20
OUTPUT_VMEM = 16 * 2 ** 20


def routed_plan(tokens, out_grad, kept_mask, routes, router, gate_weight, up_weight, down_weight):
    row_count = tokens.shape[0]
    width = tokens.shape[1]
    expert_count = lax.axis_size("expert")
    capacity = max(3 * row_count // 8, 2 * row_count // expert_count)
    logits = jnp.dot(tokens, router, preferred_element_type=jnp.float32)
    columns = lax.broadcasted_iota(jnp.int32, (row_count, expert_count), 1)
    first_hot = (routes[:, 0:1] == columns).astype(jnp.float32)
    second_hot = (routes[:, 1:2] == columns).astype(jnp.float32)
    first_logit = jnp.sum(logits * first_hot, axis=1)
    second_logit = jnp.sum(logits * second_hot, axis=1)
    gate_first = jax.nn.sigmoid(first_logit - second_logit)
    gate_second = jax.nn.sigmoid(second_logit - first_logit)
    keep_rows = kept_mask.astype(jnp.float32)
    chosen = ((first_hot + second_hot) * keep_rows[:, None]).astype(jnp.int32)
    position = jnp.cumsum(chosen, axis=0) - 1
    slot_iota = lax.broadcasted_iota(jnp.int32, (row_count, expert_count, capacity), 2)
    select_mask = (chosen[:, :, None] == 1) & (position[:, :, None] == slot_iota)
    select_bf = select_mask.astype(jnp.bfloat16)
    select_full = select_mask.astype(jnp.float32)
    token_send = jnp.einsum(
        "tec,td->ecd", select_bf, tokens, preferred_element_type=jnp.float32
    ).astype(jnp.bfloat16)
    grad_send = jnp.einsum(
        "tec,td->ecd", select_bf, out_grad, preferred_element_type=jnp.float32
    ).astype(jnp.bfloat16)
    gate_table = first_hot * gate_first[:, None] + second_hot * gate_second[:, None]
    gate_send = jnp.einsum(
        "tec,te->ec", select_full, gate_table, precision=lax.Precision.HIGHEST
    ).astype(jnp.bfloat16)
    token_recv, grad_recv, gate_recv = (
        lax.all_to_all(token_send, "expert", split_axis=0, concat_axis=0, tiled=True),
        lax.all_to_all(grad_send, "expert", split_axis=0, concat_axis=0, tiled=True),
        lax.all_to_all(gate_send, "expert", split_axis=0, concat_axis=0, tiled=True),
    )
    token_all, grad_all, gate_all = (
        lax.all_gather(token_recv, ("seq", "mp"), axis=0, tiled=True),
        lax.all_gather(grad_recv, ("seq", "mp"), axis=0, tiled=True),
        lax.all_gather(gate_recv, ("seq", "mp"), axis=0, tiled=True),
    )
    token_all = token_all.reshape(-1, width)
    grad_all = grad_all.reshape(-1, width)
    gate_all = gate_all.reshape(-1)
    gate_local = gate_weight[0]
    up_local = up_weight[0]
    down_local = down_weight[0]
    pre_gate = jnp.dot(token_all, gate_local, preferred_element_type=jnp.float32)
    pre_up = jnp.dot(token_all, up_local, preferred_element_type=jnp.float32)
    sigma = jax.nn.sigmoid(pre_gate)
    act = pre_gate * sigma
    hidden = act * pre_up
    grad_hidden = jnp.dot(grad_all, down_local.T, preferred_element_type=jnp.float32)
    gate_dot = jnp.sum(grad_hidden * hidden, axis=1)
    scaled = gate_all.astype(jnp.float32)[:, None] * grad_hidden
    grad_gate = (scaled * pre_up * sigma * (1.0 + pre_gate * (1.0 - sigma))).astype(jnp.bfloat16)
    grad_up = (scaled * act).astype(jnp.bfloat16)
    expert_grad = jnp.dot(grad_gate, gate_local.T, preferred_element_type=jnp.float32)
    expert_grad = expert_grad + jnp.dot(grad_up, up_local.T, preferred_element_type=jnp.float32)
    grad_own = lax.psum_scatter(
        expert_grad.astype(jnp.bfloat16), ("seq", "mp"), scatter_dimension=0, tiled=True
    ).astype(jnp.float32)
    dot_own = lax.psum_scatter(gate_dot, ("seq", "mp"), scatter_dimension=0, tiled=True)
    grad_back, dot_back = (
        lax.all_to_all(
            grad_own.reshape(expert_count, capacity, width).astype(jnp.bfloat16),
            "expert",
            split_axis=0,
            concat_axis=0,
            tiled=True,
        ).astype(jnp.float32),
        lax.all_to_all(
            dot_own.reshape(expert_count, capacity).astype(jnp.bfloat16),
            "expert",
            split_axis=0,
            concat_axis=0,
            tiled=True,
        ).astype(jnp.float32),
    )
    expert_sum = jnp.einsum("tec,ecd->td", select_full, grad_back, precision=lax.Precision.HIGHEST)
    dot_table = jnp.einsum("tec,ec->te", select_full, dot_back, precision=lax.Precision.HIGHEST)
    dot_first = jnp.sum(dot_table * first_hot, axis=1)
    dot_second = jnp.sum(dot_table * second_hot, axis=1)
    product = gate_first * gate_second * keep_rows
    grad_first = product * (dot_first - dot_second)
    grad_second = product * (dot_second - dot_first)
    logit_grad = first_hot * grad_first[:, None] + second_hot * grad_second[:, None]
    router_term = jnp.dot(logit_grad, router.astype(jnp.float32).T, precision=lax.Precision.HIGHEST)
    d_tokens = ((expert_sum + router_term) * keep_rows[:, None]).astype(jnp.bfloat16)
    gate_grad = jnp.stack([grad_first, grad_second], axis=1)
    return (d_tokens, gate_grad)

def shift(value, axis, step):
    size = lax.axis_size(axis)
    return lax.ppermute(value, axis, [((i + step) % size, i) for i in range(size)])


def swap(value, axis, bit):
    return lax.ppermute(value, axis, [(i ^ bit, i) for i in range(lax.axis_size(axis))])


def swap_x(value):
    return swap(value, "seq", 1)


def swap_y(value):
    return swap(value, "expert", 2)


def swap_core(value):
    return swap(value, "expert", 1)


def gather_z(rows):
    return [rows] + [shift(rows, "mp", k) for k in range(1, lax.axis_size("mp"))]


def gather_near(z_rows, cut):
    rows = jnp.concatenate(z_rows, axis=0)
    low, high = rows[:, :cut], rows[:, cut:]
    return [low, swap_x(low)], [high, swap_y(high)]


def gather_far(low, high):
    return swap_y(jnp.concatenate(low, axis=0)), swap_x(jnp.concatenate(high, axis=0))


def gather_core(low, low_far, high, high_far):
    high_far = jnp.split(high_far, 2, axis=0)
    low = jnp.concatenate(low + [low_far], axis=0)
    high = jnp.concatenate([high[0], high_far[0], high[1], high_far[1]], axis=0)
    return tuple(jnp.concatenate([mine, swap_core(mine)], axis=0) for mine in (low, high))


def scatter_half(kept, sent, first, second):
    total = kept + swap_core(sent).astype(jnp.float32)
    own, by_x, by_y, by_both = jnp.split(total, 4, axis=0)
    near, far = (by_x, [by_y, by_both]) if first is swap_x else (by_y, [by_x, by_both])
    rest = second(jnp.concatenate(far, axis=0).astype(jnp.bfloat16)).astype(jnp.float32)
    rest_own, rest_near = jnp.split(rest, 2, axis=0)
    return own + rest_own + first((near + rest_near).astype(jnp.bfloat16)).astype(jnp.float32)


def scatter_z(total):
    size = lax.axis_size("mp")
    rows = total.shape[0] // size
    result = total[:rows]
    for k in range(1, size):
        result = result + shift(total[k * rows:(k + 1) * rows].astype(jnp.bfloat16), "mp", size - k).astype(jnp.float32)
    return result


def product(a, b, b_dim):
    return lax.dot_general(a, b, (((1,), (b_dim,)), ((), ())), preferred_element_type=jnp.float32)


def part_of(length, wanted):
    return math.gcd(length, wanted)


def in_hbm(value):
    return pltpu.with_memory_space_constraint(value, pltpu.HBM)


def token_kernel(low, high, gate_weight, up_weight, pre_gate, pre_up, gate_copy, up_copy, gate_sems, up_sems):
    half = low.shape[1]
    depth = part_of(half, TOKEN_PART)
    steps = half // depth

    def copies(index):
        rows = pl.ds(pl.multiple_of(index * depth, depth), depth)
        return (
            pltpu.make_async_copy(gate_weight.at[0, rows], gate_copy.at[rows], gate_sems.at[index]),
            pltpu.make_async_copy(up_weight.at[0, rows], up_copy.at[rows], up_sems.at[index]),
        )

    @pl.loop(0, 2 * steps)
    def _(index):
        for copy in copies(index):
            copy.start()

    pre_gate[...] = jnp.zeros_like(pre_gate)
    pre_up[...] = jnp.zeros_like(pre_up)
    for first, part in ((0, low), (steps, high)):

        @pl.loop(0, steps)
        def _(step):
            for copy in copies(first + step):
                copy.wait()
            rows = pl.ds(pl.multiple_of((first + step) * depth, depth), depth)
            values = part[:, pl.ds(pl.multiple_of(step * depth, depth), depth)]
            pre_gate[...] += product(values, gate_copy[rows, :], 0)
            pre_up[...] += product(values, up_copy[rows, :], 0)


def multiply_tokens(low, high, gate_weight, up_weight):
    rows, half = low.shape
    width, hidden = gate_weight.shape[1:]
    steps = width // part_of(half, TOKEN_PART)
    return pl.pallas_call(
        token_kernel,
        out_shape=(
            pltpu.VMEM((rows, hidden), jnp.float32),
            pltpu.VMEM((rows, hidden), jnp.float32),
            pltpu.VMEM((width, hidden), jnp.bfloat16),
            pltpu.VMEM((width, hidden), jnp.bfloat16),
        ),
        in_specs=[pl.BlockSpec(memory_space=pltpu.VMEM)] * 2 + [pl.BlockSpec(memory_space=pl.ANY)] * 2,
        out_specs=(pl.BlockSpec(memory_space=pltpu.VMEM),) * 4,
        scratch_shapes=[pltpu.SemaphoreType.DMA((steps,)), pltpu.SemaphoreType.DMA((steps,))],
        compiler_params=pltpu.CompilerParams(vmem_limit_bytes=TOKEN_VMEM),
        cost_estimate=pl.CostEstimate(
            flops=4 * rows * width * hidden, bytes_accessed=4 * width * hidden, transcendentals=0
        ),
    )(low, high, in_hbm(gate_weight), in_hbm(up_weight))


def grad_kernel(
    expert, low, high, pre_gate, pre_up, down_weight, grad_gate, grad_up, dots, gate_rows, dot_sums, down, down_sems
):
    table = low.shape[1] - high.shape[1]
    half = high.shape[1]
    hidden = down.shape[0]
    depth = part_of(hidden, HIDDEN_PART)
    steps = hidden // depth

    def copy_of(index):
        rows = pl.ds(pl.multiple_of(index * depth, depth), depth)
        return pltpu.make_async_copy(down_weight.at[0, rows], down.at[rows], down_sems.at[index])

    @pl.loop(0, steps)
    def _(index):
        copy_of(index).start()

    lanes = lax.broadcasted_iota(jnp.int32, (low.shape[0], table), 1)
    gate_rows[...] = jnp.sum(
        jnp.where(lanes == expert[0], low[:, :table].astype(jnp.float32), 0.0), axis=1, keepdims=True
    )
    dot_sums[...] = jnp.zeros_like(dot_sums)

    @pl.loop(0, steps)
    def _(step):
        copy_of(step).wait()
        span = pl.ds(pl.multiple_of(step * depth, depth), depth)
        grad_hidden = product(low[:, table:], down[span, :half], 1) + product(high[...], down[span, half:], 1)
        gates = pre_gate[:, span]
        ups = pre_up[:, span]
        sigma = jax.nn.sigmoid(gates)
        act = gates * sigma
        dot_sums[...] += jnp.sum(grad_hidden * (act * ups), axis=1, keepdims=True)
        scaled = gate_rows[...] * grad_hidden
        grad_gate[:, span] = (scaled * ups * sigma * (1.0 + gates * (1.0 - sigma))).astype(jnp.bfloat16)
        grad_up[:, span] = (scaled * act).astype(jnp.bfloat16)

    dots[...] = jnp.where(lanes == expert[0], dot_sums[...], 0.0).astype(jnp.bfloat16)


def multiply_grads(expert, low, high, pre_gate, pre_up, down_weight):
    rows, hidden = pre_gate.shape
    width = down_weight.shape[2]
    table = low.shape[1] - high.shape[1]
    return pl.pallas_call(
        grad_kernel,
        out_shape=(
            pltpu.VMEM((rows, hidden), jnp.bfloat16),
            pltpu.VMEM((rows, hidden), jnp.bfloat16),
            pltpu.VMEM((rows, table), jnp.bfloat16),
        ),
        in_specs=[pl.BlockSpec(memory_space=pltpu.SMEM)]
        + [pl.BlockSpec(memory_space=pltpu.VMEM)] * 4
        + [pl.BlockSpec(memory_space=pl.ANY)],
        out_specs=(pl.BlockSpec(memory_space=pltpu.VMEM),) * 3,
        scratch_shapes=[
            pltpu.VMEM((rows, 1), jnp.float32),
            pltpu.VMEM((rows, 1), jnp.float32),
            pltpu.VMEM((hidden, width), jnp.bfloat16),
            pltpu.SemaphoreType.DMA((hidden // part_of(hidden, HIDDEN_PART),)),
        ],
        compiler_params=pltpu.CompilerParams(vmem_limit_bytes=GRAD_VMEM),
        cost_estimate=pl.CostEstimate(
            flops=2 * rows * width * hidden, bytes_accessed=2 * width * hidden, transcendentals=rows * hidden
        ),
    )(expert, low, high, pre_gate, pre_up, in_hbm(down_weight))


def output_kernel(first, grad_gate, grad_up, gate_copy, up_copy, *refs):
    dots, kept, sent = refs if len(refs) == 3 else (None,) + refs
    rows = kept.shape[0]
    columns = kept.shape[1] - (0 if dots is None else dots.shape[1])
    part = part_of(columns, COLUMN_PART)

    @pl.loop(0, columns // part)
    def _(step):
        span = pl.ds(pl.multiple_of(first + step * part, part), part)
        place = pl.ds(pl.multiple_of(step * part, part), part)
        result = product(grad_gate[...], gate_copy[span, :], 1) + product(grad_up[...], up_copy[span, :], 1)
        kept[:, place] = result[:rows]
        sent[:, place] = result[rows:].astype(jnp.bfloat16)

    if dots is not None:
        kept[:, columns:] = dots[:rows, :].astype(jnp.float32)
        sent[:, columns:] = dots[rows:, :]


def multiply_outputs(first, columns, grad_gate, grad_up, gate_copy, up_copy, *dots):
    rows, hidden = grad_gate.shape
    total = columns + sum(value.shape[1] for value in dots)
    return pl.pallas_call(
        functools.partial(output_kernel, first),
        out_shape=(
            pltpu.VMEM((rows // 2, total), jnp.float32),
            pltpu.VMEM((rows // 2, total), jnp.bfloat16),
        ),
        in_specs=[pl.BlockSpec(memory_space=pltpu.VMEM)] * (4 + len(dots)),
        out_specs=(pl.BlockSpec(memory_space=pltpu.VMEM),) * 2,
        compiler_params=pltpu.CompilerParams(vmem_limit_bytes=OUTPUT_VMEM),
        cost_estimate=pl.CostEstimate(
            flops=4 * rows * columns * hidden, bytes_accessed=4 * rows * columns, transcendentals=0
        ),
    )(grad_gate, grad_up, gate_copy, up_copy, *dots)


def gathered_plan(tokens, out_grad, kept_mask, routes, router, gate_weight, up_weight, down_weight):
    row_count, width = tokens.shape
    expert_count = lax.axis_size("expert")
    columns = lax.broadcasted_iota(jnp.int32, (row_count, expert_count), 1)
    first_hot = (routes[:, 0:1] == columns).astype(jnp.float32)
    second_hot = (routes[:, 1:2] == columns).astype(jnp.float32)
    keep_rows = kept_mask.astype(jnp.float32)
    half = width // 2
    table = 128
    token_z = gather_z(tokens)
    logits = jnp.dot(tokens, router, preferred_element_type=jnp.float32)
    first_logit = jnp.sum(logits * first_hot, axis=1)
    second_logit = jnp.sum(logits * second_hot, axis=1)
    gate_first = jax.nn.sigmoid(first_logit - second_logit)
    gate_second = jax.nn.sigmoid(second_logit - first_logit)
    gate_table = (first_hot * gate_first[:, None] + second_hot * gate_second[:, None]) * keep_rows[:, None]
    gate_table = jnp.pad(gate_table.astype(jnp.bfloat16), ((0, 0), (0, table - expert_count)))
    grad_rows, token_z[1] = lax.optimization_barrier((jnp.concatenate([gate_table, out_grad], axis=1), token_z[1]))
    grad_z = gather_z(grad_rows)
    token_near = gather_near(token_z, half)
    token_far = gather_far(*token_near)
    grad_z, token_far = lax.optimization_barrier((grad_z, token_far))
    grad_near = gather_near(grad_z, half + table)
    token_halves = gather_core(token_near[0], token_far[0], token_near[1], token_far[1])
    grad_far = gather_far(*grad_near)
    pre_gate, pre_up, gate_copy, up_copy = multiply_tokens(*token_halves, gate_weight, up_weight)
    grad_far, pre_gate = lax.optimization_barrier((grad_far, pre_gate))
    grad_halves = gather_core(grad_near[0], grad_far[0], grad_near[1], grad_far[1])
    expert = lax.axis_index("expert").astype(jnp.int32).reshape(1)
    grad_gate, grad_up, dots = multiply_grads(expert, *grad_halves, pre_gate, pre_up, down_weight)
    kept, sent = multiply_outputs(0, half, grad_gate, grad_up, gate_copy, up_copy, dots)
    sent, grad_gate = lax.optimization_barrier((sent, grad_gate))
    low = scatter_z(scatter_half(kept, sent, swap_x, swap_y))
    kept, sent = multiply_outputs(half, half, grad_gate, grad_up, gate_copy, up_copy)
    high = scatter_z(scatter_half(kept, sent, swap_y, swap_x))
    expert_sum = jnp.concatenate([low[:, :half], high], axis=1)
    dot_table = low[:, half:half + expert_count]
    dot_first = jnp.sum(dot_table * first_hot, axis=1)
    dot_second = jnp.sum(dot_table * second_hot, axis=1)
    product = gate_first * gate_second * keep_rows
    grad_first = product * (dot_first - dot_second)
    grad_second = product * (dot_second - dot_first)
    logit_grad = first_hot * grad_first[:, None] + second_hot * grad_second[:, None]
    router_term = jnp.dot(logit_grad, router.astype(jnp.float32).T, precision=lax.Precision.HIGHEST)
    d_tokens = ((expert_sum + router_term) * keep_rows[:, None]).astype(jnp.bfloat16)
    gate_grad = jnp.stack([grad_first, grad_second], axis=1)
    return (d_tokens, gate_grad)


def solution(mesh):
    gathers = mesh.shape["seq"] == 2 and mesh.shape["expert"] == 4
    return jax.shard_map(
        gathered_plan if gathers else routed_plan,
        mesh=mesh,
        in_specs=(
            P(("seq", "expert", "mp"), None),
            P(("seq", "expert", "mp"), None),
            P(("seq", "expert", "mp")),
            P(("seq", "expert", "mp"), None),
            P(),
            P("expert", None, ("seq", "mp")),
            P("expert", None, ("seq", "mp")),
            P("expert", ("seq", "mp"), None),
        ),
        out_specs=(P(("seq", "expert", "mp"), None), P(("seq", "expert", "mp"), None)),
        check_vma=False,
    )
```

```python
import functools
import math

import jax
import jax.numpy as jnp
from jax import lax
from jax.experimental import pallas as pl
from jax.experimental.pallas import tpu as pltpu
from jax.sharding import PartitionSpec as P

TOKEN_PART = 512
HIDDEN_PART = 256
COLUMN_PART = 512
TOKEN_VMEM = 16 * 2 ** 20
GRAD_VMEM = 20 * 2 ** 20
OUTPUT_VMEM = 16 * 2 ** 20


def routed_plan(tokens, out_grad, kept_mask, routes, router, gate_weight, up_weight, down_weight):
    row_count = tokens.shape[0]
    width = tokens.shape[1]
    expert_count = lax.axis_size("expert")
    capacity = max(3 * row_count // 8, 2 * row_count // expert_count)
    logits = jnp.dot(tokens, router, preferred_element_type=jnp.float32)
    columns = lax.broadcasted_iota(jnp.int32, (row_count, expert_count), 1)
    first_hot = (routes[:, 0:1] == columns).astype(jnp.float32)
    second_hot = (routes[:, 1:2] == columns).astype(jnp.float32)
    first_logit = jnp.sum(logits * first_hot, axis=1)
    second_logit = jnp.sum(logits * second_hot, axis=1)
    gate_first = jax.nn.sigmoid(first_logit - second_logit)
    gate_second = jax.nn.sigmoid(second_logit - first_logit)
    keep_rows = kept_mask.astype(jnp.float32)
    chosen = ((first_hot + second_hot) * keep_rows[:, None]).astype(jnp.int32)
    position = jnp.cumsum(chosen, axis=0) - 1
    slot_iota = lax.broadcasted_iota(jnp.int32, (row_count, expert_count, capacity), 2)
    select_mask = (chosen[:, :, None] == 1) & (position[:, :, None] == slot_iota)
    select_bf = select_mask.astype(jnp.bfloat16)
    select_full = select_mask.astype(jnp.float32)
    token_send = jnp.einsum(
        "tec,td->ecd", select_bf, tokens, preferred_element_type=jnp.float32
    ).astype(jnp.bfloat16)
    grad_send = jnp.einsum(
        "tec,td->ecd", select_bf, out_grad, preferred_element_type=jnp.float32
    ).astype(jnp.bfloat16)
    gate_table = first_hot * gate_first[:, None] + second_hot * gate_second[:, None]
    gate_send = jnp.einsum(
        "tec,te->ec", select_full, gate_table, precision=lax.Precision.HIGHEST
    ).astype(jnp.bfloat16)
    token_recv, grad_recv, gate_recv = (
        lax.all_to_all(token_send, "expert", split_axis=0, concat_axis=0, tiled=True),
        lax.all_to_all(grad_send, "expert", split_axis=0, concat_axis=0, tiled=True),
        lax.all_to_all(gate_send, "expert", split_axis=0, concat_axis=0, tiled=True),
    )
    token_all, grad_all, gate_all = (
        lax.all_gather(token_recv, ("seq", "mp"), axis=0, tiled=True),
        lax.all_gather(grad_recv, ("seq", "mp"), axis=0, tiled=True),
        lax.all_gather(gate_recv, ("seq", "mp"), axis=0, tiled=True),
    )
    token_all = token_all.reshape(-1, width)
    grad_all = grad_all.reshape(-1, width)
    gate_all = gate_all.reshape(-1)
    gate_local = gate_weight[0]
    up_local = up_weight[0]
    down_local = down_weight[0]
    pre_gate = jnp.dot(token_all, gate_local, preferred_element_type=jnp.float32)
    pre_up = jnp.dot(token_all, up_local, preferred_element_type=jnp.float32)
    sigma = jax.nn.sigmoid(pre_gate)
    act = pre_gate * sigma
    hidden = act * pre_up
    grad_hidden = jnp.dot(grad_all, down_local.T, preferred_element_type=jnp.float32)
    gate_dot = jnp.sum(grad_hidden * hidden, axis=1)
    scaled = gate_all.astype(jnp.float32)[:, None] * grad_hidden
    grad_gate = (scaled * pre_up * sigma * (1.0 + pre_gate * (1.0 - sigma))).astype(jnp.bfloat16)
    grad_up = (scaled * act).astype(jnp.bfloat16)
    expert_grad = jnp.dot(grad_gate, gate_local.T, preferred_element_type=jnp.float32)
    expert_grad = expert_grad + jnp.dot(grad_up, up_local.T, preferred_element_type=jnp.float32)
    grad_own = lax.psum_scatter(
        expert_grad.astype(jnp.bfloat16), ("seq", "mp"), scatter_dimension=0, tiled=True
    ).astype(jnp.float32)
    dot_own = lax.psum_scatter(gate_dot, ("seq", "mp"), scatter_dimension=0, tiled=True)
    grad_back, dot_back = (
        lax.all_to_all(
            grad_own.reshape(expert_count, capacity, width).astype(jnp.bfloat16),
            "expert",
            split_axis=0,
            concat_axis=0,
            tiled=True,
        ).astype(jnp.float32),
        lax.all_to_all(
            dot_own.reshape(expert_count, capacity).astype(jnp.bfloat16),
            "expert",
            split_axis=0,
            concat_axis=0,
            tiled=True,
        ).astype(jnp.float32),
    )
    expert_sum = jnp.einsum("tec,ecd->td", select_full, grad_back, precision=lax.Precision.HIGHEST)
    dot_table = jnp.einsum("tec,ec->te", select_full, dot_back, precision=lax.Precision.HIGHEST)
    dot_first = jnp.sum(dot_table * first_hot, axis=1)
    dot_second = jnp.sum(dot_table * second_hot, axis=1)
    product = gate_first * gate_second * keep_rows
    grad_first = product * (dot_first - dot_second)
    grad_second = product * (dot_second - dot_first)
    logit_grad = first_hot * grad_first[:, None] + second_hot * grad_second[:, None]
    router_term = jnp.dot(logit_grad, router.astype(jnp.float32).T, precision=lax.Precision.HIGHEST)
    d_tokens = ((expert_sum + router_term) * keep_rows[:, None]).astype(jnp.bfloat16)
    gate_grad = jnp.stack([grad_first, grad_second], axis=1)
    return (d_tokens, gate_grad)

def shift(value, axis, step):
    size = lax.axis_size(axis)
    return lax.ppermute(value, axis, [((i + step) % size, i) for i in range(size)])


def swap(value, axis, bit):
    return lax.ppermute(value, axis, [(i ^ bit, i) for i in range(lax.axis_size(axis))])


def swap_x(value):
    return swap(value, "seq", 1)


def swap_y(value):
    return swap(value, "expert", 2)


def swap_core(value):
    return swap(value, "expert", 1)


def after_others(values, others):
    return lax.optimization_barrier((values, others))[0]


def gather_z(rows):
    return [rows] + [shift(rows, "mp", k) for k in range(1, lax.axis_size("mp"))]


def gather_near(z_rows, cut):
    rows = jnp.concatenate(z_rows, axis=0)
    low, high = rows[:, :cut], rows[:, cut:]
    return [low, swap_x(low)], [high, swap_y(high)]


def gather_far(low, high):
    return swap_y(jnp.concatenate(low, axis=0)), swap_x(jnp.concatenate(high, axis=0))


def gather_core(low, low_far, high, high_far):
    high_far = jnp.split(high_far, 2, axis=0)
    low = jnp.concatenate(low + [low_far], axis=0)
    high = jnp.concatenate([high[0], high_far[0], high[1], high_far[1]], axis=0)
    return tuple(jnp.concatenate([mine, swap_core(mine)], axis=0) for mine in (low, high))


def scatter_core(kept, sent):
    return kept + swap_core(sent).astype(jnp.float32)


def send(value, exchange):
    return exchange(value.astype(jnp.bfloat16)).astype(jnp.float32)


def scatter_far(total, cut):
    low, low_x, low_y, low_both = jnp.split(total[:, :cut], 4, axis=0)
    high, high_x, high_y, high_both = jnp.split(total[:, cut:], 4, axis=0)
    low_far = send(jnp.concatenate([low_y, low_both], axis=0), swap_y)
    high_far = send(jnp.concatenate([high_x, high_both], axis=0), swap_x)
    return jnp.concatenate([low, low_x], axis=0) + low_far, jnp.concatenate([high, high_y], axis=0) + high_far


def scatter_near(low, high):
    low, low_x = jnp.split(low, 2, axis=0)
    high, high_y = jnp.split(high, 2, axis=0)
    return jnp.concatenate([low + send(low_x, swap_x), high + send(high_y, swap_y)], axis=1)


def scatter_z(total):
    size = lax.axis_size("mp")
    rows = total.shape[0] // size
    result = total[:rows]
    for k in range(1, size):
        result = result + send(total[k * rows:(k + 1) * rows], lambda value: shift(value, "mp", size - k))
    return result


def product(a, b, b_dim):
    return lax.dot_general(a, b, (((1,), (b_dim,)), ((), ())), preferred_element_type=jnp.float32)


def part_of(length, wanted):
    return math.gcd(length, wanted)


def in_hbm(value):
    return pltpu.with_memory_space_constraint(value, pltpu.HBM)


def token_kernel(first, tokens, gate_weight, up_weight, *refs):
    before, (pre_gate, pre_up, gate_copy, up_copy, gate_sems, up_sems) = refs[:-6], refs[-6:]
    width = tokens.shape[1]
    depth = part_of(width, TOKEN_PART)
    steps = width // depth

    def copies(index):
        source = pl.ds(pl.multiple_of(first + index * depth, depth), depth)
        rows = pl.ds(pl.multiple_of(index * depth, depth), depth)
        return (
            pltpu.make_async_copy(gate_weight.at[0, source], gate_copy.at[rows], gate_sems.at[index]),
            pltpu.make_async_copy(up_weight.at[0, source], up_copy.at[rows], up_sems.at[index]),
        )

    @pl.loop(0, steps)
    def _(index):
        for copy in copies(index):
            copy.start()

    pre_gate[...] = before[0][...] if before else jnp.zeros_like(pre_gate)
    pre_up[...] = before[1][...] if before else jnp.zeros_like(pre_up)

    @pl.loop(0, steps)
    def _(step):
        for copy in copies(step):
            copy.wait()
        rows = pl.ds(pl.multiple_of(step * depth, depth), depth)
        pre_gate[...] += product(tokens[:, rows], gate_copy[rows, :], 0)
        pre_up[...] += product(tokens[:, rows], up_copy[rows, :], 0)


def multiply_tokens(first, tokens, gate_weight, up_weight, *before):
    rows, width = tokens.shape
    hidden = gate_weight.shape[2]
    steps = width // part_of(width, TOKEN_PART)
    return pl.pallas_call(
        functools.partial(token_kernel, first),
        out_shape=(
            pltpu.VMEM((rows, hidden), jnp.float32),
            pltpu.VMEM((rows, hidden), jnp.float32),
            pltpu.VMEM((width, hidden), jnp.bfloat16),
            pltpu.VMEM((width, hidden), jnp.bfloat16),
        ),
        in_specs=[pl.BlockSpec(memory_space=pltpu.VMEM)]
        + [pl.BlockSpec(memory_space=pl.ANY)] * 2
        + [pl.BlockSpec(memory_space=pltpu.VMEM)] * len(before),
        out_specs=(pl.BlockSpec(memory_space=pltpu.VMEM),) * 4,
        scratch_shapes=[pltpu.SemaphoreType.DMA((steps,)), pltpu.SemaphoreType.DMA((steps,))],
        compiler_params=pltpu.CompilerParams(vmem_limit_bytes=TOKEN_VMEM),
        cost_estimate=pl.CostEstimate(
            flops=4 * rows * width * hidden, bytes_accessed=4 * width * hidden, transcendentals=0
        ),
    )(tokens, in_hbm(gate_weight), in_hbm(up_weight), *before)


def grad_kernel(
    expert, low, high, pre_gate, pre_up, down_weight, grad_gate, grad_up, dots, gate_rows, dot_sums, down, down_sems
):
    table = low.shape[1] - high.shape[1]
    half = high.shape[1]
    hidden = down.shape[0]
    depth = part_of(hidden, HIDDEN_PART)
    steps = hidden // depth

    def copy_of(index):
        rows = pl.ds(pl.multiple_of(index * depth, depth), depth)
        return pltpu.make_async_copy(down_weight.at[0, rows], down.at[rows], down_sems.at[index])

    @pl.loop(0, steps)
    def _(index):
        copy_of(index).start()

    lanes = lax.broadcasted_iota(jnp.int32, (low.shape[0], table), 1)
    gate_rows[...] = jnp.sum(
        jnp.where(lanes == expert[0], low[:, :table].astype(jnp.float32), 0.0), axis=1, keepdims=True
    )
    dot_sums[...] = jnp.zeros_like(dot_sums)

    @pl.loop(0, steps)
    def _(step):
        copy_of(step).wait()
        span = pl.ds(pl.multiple_of(step * depth, depth), depth)
        grad_hidden = product(low[:, table:], down[span, :half], 1) + product(high[...], down[span, half:], 1)
        gates = pre_gate[:, span]
        ups = pre_up[:, span]
        sigma = jax.nn.sigmoid(gates)
        act = gates * sigma
        dot_sums[...] += jnp.sum(grad_hidden * (act * ups), axis=1, keepdims=True)
        scaled = gate_rows[...] * grad_hidden
        grad_gate[:, span] = (scaled * ups * sigma * (1.0 + gates * (1.0 - sigma))).astype(jnp.bfloat16)
        grad_up[:, span] = (scaled * act).astype(jnp.bfloat16)

    dots[...] = jnp.where(lanes == expert[0], dot_sums[...], 0.0).astype(jnp.bfloat16)


def multiply_grads(expert, low, high, pre_gate, pre_up, down_weight):
    rows, hidden = pre_gate.shape
    width = down_weight.shape[2]
    table = low.shape[1] - high.shape[1]
    return pl.pallas_call(
        grad_kernel,
        out_shape=(
            pltpu.VMEM((rows, hidden), jnp.bfloat16),
            pltpu.VMEM((rows, hidden), jnp.bfloat16),
            pltpu.VMEM((rows, table), jnp.bfloat16),
        ),
        in_specs=[pl.BlockSpec(memory_space=pltpu.SMEM)]
        + [pl.BlockSpec(memory_space=pltpu.VMEM)] * 4
        + [pl.BlockSpec(memory_space=pl.ANY)],
        out_specs=(pl.BlockSpec(memory_space=pltpu.VMEM),) * 3,
        scratch_shapes=[
            pltpu.VMEM((rows, 1), jnp.float32),
            pltpu.VMEM((rows, 1), jnp.float32),
            pltpu.VMEM((hidden, width), jnp.bfloat16),
            pltpu.SemaphoreType.DMA((hidden // part_of(hidden, HIDDEN_PART),)),
        ],
        compiler_params=pltpu.CompilerParams(vmem_limit_bytes=GRAD_VMEM),
        cost_estimate=pl.CostEstimate(
            flops=2 * rows * width * hidden, bytes_accessed=2 * width * hidden, transcendentals=rows * hidden
        ),
    )(expert, low, high, pre_gate, pre_up, in_hbm(down_weight))


def output_kernel(grad_gate, grad_up, gate_copy, up_copy, *refs):
    dots, kept, sent = refs if len(refs) == 3 else (None,) + refs
    rows = kept.shape[0]
    columns = kept.shape[1] - (0 if dots is None else dots.shape[1])
    part = part_of(columns, COLUMN_PART)

    @pl.loop(0, columns // part)
    def _(step):
        span = pl.ds(pl.multiple_of(step * part, part), part)
        result = product(grad_gate[...], gate_copy[span, :], 1) + product(grad_up[...], up_copy[span, :], 1)
        kept[:, span] = result[:rows]
        sent[:, span] = result[rows:].astype(jnp.bfloat16)

    if dots is not None:
        kept[:, columns:] = dots[:rows, :].astype(jnp.float32)
        sent[:, columns:] = dots[rows:, :]


def multiply_outputs(grad_gate, grad_up, gate_copy, up_copy, *dots):
    rows, hidden = grad_gate.shape
    columns = gate_copy.shape[0]
    total = columns + sum(value.shape[1] for value in dots)
    return pl.pallas_call(
        output_kernel,
        out_shape=(
            pltpu.VMEM((rows // 2, total), jnp.float32),
            pltpu.VMEM((rows // 2, total), jnp.bfloat16),
        ),
        in_specs=[pl.BlockSpec(memory_space=pltpu.VMEM)] * (4 + len(dots)),
        out_specs=(pl.BlockSpec(memory_space=pltpu.VMEM),) * 2,
        compiler_params=pltpu.CompilerParams(vmem_limit_bytes=OUTPUT_VMEM),
        cost_estimate=pl.CostEstimate(
            flops=4 * rows * columns * hidden, bytes_accessed=4 * rows * columns, transcendentals=0
        ),
    )(grad_gate, grad_up, gate_copy, up_copy, *dots)


def gathered_plan(tokens, out_grad, kept_mask, routes, router, gate_weight, up_weight, down_weight):
    row_count, width = tokens.shape
    expert_count = lax.axis_size("expert")
    columns = lax.broadcasted_iota(jnp.int32, (row_count, expert_count), 1)
    first_hot = (routes[:, 0:1] == columns).astype(jnp.float32)
    second_hot = (routes[:, 1:2] == columns).astype(jnp.float32)
    keep_rows = kept_mask.astype(jnp.float32)
    half = width // 2
    table = 128
    token_z = gather_z(tokens)
    logits = jnp.dot(tokens, router, preferred_element_type=jnp.float32)
    first_logit = jnp.sum(logits * first_hot, axis=1)
    second_logit = jnp.sum(logits * second_hot, axis=1)
    gate_first = jax.nn.sigmoid(first_logit - second_logit)
    gate_second = jax.nn.sigmoid(second_logit - first_logit)
    gate_table = (first_hot * gate_first[:, None] + second_hot * gate_second[:, None]) * keep_rows[:, None]
    gate_table = jnp.pad(gate_table.astype(jnp.bfloat16), ((0, 0), (0, table - expert_count)))
    grad_z = gather_z(after_others(jnp.concatenate([gate_table, out_grad], axis=1), token_z[1]))
    token_near = gather_near(token_z, half)
    token_far = gather_far(*after_others(token_near, grad_z[1]))
    grad_near = gather_near(after_others(grad_z, token_far), half + table)
    token_low, token_high = gather_core(token_near[0], token_far[0], token_near[1], token_far[1])
    before = multiply_tokens(0, token_low, gate_weight, up_weight)
    grad_far = gather_far(*after_others(grad_near, before[0]))
    after = multiply_tokens(half, token_high, gate_weight, up_weight, before[0], before[1])
    grad_far = after_others(grad_far, after[0])
    grad_halves = gather_core(grad_near[0], grad_far[0], grad_near[1], grad_far[1])
    expert = lax.axis_index("expert").astype(jnp.int32).reshape(1)
    grad_gate, grad_up, dots = multiply_grads(expert, *grad_halves, after[0], after[1], down_weight)
    kept, sent = multiply_outputs(grad_gate, grad_up, before[2], before[3], dots)
    chunk = scatter_core(kept, sent)
    kept, sent = multiply_outputs(grad_gate, grad_up, after[2], after[3])
    chunk = scatter_far(after_others(chunk, sent), half // 2)
    later = scatter_core(kept, sent)
    chunk = scatter_near(*after_others(chunk, later))
    later = scatter_far(later, half // 2)
    chunk = scatter_z(after_others(chunk, later))
    later = scatter_z(scatter_near(*later))
    expert_sum = jnp.concatenate([chunk[:, :half], later], axis=1)
    dot_table = chunk[:, half:half + expert_count]
    dot_first = jnp.sum(dot_table * first_hot, axis=1)
    dot_second = jnp.sum(dot_table * second_hot, axis=1)
    product = gate_first * gate_second * keep_rows
    grad_first = product * (dot_first - dot_second)
    grad_second = product * (dot_second - dot_first)
    logit_grad = first_hot * grad_first[:, None] + second_hot * grad_second[:, None]
    router_term = jnp.dot(logit_grad, router.astype(jnp.float32).T, precision=lax.Precision.HIGHEST)
    d_tokens = ((expert_sum + router_term) * keep_rows[:, None]).astype(jnp.bfloat16)
    gate_grad = jnp.stack([grad_first, grad_second], axis=1)
    return (d_tokens, gate_grad)


def solution(mesh):
    gathers = mesh.shape["seq"] == 2 and mesh.shape["expert"] == 4
    return jax.shard_map(
        gathered_plan if gathers else routed_plan,
        mesh=mesh,
        in_specs=(
            P(("seq", "expert", "mp"), None),
            P(("seq", "expert", "mp"), None),
            P(("seq", "expert", "mp")),
            P(("seq", "expert", "mp"), None),
            P(),
            P("expert", None, ("seq", "mp")),
            P("expert", None, ("seq", "mp")),
            P("expert", ("seq", "mp"), None),
        ),
        out_specs=(P(("seq", "expert", "mp"), None), P(("seq", "expert", "mp"), None)),
        check_vma=False,
    )
```

```python
import functools
import math

import jax
import jax.numpy as jnp
from jax import lax
from jax.experimental import pallas as pl
from jax.experimental.pallas import tpu as pltpu
from jax.sharding import PartitionSpec as P

TOKEN_PART = 512
HIDDEN_PART = 256
COLUMN_PART = 512
TOKEN_VMEM = 16 * 2 ** 20
GRAD_VMEM = 20 * 2 ** 20
OUTPUT_VMEM = 16 * 2 ** 20


def routed_plan(tokens, out_grad, kept_mask, routes, router, gate_weight, up_weight, down_weight):
    row_count = tokens.shape[0]
    width = tokens.shape[1]
    expert_count = lax.axis_size("expert")
    capacity = max(3 * row_count // 8, 2 * row_count // expert_count)
    logits = jnp.dot(tokens, router, preferred_element_type=jnp.float32)
    columns = lax.broadcasted_iota(jnp.int32, (row_count, expert_count), 1)
    first_hot = (routes[:, 0:1] == columns).astype(jnp.float32)
    second_hot = (routes[:, 1:2] == columns).astype(jnp.float32)
    first_logit = jnp.sum(logits * first_hot, axis=1)
    second_logit = jnp.sum(logits * second_hot, axis=1)
    gate_first = jax.nn.sigmoid(first_logit - second_logit)
    gate_second = jax.nn.sigmoid(second_logit - first_logit)
    keep_rows = kept_mask.astype(jnp.float32)
    chosen = ((first_hot + second_hot) * keep_rows[:, None]).astype(jnp.int32)
    position = jnp.cumsum(chosen, axis=0) - 1
    slot_iota = lax.broadcasted_iota(jnp.int32, (row_count, expert_count, capacity), 2)
    select_mask = (chosen[:, :, None] == 1) & (position[:, :, None] == slot_iota)
    select_bf = select_mask.astype(jnp.bfloat16)
    select_full = select_mask.astype(jnp.float32)
    token_send = jnp.einsum(
        "tec,td->ecd", select_bf, tokens, preferred_element_type=jnp.float32
    ).astype(jnp.bfloat16)
    grad_send = jnp.einsum(
        "tec,td->ecd", select_bf, out_grad, preferred_element_type=jnp.float32
    ).astype(jnp.bfloat16)
    gate_table = first_hot * gate_first[:, None] + second_hot * gate_second[:, None]
    gate_send = jnp.einsum(
        "tec,te->ec", select_full, gate_table, precision=lax.Precision.HIGHEST
    ).astype(jnp.bfloat16)
    token_recv, grad_recv, gate_recv = (
        lax.all_to_all(token_send, "expert", split_axis=0, concat_axis=0, tiled=True),
        lax.all_to_all(grad_send, "expert", split_axis=0, concat_axis=0, tiled=True),
        lax.all_to_all(gate_send, "expert", split_axis=0, concat_axis=0, tiled=True),
    )
    token_all, grad_all, gate_all = (
        lax.all_gather(token_recv, ("seq", "mp"), axis=0, tiled=True),
        lax.all_gather(grad_recv, ("seq", "mp"), axis=0, tiled=True),
        lax.all_gather(gate_recv, ("seq", "mp"), axis=0, tiled=True),
    )
    token_all = token_all.reshape(-1, width)
    grad_all = grad_all.reshape(-1, width)
    gate_all = gate_all.reshape(-1)
    gate_local = gate_weight[0]
    up_local = up_weight[0]
    down_local = down_weight[0]
    pre_gate = jnp.dot(token_all, gate_local, preferred_element_type=jnp.float32)
    pre_up = jnp.dot(token_all, up_local, preferred_element_type=jnp.float32)
    sigma = jax.nn.sigmoid(pre_gate)
    act = pre_gate * sigma
    hidden = act * pre_up
    grad_hidden = jnp.dot(grad_all, down_local.T, preferred_element_type=jnp.float32)
    gate_dot = jnp.sum(grad_hidden * hidden, axis=1)
    scaled = gate_all.astype(jnp.float32)[:, None] * grad_hidden
    grad_gate = (scaled * pre_up * sigma * (1.0 + pre_gate * (1.0 - sigma))).astype(jnp.bfloat16)
    grad_up = (scaled * act).astype(jnp.bfloat16)
    expert_grad = jnp.dot(grad_gate, gate_local.T, preferred_element_type=jnp.float32)
    expert_grad = expert_grad + jnp.dot(grad_up, up_local.T, preferred_element_type=jnp.float32)
    grad_own = lax.psum_scatter(
        expert_grad.astype(jnp.bfloat16), ("seq", "mp"), scatter_dimension=0, tiled=True
    ).astype(jnp.float32)
    dot_own = lax.psum_scatter(gate_dot, ("seq", "mp"), scatter_dimension=0, tiled=True)
    grad_back, dot_back = (
        lax.all_to_all(
            grad_own.reshape(expert_count, capacity, width).astype(jnp.bfloat16),
            "expert",
            split_axis=0,
            concat_axis=0,
            tiled=True,
        ).astype(jnp.float32),
        lax.all_to_all(
            dot_own.reshape(expert_count, capacity).astype(jnp.bfloat16),
            "expert",
            split_axis=0,
            concat_axis=0,
            tiled=True,
        ).astype(jnp.float32),
    )
    expert_sum = jnp.einsum("tec,ecd->td", select_full, grad_back, precision=lax.Precision.HIGHEST)
    dot_table = jnp.einsum("tec,ec->te", select_full, dot_back, precision=lax.Precision.HIGHEST)
    dot_first = jnp.sum(dot_table * first_hot, axis=1)
    dot_second = jnp.sum(dot_table * second_hot, axis=1)
    product = gate_first * gate_second * keep_rows
    grad_first = product * (dot_first - dot_second)
    grad_second = product * (dot_second - dot_first)
    logit_grad = first_hot * grad_first[:, None] + second_hot * grad_second[:, None]
    router_term = jnp.dot(logit_grad, router.astype(jnp.float32).T, precision=lax.Precision.HIGHEST)
    d_tokens = ((expert_sum + router_term) * keep_rows[:, None]).astype(jnp.bfloat16)
    gate_grad = jnp.stack([grad_first, grad_second], axis=1)
    return (d_tokens, gate_grad)

def shift(value, axis, step):
    size = lax.axis_size(axis)
    return lax.ppermute(value, axis, [((i + step) % size, i) for i in range(size)])


def swap(value, axis, bit):
    return lax.ppermute(value, axis, [(i ^ bit, i) for i in range(lax.axis_size(axis))])


def swap_x(value):
    return swap(value, "seq", 1)


def swap_y(value):
    return swap(value, "expert", 2)


def swap_core(value):
    return swap(value, "expert", 1)


def after_others(values, others):
    return lax.optimization_barrier((values, others))[0]


def gather_z(rows):
    return jnp.concatenate([rows] + [shift(rows, "mp", k) for k in range(1, lax.axis_size("mp"))], axis=0)


def gather_z_whole(rows):
    size, count = lax.axis_size("mp"), rows.shape[0]
    whole = lax.all_gather(rows, "mp", axis=0, tiled=True)
    start = lax.axis_index("mp") * count
    return lax.dynamic_slice_in_dim(jnp.concatenate([whole, whole], axis=0), start, size * count, 0)


def gather_near(z_rows, cut):
    low, high = z_rows[:, :cut], z_rows[:, cut:]
    return [low, swap_x(low)], [high, swap_y(high)]


def gather_far(low, high):
    return swap_y(jnp.concatenate(low, axis=0)), swap_x(jnp.concatenate(high, axis=0))


def gather_core(low, low_far, high, high_far):
    high_far = jnp.split(high_far, 2, axis=0)
    low = jnp.concatenate(low + [low_far], axis=0)
    high = jnp.concatenate([high[0], high_far[0], high[1], high_far[1]], axis=0)
    return tuple(jnp.concatenate([mine, swap_core(mine)], axis=0) for mine in (low, high))


def scatter_core(kept, sent):
    return kept + swap_core(sent).astype(jnp.float32)


def send(value, exchange):
    return exchange(value.astype(jnp.bfloat16)).astype(jnp.float32)


def scatter_far(total, cut):
    low, low_x, low_y, low_both = jnp.split(total[:, :cut], 4, axis=0)
    high, high_x, high_y, high_both = jnp.split(total[:, cut:], 4, axis=0)
    low_far = send(jnp.concatenate([low_y, low_both], axis=0), swap_y)
    high_far = send(jnp.concatenate([high_x, high_both], axis=0), swap_x)
    return jnp.concatenate([low, low_x], axis=0) + low_far, jnp.concatenate([high, high_y], axis=0) + high_far


def scatter_near(low, high):
    low, low_x = jnp.split(low, 2, axis=0)
    high, high_y = jnp.split(high, 2, axis=0)
    return jnp.concatenate([low + send(low_x, swap_x), high + send(high_y, swap_y)], axis=1)


def scatter_z(total):
    size = lax.axis_size("mp")
    rows = total.shape[0] // size
    result = total[:rows]
    for k in range(1, size):
        result = result + send(total[k * rows:(k + 1) * rows], lambda value: shift(value, "mp", size - k))
    return result


def product(a, b, b_dim):
    return lax.dot_general(a, b, (((1,), (b_dim,)), ((), ())), preferred_element_type=jnp.float32)


def part_of(length, wanted):
    return math.gcd(length, wanted)


def in_hbm(value):
    return pltpu.with_memory_space_constraint(value, pltpu.HBM)


def token_kernel(first, tokens, gate_weight, up_weight, *refs):
    before, (pre_gate, pre_up, gate_copy, up_copy, gate_sems, up_sems) = refs[:-6], refs[-6:]
    width = tokens.shape[1]
    depth = part_of(width, TOKEN_PART)
    steps = width // depth

    def copies(index):
        source = pl.ds(pl.multiple_of(first + index * depth, depth), depth)
        rows = pl.ds(pl.multiple_of(index * depth, depth), depth)
        return (
            pltpu.make_async_copy(gate_weight.at[0, source], gate_copy.at[rows], gate_sems.at[index]),
            pltpu.make_async_copy(up_weight.at[0, source], up_copy.at[rows], up_sems.at[index]),
        )

    @pl.loop(0, steps)
    def _(index):
        for copy in copies(index):
            copy.start()

    pre_gate[...] = before[0][...] if before else jnp.zeros_like(pre_gate)
    pre_up[...] = before[1][...] if before else jnp.zeros_like(pre_up)

    @pl.loop(0, steps)
    def _(step):
        for copy in copies(step):
            copy.wait()
        rows = pl.ds(pl.multiple_of(step * depth, depth), depth)
        pre_gate[...] += product(tokens[:, rows], gate_copy[rows, :], 0)
        pre_up[...] += product(tokens[:, rows], up_copy[rows, :], 0)


def multiply_tokens(first, tokens, gate_weight, up_weight, *before):
    rows, width = tokens.shape
    hidden = gate_weight.shape[2]
    steps = width // part_of(width, TOKEN_PART)
    return pl.pallas_call(
        functools.partial(token_kernel, first),
        out_shape=(
            pltpu.VMEM((rows, hidden), jnp.float32),
            pltpu.VMEM((rows, hidden), jnp.float32),
            pltpu.VMEM((width, hidden), jnp.bfloat16),
            pltpu.VMEM((width, hidden), jnp.bfloat16),
        ),
        in_specs=[pl.BlockSpec(memory_space=pltpu.VMEM)]
        + [pl.BlockSpec(memory_space=pl.ANY)] * 2
        + [pl.BlockSpec(memory_space=pltpu.VMEM)] * len(before),
        out_specs=(pl.BlockSpec(memory_space=pltpu.VMEM),) * 4,
        scratch_shapes=[pltpu.SemaphoreType.DMA((steps,)), pltpu.SemaphoreType.DMA((steps,))],
        compiler_params=pltpu.CompilerParams(vmem_limit_bytes=TOKEN_VMEM),
        cost_estimate=pl.CostEstimate(
            flops=4 * rows * width * hidden, bytes_accessed=4 * width * hidden, transcendentals=0
        ),
    )(tokens, in_hbm(gate_weight), in_hbm(up_weight), *before)


def grad_kernel(
    expert, low, high, pre_gate, pre_up, down_weight, grad_gate, grad_up, dots, gate_rows, dot_sums, down, down_sems
):
    table = low.shape[1] - high.shape[1]
    half = high.shape[1]
    hidden = down.shape[0]
    depth = part_of(hidden, HIDDEN_PART)
    steps = hidden // depth

    def copy_of(index):
        rows = pl.ds(pl.multiple_of(index * depth, depth), depth)
        return pltpu.make_async_copy(down_weight.at[0, rows], down.at[rows], down_sems.at[index])

    @pl.loop(0, steps)
    def _(index):
        copy_of(index).start()

    lanes = lax.broadcasted_iota(jnp.int32, (low.shape[0], table), 1)
    gate_rows[...] = jnp.sum(
        jnp.where(lanes == expert[0], low[:, :table].astype(jnp.float32), 0.0), axis=1, keepdims=True
    )
    dot_sums[...] = jnp.zeros_like(dot_sums)

    @pl.loop(0, steps)
    def _(step):
        copy_of(step).wait()
        span = pl.ds(pl.multiple_of(step * depth, depth), depth)
        grad_hidden = product(low[:, table:], down[span, :half], 1) + product(high[...], down[span, half:], 1)
        gates = pre_gate[:, span]
        ups = pre_up[:, span]
        sigma = jax.nn.sigmoid(gates)
        act = gates * sigma
        dot_sums[...] += jnp.sum(grad_hidden * (act * ups), axis=1, keepdims=True)
        scaled = gate_rows[...] * grad_hidden
        grad_gate[:, span] = (scaled * ups * sigma * (1.0 + gates * (1.0 - sigma))).astype(jnp.bfloat16)
        grad_up[:, span] = (scaled * act).astype(jnp.bfloat16)

    dots[...] = jnp.where(lanes == expert[0], dot_sums[...], 0.0).astype(jnp.bfloat16)


def multiply_grads(expert, low, high, pre_gate, pre_up, down_weight):
    rows, hidden = pre_gate.shape
    width = down_weight.shape[2]
    table = low.shape[1] - high.shape[1]
    return pl.pallas_call(
        grad_kernel,
        out_shape=(
            pltpu.VMEM((rows, hidden), jnp.bfloat16),
            pltpu.VMEM((rows, hidden), jnp.bfloat16),
            pltpu.VMEM((rows, table), jnp.bfloat16),
        ),
        in_specs=[pl.BlockSpec(memory_space=pltpu.SMEM)]
        + [pl.BlockSpec(memory_space=pltpu.VMEM)] * 4
        + [pl.BlockSpec(memory_space=pl.ANY)],
        out_specs=(pl.BlockSpec(memory_space=pltpu.VMEM),) * 3,
        scratch_shapes=[
            pltpu.VMEM((rows, 1), jnp.float32),
            pltpu.VMEM((rows, 1), jnp.float32),
            pltpu.VMEM((hidden, width), jnp.bfloat16),
            pltpu.SemaphoreType.DMA((hidden // part_of(hidden, HIDDEN_PART),)),
        ],
        compiler_params=pltpu.CompilerParams(vmem_limit_bytes=GRAD_VMEM),
        cost_estimate=pl.CostEstimate(
            flops=2 * rows * width * hidden, bytes_accessed=2 * width * hidden, transcendentals=rows * hidden
        ),
    )(expert, low, high, pre_gate, pre_up, in_hbm(down_weight))


def output_kernel(grad_gate, grad_up, gate_copy, up_copy, *refs):
    dots, kept, sent = refs if len(refs) == 3 else (None,) + refs
    rows = kept.shape[0]
    columns = kept.shape[1] - (0 if dots is None else dots.shape[1])
    part = part_of(columns, COLUMN_PART)

    @pl.loop(0, columns // part)
    def _(step):
        span = pl.ds(pl.multiple_of(step * part, part), part)
        result = product(grad_gate[...], gate_copy[span, :], 1) + product(grad_up[...], up_copy[span, :], 1)
        kept[:, span] = result[:rows]
        sent[:, span] = result[rows:].astype(jnp.bfloat16)

    if dots is not None:
        kept[:, columns:] = dots[:rows, :].astype(jnp.float32)
        sent[:, columns:] = dots[rows:, :]


def multiply_outputs(grad_gate, grad_up, gate_copy, up_copy, *dots):
    rows, hidden = grad_gate.shape
    columns = gate_copy.shape[0]
    total = columns + sum(value.shape[1] for value in dots)
    return pl.pallas_call(
        output_kernel,
        out_shape=(
            pltpu.VMEM((rows // 2, total), jnp.float32),
            pltpu.VMEM((rows // 2, total), jnp.bfloat16),
        ),
        in_specs=[pl.BlockSpec(memory_space=pltpu.VMEM)] * (4 + len(dots)),
        out_specs=(pl.BlockSpec(memory_space=pltpu.VMEM),) * 2,
        compiler_params=pltpu.CompilerParams(vmem_limit_bytes=OUTPUT_VMEM),
        cost_estimate=pl.CostEstimate(
            flops=4 * rows * columns * hidden, bytes_accessed=4 * rows * columns, transcendentals=0
        ),
    )(grad_gate, grad_up, gate_copy, up_copy, *dots)


def gathered_plan(tokens, out_grad, kept_mask, routes, router, gate_weight, up_weight, down_weight):
    row_count, width = tokens.shape
    expert_count = lax.axis_size("expert")
    columns = lax.broadcasted_iota(jnp.int32, (row_count, expert_count), 1)
    first_hot = (routes[:, 0:1] == columns).astype(jnp.float32)
    second_hot = (routes[:, 1:2] == columns).astype(jnp.float32)
    keep_rows = kept_mask.astype(jnp.float32)
    half = width // 2
    table = 128
    token_z = gather_z(tokens)
    logits = jnp.dot(tokens, router, preferred_element_type=jnp.float32)
    first_logit = jnp.sum(logits * first_hot, axis=1)
    second_logit = jnp.sum(logits * second_hot, axis=1)
    gate_first = jax.nn.sigmoid(first_logit - second_logit)
    gate_second = jax.nn.sigmoid(second_logit - first_logit)
    gate_table = (first_hot * gate_first[:, None] + second_hot * gate_second[:, None]) * keep_rows[:, None]
    gate_table = jnp.pad(gate_table.astype(jnp.bfloat16), ((0, 0), (0, table - expert_count)))
    grad_z = gather_z_whole(jnp.concatenate([gate_table, out_grad], axis=1))
    token_near = gather_near(token_z, half)
    token_far = gather_far(*token_near)
    grad_near = gather_near(after_others(grad_z, token_far), half + table)
    token_low, token_high = gather_core(token_near[0], token_far[0], token_near[1], token_far[1])
    before = multiply_tokens(0, token_low, gate_weight, up_weight)
    grad_far = gather_far(*after_others(grad_near, before[0]))
    after = multiply_tokens(half, token_high, gate_weight, up_weight, before[0], before[1])
    grad_far = after_others(grad_far, after[0])
    grad_halves = gather_core(grad_near[0], grad_far[0], grad_near[1], grad_far[1])
    expert = lax.axis_index("expert").astype(jnp.int32).reshape(1)
    grad_gate, grad_up, dots = multiply_grads(expert, *grad_halves, after[0], after[1], down_weight)
    kept, sent = multiply_outputs(grad_gate, grad_up, before[2], before[3], dots)
    chunk = scatter_core(kept, sent)
    kept, sent = multiply_outputs(grad_gate, grad_up, after[2], after[3])
    chunk = scatter_far(after_others(chunk, sent), half // 2)
    later = scatter_core(kept, sent)
    chunk = scatter_near(*after_others(chunk, later))
    later = scatter_far(later, half // 2)
    chunk = scatter_z(after_others(chunk, later))
    later = scatter_z(scatter_near(*later))
    expert_sum = jnp.concatenate([chunk[:, :half], later], axis=1)
    dot_table = chunk[:, half:half + expert_count]
    dot_first = jnp.sum(dot_table * first_hot, axis=1)
    dot_second = jnp.sum(dot_table * second_hot, axis=1)
    product = gate_first * gate_second * keep_rows
    grad_first = product * (dot_first - dot_second)
    grad_second = product * (dot_second - dot_first)
    logit_grad = first_hot * grad_first[:, None] + second_hot * grad_second[:, None]
    router_term = jnp.dot(logit_grad, router.astype(jnp.float32).T, precision=lax.Precision.HIGHEST)
    d_tokens = ((expert_sum + router_term) * keep_rows[:, None]).astype(jnp.bfloat16)
    gate_grad = jnp.stack([grad_first, grad_second], axis=1)
    return (d_tokens, gate_grad)


def solution(mesh):
    gathers = mesh.shape["seq"] == 2 and mesh.shape["expert"] == 4
    return jax.shard_map(
        gathered_plan if gathers else routed_plan,
        mesh=mesh,
        in_specs=(
            P(("seq", "expert", "mp"), None),
            P(("seq", "expert", "mp"), None),
            P(("seq", "expert", "mp")),
            P(("seq", "expert", "mp"), None),
            P(),
            P("expert", None, ("seq", "mp")),
            P("expert", None, ("seq", "mp")),
            P("expert", ("seq", "mp"), None),
        ),
        out_specs=(P(("seq", "expert", "mp"), None), P(("seq", "expert", "mp"), None)),
        check_vma=False,
    )
```

```python
import functools
import math

import jax
import jax.numpy as jnp
from jax import lax
from jax.experimental import pallas as pl
from jax.experimental.pallas import tpu as pltpu
from jax.sharding import PartitionSpec as P

TOKEN_PART = 512
HIDDEN_PART = 256
COLUMN_PART = 512
TOKEN_VMEM = 16 * 2 ** 20
GRAD_VMEM = 20 * 2 ** 20
OUTPUT_VMEM = 16 * 2 ** 20


def routed_plan(tokens, out_grad, kept_mask, routes, router, gate_weight, up_weight, down_weight):
    row_count = tokens.shape[0]
    width = tokens.shape[1]
    expert_count = lax.axis_size("expert")
    capacity = max(3 * row_count // 8, 2 * row_count // expert_count)
    logits = jnp.dot(tokens, router, preferred_element_type=jnp.float32)
    columns = lax.broadcasted_iota(jnp.int32, (row_count, expert_count), 1)
    first_hot = (routes[:, 0:1] == columns).astype(jnp.float32)
    second_hot = (routes[:, 1:2] == columns).astype(jnp.float32)
    first_logit = jnp.sum(logits * first_hot, axis=1)
    second_logit = jnp.sum(logits * second_hot, axis=1)
    gate_first = jax.nn.sigmoid(first_logit - second_logit)
    gate_second = jax.nn.sigmoid(second_logit - first_logit)
    keep_rows = kept_mask.astype(jnp.float32)
    chosen = ((first_hot + second_hot) * keep_rows[:, None]).astype(jnp.int32)
    position = jnp.cumsum(chosen, axis=0) - 1
    slot_iota = lax.broadcasted_iota(jnp.int32, (row_count, expert_count, capacity), 2)
    select_mask = (chosen[:, :, None] == 1) & (position[:, :, None] == slot_iota)
    select_bf = select_mask.astype(jnp.bfloat16)
    select_full = select_mask.astype(jnp.float32)
    token_send = jnp.einsum(
        "tec,td->ecd", select_bf, tokens, preferred_element_type=jnp.float32
    ).astype(jnp.bfloat16)
    grad_send = jnp.einsum(
        "tec,td->ecd", select_bf, out_grad, preferred_element_type=jnp.float32
    ).astype(jnp.bfloat16)
    gate_table = first_hot * gate_first[:, None] + second_hot * gate_second[:, None]
    gate_send = jnp.einsum(
        "tec,te->ec", select_full, gate_table, precision=lax.Precision.HIGHEST
    ).astype(jnp.bfloat16)
    token_recv, grad_recv, gate_recv = (
        lax.all_to_all(token_send, "expert", split_axis=0, concat_axis=0, tiled=True),
        lax.all_to_all(grad_send, "expert", split_axis=0, concat_axis=0, tiled=True),
        lax.all_to_all(gate_send, "expert", split_axis=0, concat_axis=0, tiled=True),
    )
    token_all, grad_all, gate_all = (
        lax.all_gather(token_recv, ("seq", "mp"), axis=0, tiled=True),
        lax.all_gather(grad_recv, ("seq", "mp"), axis=0, tiled=True),
        lax.all_gather(gate_recv, ("seq", "mp"), axis=0, tiled=True),
    )
    token_all = token_all.reshape(-1, width)
    grad_all = grad_all.reshape(-1, width)
    gate_all = gate_all.reshape(-1)
    gate_local = gate_weight[0]
    up_local = up_weight[0]
    down_local = down_weight[0]
    pre_gate = jnp.dot(token_all, gate_local, preferred_element_type=jnp.float32)
    pre_up = jnp.dot(token_all, up_local, preferred_element_type=jnp.float32)
    sigma = jax.nn.sigmoid(pre_gate)
    act = pre_gate * sigma
    hidden = act * pre_up
    grad_hidden = jnp.dot(grad_all, down_local.T, preferred_element_type=jnp.float32)
    gate_dot = jnp.sum(grad_hidden * hidden, axis=1)
    scaled = gate_all.astype(jnp.float32)[:, None] * grad_hidden
    grad_gate = (scaled * pre_up * sigma * (1.0 + pre_gate * (1.0 - sigma))).astype(jnp.bfloat16)
    grad_up = (scaled * act).astype(jnp.bfloat16)
    expert_grad = jnp.dot(grad_gate, gate_local.T, preferred_element_type=jnp.float32)
    expert_grad = expert_grad + jnp.dot(grad_up, up_local.T, preferred_element_type=jnp.float32)
    grad_own = lax.psum_scatter(
        expert_grad.astype(jnp.bfloat16), ("seq", "mp"), scatter_dimension=0, tiled=True
    ).astype(jnp.float32)
    dot_own = lax.psum_scatter(gate_dot, ("seq", "mp"), scatter_dimension=0, tiled=True)
    grad_back, dot_back = (
        lax.all_to_all(
            grad_own.reshape(expert_count, capacity, width).astype(jnp.bfloat16),
            "expert",
            split_axis=0,
            concat_axis=0,
            tiled=True,
        ).astype(jnp.float32),
        lax.all_to_all(
            dot_own.reshape(expert_count, capacity).astype(jnp.bfloat16),
            "expert",
            split_axis=0,
            concat_axis=0,
            tiled=True,
        ).astype(jnp.float32),
    )
    expert_sum = jnp.einsum("tec,ecd->td", select_full, grad_back, precision=lax.Precision.HIGHEST)
    dot_table = jnp.einsum("tec,ec->te", select_full, dot_back, precision=lax.Precision.HIGHEST)
    dot_first = jnp.sum(dot_table * first_hot, axis=1)
    dot_second = jnp.sum(dot_table * second_hot, axis=1)
    product = gate_first * gate_second * keep_rows
    grad_first = product * (dot_first - dot_second)
    grad_second = product * (dot_second - dot_first)
    logit_grad = first_hot * grad_first[:, None] + second_hot * grad_second[:, None]
    router_term = jnp.dot(logit_grad, router.astype(jnp.float32).T, precision=lax.Precision.HIGHEST)
    d_tokens = ((expert_sum + router_term) * keep_rows[:, None]).astype(jnp.bfloat16)
    gate_grad = jnp.stack([grad_first, grad_second], axis=1)
    return (d_tokens, gate_grad)

def shift(value, axis, step):
    size = lax.axis_size(axis)
    return lax.ppermute(value, axis, [((i + step) % size, i) for i in range(size)])


def swap(value, axis, bit):
    return lax.ppermute(value, axis, [(i ^ bit, i) for i in range(lax.axis_size(axis))])


def swap_x(value):
    return swap(value, "seq", 1)


def swap_y(value):
    return swap(value, "expert", 2)


def swap_core(value):
    return swap(value, "expert", 1)


def after_others(values, others):
    return lax.optimization_barrier((values, others))[0]


def gather_z(rows):
    return [rows] + [shift(rows, "mp", k) for k in range(1, lax.axis_size("mp"))]


def gather_near(z_rows, cut):
    rows = jnp.concatenate(z_rows, axis=0)
    low, high = rows[:, :cut], rows[:, cut:]
    return [low, swap_x(low)], [high, swap_y(high)]


def gather_far(low, high):
    return swap_y(jnp.concatenate(low, axis=0)), swap_x(jnp.concatenate(high, axis=0))


def gather_core(low, low_far, high, high_far):
    high_far = jnp.split(high_far, 2, axis=0)
    low = jnp.concatenate(low + [low_far], axis=0)
    high = jnp.concatenate([high[0], high_far[0], high[1], high_far[1]], axis=0)
    return tuple(jnp.concatenate([mine, swap_core(mine)], axis=0) for mine in (low, high))


def scatter_core(kept, sent):
    return kept + swap_core(sent).astype(jnp.float32)


def send(value, exchange):
    return exchange(value.astype(jnp.bfloat16)).astype(jnp.float32)


def scatter_far(total, cut):
    low, low_x, low_y, low_both = jnp.split(total[:, :cut], 4, axis=0)
    high, high_x, high_y, high_both = jnp.split(total[:, cut:], 4, axis=0)
    low_far = send(jnp.concatenate([low_y, low_both], axis=0), swap_y)
    high_far = send(jnp.concatenate([high_x, high_both], axis=0), swap_x)
    return jnp.concatenate([low, low_x], axis=0) + low_far, jnp.concatenate([high, high_y], axis=0) + high_far


def scatter_near(low, high):
    low, low_x = jnp.split(low, 2, axis=0)
    high, high_y = jnp.split(high, 2, axis=0)
    return jnp.concatenate([low + send(low_x, swap_x), high + send(high_y, swap_y)], axis=1)


def scatter_z(total):
    size = lax.axis_size("mp")
    rows = total.shape[0] // size
    result = total[:rows]
    for k in range(1, size):
        result = result + send(total[k * rows:(k + 1) * rows], lambda value: shift(value, "mp", size - k))
    return result


def product(a, b, b_dim):
    return lax.dot_general(a, b, (((1,), (b_dim,)), ((), ())), preferred_element_type=jnp.float32)


def part_of(length, wanted):
    return math.gcd(length, wanted)


def in_hbm(value):
    return pltpu.with_memory_space_constraint(value, pltpu.HBM)


def fetch_kernel(first, *refs):
    count = (len(refs) - 1) // 2
    sems = refs[-1]
    copies = []
    for index in range(count):
        target = refs[count + index]
        source = refs[index].at[0, pl.ds(first, target.shape[0])]
        copies.append(pltpu.make_async_copy(source, target, sems.at[index]))
    for copy in copies:
        copy.start()
    for copy in copies:
        copy.wait()


def fetch(first, length, *weights):
    shapes = [(length, value.shape[2]) for value in weights]
    return pl.pallas_call(
        functools.partial(fetch_kernel, first),
        out_shape=tuple(pltpu.VMEM(shape, jnp.bfloat16) for shape in shapes),
        in_specs=[pl.BlockSpec(memory_space=pl.ANY)] * len(weights),
        out_specs=(pl.BlockSpec(memory_space=pltpu.VMEM),) * len(weights),
        scratch_shapes=[pltpu.SemaphoreType.DMA((len(weights),))],
        compiler_params=pltpu.CompilerParams(vmem_limit_bytes=TOKEN_VMEM),
        cost_estimate=pl.CostEstimate(
            flops=0, bytes_accessed=sum(2 * rows * hidden for rows, hidden in shapes), transcendentals=0
        ),
    )(*[in_hbm(value) for value in weights])


def token_kernel(first, tokens, gate, up, *refs):
    pre_gate, pre_up = refs[2:4]
    depth = part_of(tokens.shape[1], TOKEN_PART)
    copies = []
    if first:
        for index in range(2):
            source = refs[index].at[0, pl.ds(first, gate.shape[0])]
            copies.append(pltpu.make_async_copy(source, refs[4 + index], refs[6].at[index]))
    for copy in copies:
        copy.start()
    pre_gate[...] = jnp.zeros_like(pre_gate) if first else refs[0][...]
    pre_up[...] = jnp.zeros_like(pre_up) if first else refs[1][...]

    @pl.loop(0, tokens.shape[1] // depth)
    def _(step):
        rows = pl.ds(pl.multiple_of(step * depth, depth), depth)
        pre_gate[...] += product(tokens[:, rows], gate[rows, :], 0)
        pre_up[...] += product(tokens[:, rows], up[rows, :], 0)

    for copy in copies:
        copy.wait()


def multiply_tokens(tokens, gate, up, first, *others):
    rows, width = tokens.shape
    hidden = gate.shape[1]
    sums = (pltpu.VMEM((rows, hidden), jnp.float32),) * 2
    fetched = (pltpu.VMEM(gate.shape, jnp.bfloat16),) * 2 if first else ()
    if first:
        others = [in_hbm(value) for value in others]
    return pl.pallas_call(
        functools.partial(token_kernel, first),
        out_shape=sums + fetched,
        in_specs=[pl.BlockSpec(memory_space=pltpu.VMEM)] * 3
        + [pl.BlockSpec(memory_space=pl.ANY if first else pltpu.VMEM)] * 2,
        out_specs=(pl.BlockSpec(memory_space=pltpu.VMEM),) * len(sums + fetched),
        scratch_shapes=[pltpu.SemaphoreType.DMA((2,))] if first else [],
        compiler_params=pltpu.CompilerParams(vmem_limit_bytes=TOKEN_VMEM),
        cost_estimate=pl.CostEstimate(
            flops=4 * rows * width * hidden, bytes_accessed=2 * rows * width, transcendentals=0
        ),
    )(tokens, gate, up, *others)


def grad_kernel(
    expert, low, high, pre_gate, pre_up, down_weight, grad_gate, grad_up, dots, gate_rows, dot_sums, down, down_sems
):
    table = low.shape[1] - high.shape[1]
    half = high.shape[1]
    hidden = down.shape[0]
    depth = part_of(hidden, HIDDEN_PART)
    steps = hidden // depth

    def copy_of(index):
        rows = pl.ds(pl.multiple_of(index * depth, depth), depth)
        return pltpu.make_async_copy(down_weight.at[0, rows], down.at[rows], down_sems.at[index])

    @pl.loop(0, steps)
    def _(index):
        copy_of(index).start()

    lanes = lax.broadcasted_iota(jnp.int32, (low.shape[0], table), 1)
    gate_rows[...] = jnp.sum(
        jnp.where(lanes == expert[0], low[:, :table].astype(jnp.float32), 0.0), axis=1, keepdims=True
    )
    dot_sums[...] = jnp.zeros_like(dot_sums)

    @pl.loop(0, steps)
    def _(step):
        copy_of(step).wait()
        span = pl.ds(pl.multiple_of(step * depth, depth), depth)
        grad_hidden = product(low[:, table:], down[span, :half], 1) + product(high[...], down[span, half:], 1)
        gates = pre_gate[:, span]
        ups = pre_up[:, span]
        sigma = jax.nn.sigmoid(gates)
        act = gates * sigma
        dot_sums[...] += jnp.sum(grad_hidden * (act * ups), axis=1, keepdims=True)
        scaled = gate_rows[...] * grad_hidden
        grad_gate[:, span] = (scaled * ups * sigma * (1.0 + gates * (1.0 - sigma))).astype(jnp.bfloat16)
        grad_up[:, span] = (scaled * act).astype(jnp.bfloat16)

    dots[...] = jnp.where(lanes == expert[0], dot_sums[...], 0.0).astype(jnp.bfloat16)


def multiply_grads(expert, low, high, pre_gate, pre_up, down_weight):
    rows, hidden = pre_gate.shape
    width = down_weight.shape[2]
    table = low.shape[1] - high.shape[1]
    return pl.pallas_call(
        grad_kernel,
        out_shape=(
            pltpu.VMEM((rows, hidden), jnp.bfloat16),
            pltpu.VMEM((rows, hidden), jnp.bfloat16),
            pltpu.VMEM((rows, table), jnp.bfloat16),
        ),
        in_specs=[pl.BlockSpec(memory_space=pltpu.SMEM)]
        + [pl.BlockSpec(memory_space=pltpu.VMEM)] * 4
        + [pl.BlockSpec(memory_space=pl.ANY)],
        out_specs=(pl.BlockSpec(memory_space=pltpu.VMEM),) * 3,
        scratch_shapes=[
            pltpu.VMEM((rows, 1), jnp.float32),
            pltpu.VMEM((rows, 1), jnp.float32),
            pltpu.VMEM((hidden, width), jnp.bfloat16),
            pltpu.SemaphoreType.DMA((hidden // part_of(hidden, HIDDEN_PART),)),
        ],
        compiler_params=pltpu.CompilerParams(vmem_limit_bytes=GRAD_VMEM),
        cost_estimate=pl.CostEstimate(
            flops=2 * rows * width * hidden, bytes_accessed=2 * width * hidden, transcendentals=rows * hidden
        ),
    )(expert, low, high, pre_gate, pre_up, in_hbm(down_weight))


def output_kernel(grad_gate, grad_up, gate_copy, up_copy, *refs):
    dots, kept, sent = refs if len(refs) == 3 else (None,) + refs
    rows = kept.shape[0]
    columns = kept.shape[1] - (0 if dots is None else dots.shape[1])
    part = part_of(columns, COLUMN_PART)

    @pl.loop(0, columns // part)
    def _(step):
        span = pl.ds(pl.multiple_of(step * part, part), part)
        result = product(grad_gate[...], gate_copy[span, :], 1) + product(grad_up[...], up_copy[span, :], 1)
        kept[:, span] = result[:rows]
        sent[:, span] = result[rows:].astype(jnp.bfloat16)

    if dots is not None:
        kept[:, columns:] = dots[:rows, :].astype(jnp.float32)
        sent[:, columns:] = dots[rows:, :]


def multiply_outputs(grad_gate, grad_up, gate_copy, up_copy, *dots):
    rows, hidden = grad_gate.shape
    columns = gate_copy.shape[0]
    total = columns + sum(value.shape[1] for value in dots)
    return pl.pallas_call(
        output_kernel,
        out_shape=(
            pltpu.VMEM((rows // 2, total), jnp.float32),
            pltpu.VMEM((rows // 2, total), jnp.bfloat16),
        ),
        in_specs=[pl.BlockSpec(memory_space=pltpu.VMEM)] * (4 + len(dots)),
        out_specs=(pl.BlockSpec(memory_space=pltpu.VMEM),) * 2,
        compiler_params=pltpu.CompilerParams(vmem_limit_bytes=OUTPUT_VMEM),
        cost_estimate=pl.CostEstimate(
            flops=4 * rows * columns * hidden, bytes_accessed=4 * rows * columns, transcendentals=0
        ),
    )(grad_gate, grad_up, gate_copy, up_copy, *dots)


def gathered_plan(tokens, out_grad, kept_mask, routes, router, gate_weight, up_weight, down_weight):
    row_count, width = tokens.shape
    expert_count = lax.axis_size("expert")
    columns = lax.broadcasted_iota(jnp.int32, (row_count, expert_count), 1)
    first_hot = (routes[:, 0:1] == columns).astype(jnp.float32)
    second_hot = (routes[:, 1:2] == columns).astype(jnp.float32)
    keep_rows = kept_mask.astype(jnp.float32)
    half = width // 2
    table = 128
    token_z = gather_z(tokens)
    logits = jnp.dot(tokens, router, preferred_element_type=jnp.float32)
    first_logit = jnp.sum(logits * first_hot, axis=1)
    second_logit = jnp.sum(logits * second_hot, axis=1)
    gate_first = jax.nn.sigmoid(first_logit - second_logit)
    gate_second = jax.nn.sigmoid(second_logit - first_logit)
    gate_table = (first_hot * gate_first[:, None] + second_hot * gate_second[:, None]) * keep_rows[:, None]
    gate_table = jnp.pad(gate_table.astype(jnp.bfloat16), ((0, 0), (0, table - expert_count)))
    grad_z = gather_z(after_others(jnp.concatenate([gate_table, out_grad], axis=1), token_z[1]))
    gate_low, up_low = fetch(0, half, gate_weight, up_weight)
    token_near = gather_near(token_z, half)
    token_far = after_others(gather_far(*token_near), (gate_low, up_low))
    grad_near = gather_near(grad_z, half + table)
    grad_far = gather_far(*grad_near)
    token_low, token_high = gather_core(token_near[0], token_far[0], token_near[1], token_far[1])
    pre_gate, pre_up, gate_high, up_high = multiply_tokens(token_low, gate_low, up_low, half, gate_weight, up_weight)
    grad_far = after_others(grad_far, pre_gate)
    pre_gate, pre_up = multiply_tokens(token_high, gate_high, up_high, 0, pre_gate, pre_up)
    grad_halves = gather_core(grad_near[0], grad_far[0], grad_near[1], grad_far[1])
    expert = lax.axis_index("expert").astype(jnp.int32).reshape(1)
    grad_gate, grad_up, dots = multiply_grads(expert, *grad_halves, pre_gate, pre_up, down_weight)
    kept, sent = multiply_outputs(grad_gate, grad_up, gate_low, up_low, dots)
    chunk = scatter_core(kept, sent)
    kept, sent = multiply_outputs(grad_gate, grad_up, gate_high, up_high)
    chunk = scatter_far(after_others(chunk, sent), half // 2)
    later = scatter_core(kept, sent)
    chunk = scatter_near(*after_others(chunk, later))
    later = scatter_far(later, half // 2)
    chunk = scatter_z(after_others(chunk, later))
    later = scatter_z(scatter_near(*later))
    expert_sum = jnp.concatenate([chunk[:, :half], later], axis=1)
    dot_table = chunk[:, half:half + expert_count]
    dot_first = jnp.sum(dot_table * first_hot, axis=1)
    dot_second = jnp.sum(dot_table * second_hot, axis=1)
    product = gate_first * gate_second * keep_rows
    grad_first = product * (dot_first - dot_second)
    grad_second = product * (dot_second - dot_first)
    logit_grad = first_hot * grad_first[:, None] + second_hot * grad_second[:, None]
    router_term = jnp.dot(logit_grad, router.astype(jnp.float32).T, precision=lax.Precision.HIGHEST)
    d_tokens = ((expert_sum + router_term) * keep_rows[:, None]).astype(jnp.bfloat16)
    gate_grad = jnp.stack([grad_first, grad_second], axis=1)
    return (d_tokens, gate_grad)


def solution(mesh):
    gathers = mesh.shape["seq"] == 2 and mesh.shape["expert"] == 4
    return jax.shard_map(
        gathered_plan if gathers else routed_plan,
        mesh=mesh,
        in_specs=(
            P(("seq", "expert", "mp"), None),
            P(("seq", "expert", "mp"), None),
            P(("seq", "expert", "mp")),
            P(("seq", "expert", "mp"), None),
            P(),
            P("expert", None, ("seq", "mp")),
            P("expert", None, ("seq", "mp")),
            P("expert", ("seq", "mp"), None),
        ),
        out_specs=(P(("seq", "expert", "mp"), None), P(("seq", "expert", "mp"), None)),
        check_vma=False,
    )
```

```python
import functools
import math

import jax
import jax.numpy as jnp
from jax import lax
from jax.experimental import pallas as pl
from jax.experimental.pallas import tpu as pltpu
from jax.sharding import PartitionSpec as P

TOKEN_PART = 512
HIDDEN_PART = 256
COLUMN_PART = 512
TOKEN_VMEM = 6 * 2 ** 20
GRAD_VMEM = 12 * 2 ** 20
OUTPUT_VMEM = 6 * 2 ** 20


def routed_plan(tokens, out_grad, kept_mask, routes, router, gate_weight, up_weight, down_weight):
    row_count = tokens.shape[0]
    width = tokens.shape[1]
    expert_count = lax.axis_size("expert")
    capacity = max(3 * row_count // 8, 2 * row_count // expert_count)
    logits = jnp.dot(tokens, router, preferred_element_type=jnp.float32)
    columns = lax.broadcasted_iota(jnp.int32, (row_count, expert_count), 1)
    first_hot = (routes[:, 0:1] == columns).astype(jnp.float32)
    second_hot = (routes[:, 1:2] == columns).astype(jnp.float32)
    first_logit = jnp.sum(logits * first_hot, axis=1)
    second_logit = jnp.sum(logits * second_hot, axis=1)
    gate_first = jax.nn.sigmoid(first_logit - second_logit)
    gate_second = jax.nn.sigmoid(second_logit - first_logit)
    keep_rows = kept_mask.astype(jnp.float32)
    chosen = ((first_hot + second_hot) * keep_rows[:, None]).astype(jnp.int32)
    position = jnp.cumsum(chosen, axis=0) - 1
    slot_iota = lax.broadcasted_iota(jnp.int32, (row_count, expert_count, capacity), 2)
    select_mask = (chosen[:, :, None] == 1) & (position[:, :, None] == slot_iota)
    select_bf = select_mask.astype(jnp.bfloat16)
    select_full = select_mask.astype(jnp.float32)
    token_send = jnp.einsum(
        "tec,td->ecd", select_bf, tokens, preferred_element_type=jnp.float32
    ).astype(jnp.bfloat16)
    grad_send = jnp.einsum(
        "tec,td->ecd", select_bf, out_grad, preferred_element_type=jnp.float32
    ).astype(jnp.bfloat16)
    gate_table = first_hot * gate_first[:, None] + second_hot * gate_second[:, None]
    gate_send = jnp.einsum(
        "tec,te->ec", select_full, gate_table, precision=lax.Precision.HIGHEST
    ).astype(jnp.bfloat16)
    token_recv, grad_recv, gate_recv = (
        lax.all_to_all(token_send, "expert", split_axis=0, concat_axis=0, tiled=True),
        lax.all_to_all(grad_send, "expert", split_axis=0, concat_axis=0, tiled=True),
        lax.all_to_all(gate_send, "expert", split_axis=0, concat_axis=0, tiled=True),
    )
    token_all, grad_all, gate_all = (
        lax.all_gather(token_recv, ("seq", "mp"), axis=0, tiled=True),
        lax.all_gather(grad_recv, ("seq", "mp"), axis=0, tiled=True),
        lax.all_gather(gate_recv, ("seq", "mp"), axis=0, tiled=True),
    )
    token_all = token_all.reshape(-1, width)
    grad_all = grad_all.reshape(-1, width)
    gate_all = gate_all.reshape(-1)
    gate_local = gate_weight[0]
    up_local = up_weight[0]
    down_local = down_weight[0]
    pre_gate = jnp.dot(token_all, gate_local, preferred_element_type=jnp.float32)
    pre_up = jnp.dot(token_all, up_local, preferred_element_type=jnp.float32)
    sigma = jax.nn.sigmoid(pre_gate)
    act = pre_gate * sigma
    hidden = act * pre_up
    grad_hidden = jnp.dot(grad_all, down_local.T, preferred_element_type=jnp.float32)
    gate_dot = jnp.sum(grad_hidden * hidden, axis=1)
    scaled = gate_all.astype(jnp.float32)[:, None] * grad_hidden
    grad_gate = (scaled * pre_up * sigma * (1.0 + pre_gate * (1.0 - sigma))).astype(jnp.bfloat16)
    grad_up = (scaled * act).astype(jnp.bfloat16)
    expert_grad = jnp.dot(grad_gate, gate_local.T, preferred_element_type=jnp.float32)
    expert_grad = expert_grad + jnp.dot(grad_up, up_local.T, preferred_element_type=jnp.float32)
    grad_own = lax.psum_scatter(
        expert_grad.astype(jnp.bfloat16), ("seq", "mp"), scatter_dimension=0, tiled=True
    ).astype(jnp.float32)
    dot_own = lax.psum_scatter(gate_dot, ("seq", "mp"), scatter_dimension=0, tiled=True)
    grad_back, dot_back = (
        lax.all_to_all(
            grad_own.reshape(expert_count, capacity, width).astype(jnp.bfloat16),
            "expert",
            split_axis=0,
            concat_axis=0,
            tiled=True,
        ).astype(jnp.float32),
        lax.all_to_all(
            dot_own.reshape(expert_count, capacity).astype(jnp.bfloat16),
            "expert",
            split_axis=0,
            concat_axis=0,
            tiled=True,
        ).astype(jnp.float32),
    )
    expert_sum = jnp.einsum("tec,ecd->td", select_full, grad_back, precision=lax.Precision.HIGHEST)
    dot_table = jnp.einsum("tec,ec->te", select_full, dot_back, precision=lax.Precision.HIGHEST)
    dot_first = jnp.sum(dot_table * first_hot, axis=1)
    dot_second = jnp.sum(dot_table * second_hot, axis=1)
    product = gate_first * gate_second * keep_rows
    grad_first = product * (dot_first - dot_second)
    grad_second = product * (dot_second - dot_first)
    logit_grad = first_hot * grad_first[:, None] + second_hot * grad_second[:, None]
    router_term = jnp.dot(logit_grad, router.astype(jnp.float32).T, precision=lax.Precision.HIGHEST)
    d_tokens = ((expert_sum + router_term) * keep_rows[:, None]).astype(jnp.bfloat16)
    gate_grad = jnp.stack([grad_first, grad_second], axis=1)
    return (d_tokens, gate_grad)

def shift(value, axis, step):
    size = lax.axis_size(axis)
    return lax.ppermute(value, axis, [((i + step) % size, i) for i in range(size)])


def swap(value, axis, bit):
    return lax.ppermute(value, axis, [(i ^ bit, i) for i in range(lax.axis_size(axis))])


def swap_x(value):
    return swap(value, "seq", 1)


def swap_y(value):
    return swap(value, "expert", 2)


def swap_core(value):
    return swap(value, "expert", 1)


def after_others(values, others):
    return lax.optimization_barrier((values, others))[0]


def gather_z(rows):
    return [rows] + [shift(rows, "mp", k) for k in range(1, lax.axis_size("mp"))]


def gather_near(z_rows, cut):
    rows = jnp.concatenate(z_rows, axis=0)
    low, high = rows[:, :cut], rows[:, cut:]
    return [low, swap_x(low)], [high, swap_y(high)]


def gather_far(low, high):
    return swap_y(jnp.concatenate(low, axis=0)), swap_x(jnp.concatenate(high, axis=0))


def gather_core(low, low_far, high, high_far):
    high_far = jnp.split(high_far, 2, axis=0)
    low = jnp.concatenate(low + [low_far], axis=0)
    high = jnp.concatenate([high[0], high_far[0], high[1], high_far[1]], axis=0)
    return tuple(jnp.concatenate([mine, swap_core(mine)], axis=0) for mine in (low, high))


def scatter_core(kept, sent):
    return kept + swap_core(sent).astype(jnp.float32)


def send(value, exchange):
    return exchange(value.astype(jnp.bfloat16)).astype(jnp.float32)


def scatter_far(total, cut):
    low, low_x, low_y, low_both = jnp.split(total[:, :cut], 4, axis=0)
    high, high_x, high_y, high_both = jnp.split(total[:, cut:], 4, axis=0)
    low_far = send(jnp.concatenate([low_y, low_both], axis=0), swap_y)
    high_far = send(jnp.concatenate([high_x, high_both], axis=0), swap_x)
    return jnp.concatenate([low, low_x], axis=0) + low_far, jnp.concatenate([high, high_y], axis=0) + high_far


def scatter_near(low, high):
    low, low_x = jnp.split(low, 2, axis=0)
    high, high_y = jnp.split(high, 2, axis=0)
    return jnp.concatenate([low + send(low_x, swap_x), high + send(high_y, swap_y)], axis=1)


def scatter_z(total):
    size = lax.axis_size("mp")
    rows = total.shape[0] // size
    result = total[:rows]
    for k in range(1, size):
        result = result + send(total[k * rows:(k + 1) * rows], lambda value: shift(value, "mp", size - k))
    return result


def product(a, b, b_dim):
    return lax.dot_general(a, b, (((1,), (b_dim,)), ((), ())), preferred_element_type=jnp.float32)


def part_of(length, wanted):
    return math.gcd(length, wanted)


def in_hbm(value):
    return pltpu.with_memory_space_constraint(value, pltpu.HBM)


def fetch_kernel(first, _, *refs):
    count = (len(refs) - 1) // 2
    sems = refs[-1]
    copies = []
    for index in range(count):
        target = refs[count + index]
        source = refs[index].at[0, pl.ds(first, target.shape[0])]
        copies.append(pltpu.make_async_copy(source, target, sems.at[index]))
    for copy in copies:
        copy.start()
    for copy in copies:
        copy.wait()


def fetch(first, length, earlier, *weights):
    shapes = [(length, value.shape[2]) for value in weights]
    return pl.pallas_call(
        functools.partial(fetch_kernel, first),
        out_shape=tuple(pltpu.VMEM(shape, jnp.bfloat16) for shape in shapes),
        in_specs=[pl.BlockSpec(memory_space=pl.ANY)] * (1 + len(weights)),
        out_specs=(pl.BlockSpec(memory_space=pltpu.VMEM),) * len(weights),
        scratch_shapes=[pltpu.SemaphoreType.DMA((len(weights),))],
        compiler_params=pltpu.CompilerParams(vmem_limit_bytes=TOKEN_VMEM),
        cost_estimate=pl.CostEstimate(
            flops=0, bytes_accessed=sum(2 * rows * hidden for rows, hidden in shapes), transcendentals=0
        ),
    )(earlier, *[in_hbm(value) for value in weights])


def token_kernel(first, tokens, gate, up, *refs):
    pre_gate, pre_up = refs[2:4]
    depth = part_of(tokens.shape[1], TOKEN_PART)
    copies = []
    if first:
        for index in range(2):
            source = refs[index].at[0, pl.ds(first, gate.shape[0])]
            copies.append(pltpu.make_async_copy(source, refs[4 + index], refs[6].at[index]))
    for copy in copies:
        copy.start()
    pre_gate[...] = jnp.zeros_like(pre_gate) if first else refs[0][...]
    pre_up[...] = jnp.zeros_like(pre_up) if first else refs[1][...]

    @pl.loop(0, tokens.shape[1] // depth)
    def _(step):
        rows = pl.ds(pl.multiple_of(step * depth, depth), depth)
        pre_gate[...] += product(tokens[:, rows], gate[rows, :], 0)
        pre_up[...] += product(tokens[:, rows], up[rows, :], 0)

    for copy in copies:
        copy.wait()


def multiply_tokens(tokens, gate, up, first, *others):
    rows, width = tokens.shape
    hidden = gate.shape[1]
    sums = (pltpu.VMEM((rows, hidden), jnp.float32),) * 2
    fetched = (pltpu.VMEM(gate.shape, jnp.bfloat16),) * 2 if first else ()
    if first:
        others = [in_hbm(value) for value in others]
    return pl.pallas_call(
        functools.partial(token_kernel, first),
        out_shape=sums + fetched,
        in_specs=[pl.BlockSpec(memory_space=pltpu.VMEM)] * 3
        + [pl.BlockSpec(memory_space=pl.ANY if first else pltpu.VMEM)] * 2,
        out_specs=(pl.BlockSpec(memory_space=pltpu.VMEM),) * len(sums + fetched),
        scratch_shapes=[pltpu.SemaphoreType.DMA((2,))] if first else [],
        compiler_params=pltpu.CompilerParams(vmem_limit_bytes=TOKEN_VMEM),
        cost_estimate=pl.CostEstimate(
            flops=4 * rows * width * hidden, bytes_accessed=2 * rows * width, transcendentals=0
        ),
    )(tokens, gate, up, *others)


def grad_kernel(
    expert, low, high, pre_gate, pre_up, down_weight, grad_gate, grad_up, dots, gate_rows, dot_sums, down, down_sems
):
    table = low.shape[1] - high.shape[1]
    half = high.shape[1]
    depth = down.shape[1]
    steps = pre_gate.shape[1] // depth

    def copy_of(index):
        rows = pl.ds(pl.multiple_of(index * depth, depth), depth)
        slot = lax.rem(index, 2)
        return pltpu.make_async_copy(down_weight.at[0, rows], down.at[slot], down_sems.at[slot])

    for index in range(min(2, steps)):
        copy_of(index).start()

    lanes = lax.broadcasted_iota(jnp.int32, (low.shape[0], table), 1)
    gate_rows[...] = jnp.sum(
        jnp.where(lanes == expert[0], low[:, :table].astype(jnp.float32), 0.0), axis=1, keepdims=True
    )
    dot_sums[...] = jnp.zeros_like(dot_sums)

    @pl.loop(0, steps)
    def _(step):
        copy_of(step).wait()
        block = down.at[lax.rem(step, 2)]
        span = pl.ds(pl.multiple_of(step * depth, depth), depth)
        grad_hidden = product(low[:, table:], block[:, :half], 1) + product(high[...], block[:, half:], 1)
        gates = pre_gate[:, span]
        ups = pre_up[:, span]
        sigma = jax.nn.sigmoid(gates)
        act = gates * sigma
        dot_sums[...] += jnp.sum(grad_hidden * (act * ups), axis=1, keepdims=True)
        scaled = gate_rows[...] * grad_hidden
        grad_gate[:, span] = (scaled * ups * sigma * (1.0 + gates * (1.0 - sigma))).astype(jnp.bfloat16)
        grad_up[:, span] = (scaled * act).astype(jnp.bfloat16)

        @pl.when(step + 2 < steps)
        def _():
            copy_of(step + 2).start()

    dots[...] = jnp.where(lanes == expert[0], dot_sums[...], 0.0).astype(jnp.bfloat16)


def multiply_grads(expert, low, high, pre_gate, pre_up, down_weight):
    rows, hidden = pre_gate.shape
    width = down_weight.shape[2]
    table = low.shape[1] - high.shape[1]
    return pl.pallas_call(
        grad_kernel,
        out_shape=(
            pltpu.VMEM((rows, hidden), jnp.bfloat16),
            pltpu.VMEM((rows, hidden), jnp.bfloat16),
            pltpu.VMEM((rows, table), jnp.bfloat16),
        ),
        in_specs=[pl.BlockSpec(memory_space=pltpu.SMEM)]
        + [pl.BlockSpec(memory_space=pltpu.VMEM)] * 4
        + [pl.BlockSpec(memory_space=pl.ANY)],
        out_specs=(pl.BlockSpec(memory_space=pltpu.VMEM),) * 3,
        scratch_shapes=[
            pltpu.VMEM((rows, 1), jnp.float32),
            pltpu.VMEM((rows, 1), jnp.float32),
            pltpu.VMEM((2, part_of(hidden, HIDDEN_PART), width), jnp.bfloat16),
            pltpu.SemaphoreType.DMA((2,)),
        ],
        compiler_params=pltpu.CompilerParams(vmem_limit_bytes=GRAD_VMEM),
        cost_estimate=pl.CostEstimate(
            flops=2 * rows * width * hidden, bytes_accessed=2 * width * hidden, transcendentals=rows * hidden
        ),
    )(expert, low, high, pre_gate, pre_up, in_hbm(down_weight))


def output_kernel(grad_gate, grad_up, gate_copy, up_copy, *refs):
    dots, kept, sent = refs if len(refs) == 3 else (None,) + refs
    rows = kept.shape[0]
    columns = kept.shape[1] - (0 if dots is None else dots.shape[1])
    part = part_of(columns, COLUMN_PART)

    @pl.loop(0, columns // part)
    def _(step):
        span = pl.ds(pl.multiple_of(step * part, part), part)
        result = product(grad_gate[...], gate_copy[span, :], 1) + product(grad_up[...], up_copy[span, :], 1)
        kept[:, span] = result[:rows]
        sent[:, span] = result[rows:].astype(jnp.bfloat16)

    if dots is not None:
        kept[:, columns:] = dots[:rows, :].astype(jnp.float32)
        sent[:, columns:] = dots[rows:, :]


def multiply_outputs(grad_gate, grad_up, gate_copy, up_copy, *dots):
    rows, hidden = grad_gate.shape
    columns = gate_copy.shape[0]
    total = columns + sum(value.shape[1] for value in dots)
    return pl.pallas_call(
        output_kernel,
        out_shape=(
            pltpu.VMEM((rows // 2, total), jnp.float32),
            pltpu.VMEM((rows // 2, total), jnp.bfloat16),
        ),
        in_specs=[pl.BlockSpec(memory_space=pltpu.VMEM)] * (4 + len(dots)),
        out_specs=(pl.BlockSpec(memory_space=pltpu.VMEM),) * 2,
        compiler_params=pltpu.CompilerParams(vmem_limit_bytes=OUTPUT_VMEM),
        cost_estimate=pl.CostEstimate(
            flops=4 * rows * columns * hidden, bytes_accessed=4 * rows * columns, transcendentals=0
        ),
    )(grad_gate, grad_up, gate_copy, up_copy, *dots)


def gathered_plan(tokens, out_grad, kept_mask, routes, router, gate_weight, up_weight, down_weight):
    row_count, width = tokens.shape
    expert_count = lax.axis_size("expert")
    columns = lax.broadcasted_iota(jnp.int32, (row_count, expert_count), 1)
    first_hot = (routes[:, 0:1] == columns).astype(jnp.float32)
    second_hot = (routes[:, 1:2] == columns).astype(jnp.float32)
    keep_rows = kept_mask.astype(jnp.float32)
    half = width // 2
    table = 128
    token_z = gather_z(tokens)
    logits = jnp.dot(tokens, router, preferred_element_type=jnp.float32)
    first_logit = jnp.sum(logits * first_hot, axis=1)
    second_logit = jnp.sum(logits * second_hot, axis=1)
    gate_first = jax.nn.sigmoid(first_logit - second_logit)
    gate_second = jax.nn.sigmoid(second_logit - first_logit)
    gate_table = (first_hot * gate_first[:, None] + second_hot * gate_second[:, None]) * keep_rows[:, None]
    gate_table = jnp.pad(gate_table.astype(jnp.bfloat16), ((0, 0), (0, table - expert_count)))
    grad_z = gather_z(after_others(jnp.concatenate([gate_table, out_grad], axis=1), token_z[1]))
    token_near = gather_near(token_z, half)
    gate_low, up_low = fetch(0, half, token_near[0][0], gate_weight, up_weight)
    token_near = after_others(token_near, (gate_low, up_low))
    token_far = gather_far(*token_near)
    grad_near = gather_near(grad_z, half + table)
    grad_far = gather_far(*grad_near)
    token_low, token_high = gather_core(token_near[0], token_far[0], token_near[1], token_far[1])
    pre_gate, pre_up, gate_high, up_high = multiply_tokens(token_low, gate_low, up_low, half, gate_weight, up_weight)
    grad_far = after_others(grad_far, pre_gate)
    pre_gate, pre_up = multiply_tokens(token_high, gate_high, up_high, 0, pre_gate, pre_up)
    grad_halves = gather_core(grad_near[0], grad_far[0], grad_near[1], grad_far[1])
    expert = lax.axis_index("expert").astype(jnp.int32).reshape(1)
    grad_gate, grad_up, dots = multiply_grads(expert, *grad_halves, pre_gate, pre_up, down_weight)
    kept, sent = multiply_outputs(grad_gate, grad_up, gate_low, up_low, dots)
    chunk = scatter_core(kept, sent)
    kept, sent = multiply_outputs(grad_gate, grad_up, gate_high, up_high)
    chunk = scatter_far(after_others(chunk, sent), half // 2)
    later = scatter_core(kept, sent)
    chunk = scatter_near(*after_others(chunk, later))
    later = scatter_far(later, half // 2)
    chunk = scatter_z(after_others(chunk, later))
    later = scatter_z(scatter_near(*later))
    expert_sum = jnp.concatenate([chunk[:, :half], later], axis=1)
    dot_table = chunk[:, half:half + expert_count]
    dot_first = jnp.sum(dot_table * first_hot, axis=1)
    dot_second = jnp.sum(dot_table * second_hot, axis=1)
    product = gate_first * gate_second * keep_rows
    grad_first = product * (dot_first - dot_second)
    grad_second = product * (dot_second - dot_first)
    logit_grad = first_hot * grad_first[:, None] + second_hot * grad_second[:, None]
    router_term = jnp.dot(logit_grad, router.astype(jnp.float32).T, precision=lax.Precision.HIGHEST)
    d_tokens = ((expert_sum + router_term) * keep_rows[:, None]).astype(jnp.bfloat16)
    gate_grad = jnp.stack([grad_first, grad_second], axis=1)
    return (d_tokens, gate_grad)


def solution(mesh):
    gathers = mesh.shape["seq"] == 2 and mesh.shape["expert"] == 4
    return jax.shard_map(
        gathered_plan if gathers else routed_plan,
        mesh=mesh,
        in_specs=(
            P(("seq", "expert", "mp"), None),
            P(("seq", "expert", "mp"), None),
            P(("seq", "expert", "mp")),
            P(("seq", "expert", "mp"), None),
            P(),
            P("expert", None, ("seq", "mp")),
            P("expert", None, ("seq", "mp")),
            P("expert", ("seq", "mp"), None),
        ),
        out_specs=(P(("seq", "expert", "mp"), None), P(("seq", "expert", "mp"), None)),
        check_vma=False,
    )
```

```python
import functools
import math

import jax
import jax.numpy as jnp
from jax import lax
from jax.experimental import pallas as pl
from jax.experimental.pallas import tpu as pltpu
from jax.sharding import PartitionSpec as P

TOKEN_PART = 512
HIDDEN_PART = 256
COLUMN_PART = 512
TOKEN_VMEM = 6 * 2 ** 20
GRAD_VMEM = 10 * 2 ** 20
OUTPUT_VMEM = 6 * 2 ** 20


def routed_plan(tokens, out_grad, kept_mask, routes, router, gate_weight, up_weight, down_weight):
    row_count = tokens.shape[0]
    width = tokens.shape[1]
    expert_count = lax.axis_size("expert")
    capacity = max(3 * row_count // 8, 2 * row_count // expert_count)
    logits = jnp.dot(tokens, router, preferred_element_type=jnp.float32)
    columns = lax.broadcasted_iota(jnp.int32, (row_count, expert_count), 1)
    first_hot = (routes[:, 0:1] == columns).astype(jnp.float32)
    second_hot = (routes[:, 1:2] == columns).astype(jnp.float32)
    first_logit = jnp.sum(logits * first_hot, axis=1)
    second_logit = jnp.sum(logits * second_hot, axis=1)
    gate_first = jax.nn.sigmoid(first_logit - second_logit)
    gate_second = jax.nn.sigmoid(second_logit - first_logit)
    keep_rows = kept_mask.astype(jnp.float32)
    chosen = ((first_hot + second_hot) * keep_rows[:, None]).astype(jnp.int32)
    position = jnp.cumsum(chosen, axis=0) - 1
    slot_iota = lax.broadcasted_iota(jnp.int32, (row_count, expert_count, capacity), 2)
    select_mask = (chosen[:, :, None] == 1) & (position[:, :, None] == slot_iota)
    select_bf = select_mask.astype(jnp.bfloat16)
    select_full = select_mask.astype(jnp.float32)
    token_send = jnp.einsum(
        "tec,td->ecd", select_bf, tokens, preferred_element_type=jnp.float32
    ).astype(jnp.bfloat16)
    grad_send = jnp.einsum(
        "tec,td->ecd", select_bf, out_grad, preferred_element_type=jnp.float32
    ).astype(jnp.bfloat16)
    gate_table = first_hot * gate_first[:, None] + second_hot * gate_second[:, None]
    gate_send = jnp.einsum(
        "tec,te->ec", select_full, gate_table, precision=lax.Precision.HIGHEST
    ).astype(jnp.bfloat16)
    token_recv, grad_recv, gate_recv = (
        lax.all_to_all(token_send, "expert", split_axis=0, concat_axis=0, tiled=True),
        lax.all_to_all(grad_send, "expert", split_axis=0, concat_axis=0, tiled=True),
        lax.all_to_all(gate_send, "expert", split_axis=0, concat_axis=0, tiled=True),
    )
    token_all, grad_all, gate_all = (
        lax.all_gather(token_recv, ("seq", "mp"), axis=0, tiled=True),
        lax.all_gather(grad_recv, ("seq", "mp"), axis=0, tiled=True),
        lax.all_gather(gate_recv, ("seq", "mp"), axis=0, tiled=True),
    )
    token_all = token_all.reshape(-1, width)
    grad_all = grad_all.reshape(-1, width)
    gate_all = gate_all.reshape(-1)
    gate_local = gate_weight[0]
    up_local = up_weight[0]
    down_local = down_weight[0]
    pre_gate = jnp.dot(token_all, gate_local, preferred_element_type=jnp.float32)
    pre_up = jnp.dot(token_all, up_local, preferred_element_type=jnp.float32)
    sigma = jax.nn.sigmoid(pre_gate)
    act = pre_gate * sigma
    hidden = act * pre_up
    grad_hidden = jnp.dot(grad_all, down_local.T, preferred_element_type=jnp.float32)
    gate_dot = jnp.sum(grad_hidden * hidden, axis=1)
    scaled = gate_all.astype(jnp.float32)[:, None] * grad_hidden
    grad_gate = (scaled * pre_up * sigma * (1.0 + pre_gate * (1.0 - sigma))).astype(jnp.bfloat16)
    grad_up = (scaled * act).astype(jnp.bfloat16)
    expert_grad = jnp.dot(grad_gate, gate_local.T, preferred_element_type=jnp.float32)
    expert_grad = expert_grad + jnp.dot(grad_up, up_local.T, preferred_element_type=jnp.float32)
    grad_own = lax.psum_scatter(
        expert_grad.astype(jnp.bfloat16), ("seq", "mp"), scatter_dimension=0, tiled=True
    ).astype(jnp.float32)
    dot_own = lax.psum_scatter(gate_dot, ("seq", "mp"), scatter_dimension=0, tiled=True)
    grad_back, dot_back = (
        lax.all_to_all(
            grad_own.reshape(expert_count, capacity, width).astype(jnp.bfloat16),
            "expert",
            split_axis=0,
            concat_axis=0,
            tiled=True,
        ).astype(jnp.float32),
        lax.all_to_all(
            dot_own.reshape(expert_count, capacity).astype(jnp.bfloat16),
            "expert",
            split_axis=0,
            concat_axis=0,
            tiled=True,
        ).astype(jnp.float32),
    )
    expert_sum = jnp.einsum("tec,ecd->td", select_full, grad_back, precision=lax.Precision.HIGHEST)
    dot_table = jnp.einsum("tec,ec->te", select_full, dot_back, precision=lax.Precision.HIGHEST)
    dot_first = jnp.sum(dot_table * first_hot, axis=1)
    dot_second = jnp.sum(dot_table * second_hot, axis=1)
    product = gate_first * gate_second * keep_rows
    grad_first = product * (dot_first - dot_second)
    grad_second = product * (dot_second - dot_first)
    logit_grad = first_hot * grad_first[:, None] + second_hot * grad_second[:, None]
    router_term = jnp.dot(logit_grad, router.astype(jnp.float32).T, precision=lax.Precision.HIGHEST)
    d_tokens = ((expert_sum + router_term) * keep_rows[:, None]).astype(jnp.bfloat16)
    gate_grad = jnp.stack([grad_first, grad_second], axis=1)
    return (d_tokens, gate_grad)

def shift(value, axis, step):
    size = lax.axis_size(axis)
    return lax.ppermute(value, axis, [((i + step) % size, i) for i in range(size)])


def swap(value, axis, bit):
    return lax.ppermute(value, axis, [(i ^ bit, i) for i in range(lax.axis_size(axis))])


def swap_x(value):
    return swap(value, "seq", 1)


def swap_y(value):
    return swap(value, "expert", 2)


def swap_core(value):
    return swap(value, "expert", 1)


def after_others(values, others):
    return lax.optimization_barrier((values, others))[0]


def gather_z(rows):
    return [rows] + [shift(rows, "mp", k) for k in range(1, lax.axis_size("mp"))]


def gather_near(z_rows, cut):
    rows = jnp.concatenate(z_rows, axis=0)
    low, high = rows[:, :cut], rows[:, cut:]
    return [low, swap_x(low)], [high, swap_y(high)]


def gather_far(low, high):
    return swap_y(jnp.concatenate(low, axis=0)), swap_x(jnp.concatenate(high, axis=0))


def gather_core(low, low_far, high, high_far):
    high_far = jnp.split(high_far, 2, axis=0)
    low = jnp.concatenate(low + [low_far], axis=0)
    high = jnp.concatenate([high[0], high_far[0], high[1], high_far[1]], axis=0)
    return tuple(jnp.concatenate([mine, swap_core(mine)], axis=0) for mine in (low, high))


def scatter_core(kept, sent):
    return kept + swap_core(sent).astype(jnp.float32)


def send(value, exchange):
    return exchange(value.astype(jnp.bfloat16)).astype(jnp.float32)


def scatter_far(total, cut):
    low, low_x, low_y, low_both = jnp.split(total[:, :cut], 4, axis=0)
    high, high_x, high_y, high_both = jnp.split(total[:, cut:], 4, axis=0)
    low_far = send(jnp.concatenate([low_y, low_both], axis=0), swap_y)
    high_far = send(jnp.concatenate([high_x, high_both], axis=0), swap_x)
    return jnp.concatenate([low, low_x], axis=0) + low_far, jnp.concatenate([high, high_y], axis=0) + high_far


def scatter_near(low, high):
    low, low_x = jnp.split(low, 2, axis=0)
    high, high_y = jnp.split(high, 2, axis=0)
    return jnp.concatenate([low + send(low_x, swap_x), high + send(high_y, swap_y)], axis=1)


def scatter_z(total):
    size = lax.axis_size("mp")
    rows = total.shape[0] // size
    result = total[:rows]
    for k in range(1, size):
        result = result + send(total[k * rows:(k + 1) * rows], lambda value: shift(value, "mp", size - k))
    return result


def product(a, b, b_dim):
    return lax.dot_general(a, b, (((1,), (b_dim,)), ((), ())), preferred_element_type=jnp.float32)


def part_of(length, wanted):
    return math.gcd(length, wanted)


def in_hbm(value):
    return pltpu.with_memory_space_constraint(value, pltpu.HBM)


def fetch_kernel(first, _, *refs):
    count = (len(refs) - 1) // 2
    sems = refs[-1]
    copies = []
    for index in range(count):
        target = refs[count + index]
        source = refs[index].at[0, pl.ds(first, target.shape[0])]
        copies.append(pltpu.make_async_copy(source, target, sems.at[index]))
    for copy in copies:
        copy.start()
    for copy in copies:
        copy.wait()


def fetch(first, length, earlier, *weights):
    shapes = [(length, value.shape[2]) for value in weights]
    return pl.pallas_call(
        functools.partial(fetch_kernel, first),
        out_shape=tuple(pltpu.VMEM(shape, jnp.bfloat16) for shape in shapes),
        in_specs=[pl.BlockSpec(memory_space=pl.ANY)] * (1 + len(weights)),
        out_specs=(pl.BlockSpec(memory_space=pltpu.VMEM),) * len(weights),
        scratch_shapes=[pltpu.SemaphoreType.DMA((len(weights),))],
        compiler_params=pltpu.CompilerParams(vmem_limit_bytes=TOKEN_VMEM),
        cost_estimate=pl.CostEstimate(
            flops=0, bytes_accessed=sum(2 * rows * hidden for rows, hidden in shapes), transcendentals=0
        ),
    )(earlier, *[in_hbm(value) for value in weights])


def token_kernel(first, tokens, gate, up, *refs):
    pre_gate, pre_up = refs[2:4]
    depth = part_of(tokens.shape[1], TOKEN_PART)
    copies = []
    if first:
        for index in range(2):
            source = refs[index].at[0, pl.ds(first, gate.shape[0])]
            copies.append(pltpu.make_async_copy(source, refs[4 + index], refs[6].at[index]))
    for copy in copies:
        copy.start()
    pre_gate[...] = jnp.zeros_like(pre_gate) if first else refs[0][...]
    pre_up[...] = jnp.zeros_like(pre_up) if first else refs[1][...]

    @pl.loop(0, tokens.shape[1] // depth)
    def _(step):
        rows = pl.ds(pl.multiple_of(step * depth, depth), depth)
        pre_gate[...] += product(tokens[:, rows], gate[rows, :], 0)
        pre_up[...] += product(tokens[:, rows], up[rows, :], 0)

    for copy in copies:
        copy.wait()


def multiply_tokens(tokens, gate, up, first, *others):
    rows, width = tokens.shape
    hidden = gate.shape[1]
    sums = (pltpu.VMEM((rows, hidden), jnp.float32),) * 2
    fetched = (pltpu.VMEM(gate.shape, jnp.bfloat16),) * 2 if first else ()
    if first:
        others = [in_hbm(value) for value in others]
    return pl.pallas_call(
        functools.partial(token_kernel, first),
        out_shape=sums + fetched,
        in_specs=[pl.BlockSpec(memory_space=pltpu.VMEM)] * 3
        + [pl.BlockSpec(memory_space=pl.ANY if first else pltpu.VMEM)] * 2,
        out_specs=(pl.BlockSpec(memory_space=pltpu.VMEM),) * len(sums + fetched),
        scratch_shapes=[pltpu.SemaphoreType.DMA((2,))] if first else [],
        compiler_params=pltpu.CompilerParams(vmem_limit_bytes=TOKEN_VMEM),
        cost_estimate=pl.CostEstimate(
            flops=4 * rows * width * hidden, bytes_accessed=2 * rows * width, transcendentals=0
        ),
    )(tokens, gate, up, *others)


def grad_kernel(
    expert, low, high, pre_gate, pre_up, down, down_weight, grad_gate, grad_up, dots, gate_rows, dot_sums, rest, sems
):
    table = low.shape[1] - high.shape[1]
    half = high.shape[1]
    ready = down.shape[0]
    depth = part_of(ready, HIDDEN_PART)
    steps = ready // depth

    def copy_of(index):
        rows = pl.ds(pl.multiple_of(index * depth, depth), depth)
        source = pl.ds(pl.multiple_of(ready + index * depth, depth), depth)
        return pltpu.make_async_copy(down_weight.at[0, source], rest.at[rows], sems.at[index])

    for index in range(steps):
        copy_of(index).start()

    lanes = lax.broadcasted_iota(jnp.int32, (low.shape[0], table), 1)
    gate_rows[...] = jnp.sum(
        jnp.where(lanes == expert[0], low[:, :table].astype(jnp.float32), 0.0), axis=1, keepdims=True
    )
    dot_sums[...] = jnp.zeros_like(dot_sums)

    def block(weights, first, step):
        rows = pl.ds(pl.multiple_of(step * depth, depth), depth)
        span = pl.ds(pl.multiple_of(first + step * depth, depth), depth)
        grad_hidden = product(low[:, table:], weights[rows, :half], 1) + product(high[...], weights[rows, half:], 1)
        gates = pre_gate[:, span]
        ups = pre_up[:, span]
        sigma = jax.nn.sigmoid(gates)
        act = gates * sigma
        dot_sums[...] += jnp.sum(grad_hidden * (act * ups), axis=1, keepdims=True)
        scaled = gate_rows[...] * grad_hidden
        grad_gate[:, span] = (scaled * ups * sigma * (1.0 + gates * (1.0 - sigma))).astype(jnp.bfloat16)
        grad_up[:, span] = (scaled * act).astype(jnp.bfloat16)

    @pl.loop(0, steps)
    def _(step):
        block(down, 0, step)

    @pl.loop(0, steps)
    def _(step):
        copy_of(step).wait()
        block(rest, ready, step)

    dots[...] = jnp.where(lanes == expert[0], dot_sums[...], 0.0).astype(jnp.bfloat16)


def multiply_grads(expert, low, high, pre_gate, pre_up, down, down_weight):
    rows, hidden = pre_gate.shape
    width = down_weight.shape[2]
    table = low.shape[1] - high.shape[1]
    return pl.pallas_call(
        grad_kernel,
        out_shape=(
            pltpu.VMEM((rows, hidden), jnp.bfloat16),
            pltpu.VMEM((rows, hidden), jnp.bfloat16),
            pltpu.VMEM((rows, table), jnp.bfloat16),
        ),
        in_specs=[pl.BlockSpec(memory_space=pltpu.SMEM)]
        + [pl.BlockSpec(memory_space=pltpu.VMEM)] * 5
        + [pl.BlockSpec(memory_space=pl.ANY)],
        out_specs=(pl.BlockSpec(memory_space=pltpu.VMEM),) * 3,
        scratch_shapes=[
            pltpu.VMEM((rows, 1), jnp.float32),
            pltpu.VMEM((rows, 1), jnp.float32),
            pltpu.VMEM((hidden // 2, width), jnp.bfloat16),
            pltpu.SemaphoreType.DMA((hidden // 2 // part_of(hidden // 2, HIDDEN_PART),)),
        ],
        compiler_params=pltpu.CompilerParams(vmem_limit_bytes=GRAD_VMEM),
        cost_estimate=pl.CostEstimate(
            flops=2 * rows * width * hidden, bytes_accessed=width * hidden, transcendentals=rows * hidden
        ),
    )(expert, low, high, pre_gate, pre_up, down, in_hbm(down_weight))


def output_kernel(grad_gate, grad_up, gate_copy, up_copy, *refs):
    dots, kept, sent = refs if len(refs) == 3 else (None,) + refs
    rows = kept.shape[0]
    columns = kept.shape[1] - (0 if dots is None else dots.shape[1])
    part = part_of(columns, COLUMN_PART)

    @pl.loop(0, columns // part)
    def _(step):
        span = pl.ds(pl.multiple_of(step * part, part), part)
        result = product(grad_gate[...], gate_copy[span, :], 1) + product(grad_up[...], up_copy[span, :], 1)
        kept[:, span] = result[:rows]
        sent[:, span] = result[rows:].astype(jnp.bfloat16)

    if dots is not None:
        kept[:, columns:] = dots[:rows, :].astype(jnp.float32)
        sent[:, columns:] = dots[rows:, :]


def multiply_outputs(grad_gate, grad_up, gate_copy, up_copy, *dots):
    rows, hidden = grad_gate.shape
    columns = gate_copy.shape[0]
    total = columns + sum(value.shape[1] for value in dots)
    return pl.pallas_call(
        output_kernel,
        out_shape=(
            pltpu.VMEM((rows // 2, total), jnp.float32),
            pltpu.VMEM((rows // 2, total), jnp.bfloat16),
        ),
        in_specs=[pl.BlockSpec(memory_space=pltpu.VMEM)] * (4 + len(dots)),
        out_specs=(pl.BlockSpec(memory_space=pltpu.VMEM),) * 2,
        compiler_params=pltpu.CompilerParams(vmem_limit_bytes=OUTPUT_VMEM),
        cost_estimate=pl.CostEstimate(
            flops=4 * rows * columns * hidden, bytes_accessed=4 * rows * columns, transcendentals=0
        ),
    )(grad_gate, grad_up, gate_copy, up_copy, *dots)


def gathered_plan(tokens, out_grad, kept_mask, routes, router, gate_weight, up_weight, down_weight):
    row_count, width = tokens.shape
    expert_count = lax.axis_size("expert")
    columns = lax.broadcasted_iota(jnp.int32, (row_count, expert_count), 1)
    first_hot = (routes[:, 0:1] == columns).astype(jnp.float32)
    second_hot = (routes[:, 1:2] == columns).astype(jnp.float32)
    keep_rows = kept_mask.astype(jnp.float32)
    half = width // 2
    table = 128
    token_z = gather_z(tokens)
    logits = jnp.dot(tokens, router, preferred_element_type=jnp.float32)
    first_logit = jnp.sum(logits * first_hot, axis=1)
    second_logit = jnp.sum(logits * second_hot, axis=1)
    gate_first = jax.nn.sigmoid(first_logit - second_logit)
    gate_second = jax.nn.sigmoid(second_logit - first_logit)
    gate_table = (first_hot * gate_first[:, None] + second_hot * gate_second[:, None]) * keep_rows[:, None]
    gate_table = jnp.pad(gate_table.astype(jnp.bfloat16), ((0, 0), (0, table - expert_count)))
    grad_z = gather_z(after_others(jnp.concatenate([gate_table, out_grad], axis=1), token_z[1]))
    token_near = gather_near(token_z, half)
    gate_low, up_low = fetch(0, half, token_near[0][0], gate_weight, up_weight)
    token_near = after_others(token_near, (gate_low, up_low))
    token_far = gather_far(*token_near)
    grad_near = gather_near(grad_z, half + table)
    (down,) = fetch(0, down_weight.shape[1] // 2, grad_near[1][1], down_weight)
    grad_far = gather_far(*after_others(grad_near, token_far))
    token_far = after_others(token_far, down)
    token_low, token_high = gather_core(token_near[0], token_far[0], token_near[1], token_far[1])
    pre_gate, pre_up, gate_high, up_high = multiply_tokens(token_low, gate_low, up_low, half, gate_weight, up_weight)
    grad_far = after_others(grad_far, pre_gate)
    pre_gate, pre_up = multiply_tokens(token_high, gate_high, up_high, 0, pre_gate, pre_up)
    grad_halves = gather_core(grad_near[0], grad_far[0], grad_near[1], grad_far[1])
    expert = lax.axis_index("expert").astype(jnp.int32).reshape(1)
    grad_gate, grad_up, dots = multiply_grads(expert, *grad_halves, pre_gate, pre_up, down, down_weight)
    kept, sent = multiply_outputs(grad_gate, grad_up, gate_low, up_low, dots)
    chunk = scatter_core(kept, sent)
    kept, sent = multiply_outputs(grad_gate, grad_up, gate_high, up_high)
    chunk = scatter_far(after_others(chunk, sent), half // 2)
    later = scatter_core(kept, sent)
    chunk = scatter_near(*after_others(chunk, later))
    later = scatter_far(later, half // 2)
    chunk = scatter_z(after_others(chunk, later))
    later = scatter_z(scatter_near(*later))
    expert_sum = jnp.concatenate([chunk[:, :half], later], axis=1)
    dot_table = chunk[:, half:half + expert_count]
    dot_first = jnp.sum(dot_table * first_hot, axis=1)
    dot_second = jnp.sum(dot_table * second_hot, axis=1)
    product = gate_first * gate_second * keep_rows
    grad_first = product * (dot_first - dot_second)
    grad_second = product * (dot_second - dot_first)
    logit_grad = first_hot * grad_first[:, None] + second_hot * grad_second[:, None]
    router_term = jnp.dot(logit_grad, router.astype(jnp.float32).T, precision=lax.Precision.HIGHEST)
    d_tokens = ((expert_sum + router_term) * keep_rows[:, None]).astype(jnp.bfloat16)
    gate_grad = jnp.stack([grad_first, grad_second], axis=1)
    return (d_tokens, gate_grad)


def solution(mesh):
    gathers = mesh.shape["seq"] == 2 and mesh.shape["expert"] == 4
    return jax.shard_map(
        gathered_plan if gathers else routed_plan,
        mesh=mesh,
        in_specs=(
            P(("seq", "expert", "mp"), None),
            P(("seq", "expert", "mp"), None),
            P(("seq", "expert", "mp")),
            P(("seq", "expert", "mp"), None),
            P(),
            P("expert", None, ("seq", "mp")),
            P("expert", None, ("seq", "mp")),
            P("expert", ("seq", "mp"), None),
        ),
        out_specs=(P(("seq", "expert", "mp"), None), P(("seq", "expert", "mp"), None)),
        check_vma=False,
    )
```

```python
import functools
import math

import jax
import jax.numpy as jnp
from jax import lax
from jax.experimental import pallas as pl
from jax.experimental.pallas import tpu as pltpu
from jax.sharding import PartitionSpec as P

TOKEN_PART = 512
HIDDEN_PART = 256
COLUMN_PART = 512
TOKEN_VMEM = 6 * 2 ** 20
GRAD_VMEM = 10 * 2 ** 20
OUTPUT_VMEM = 6 * 2 ** 20


def routed_plan(tokens, out_grad, kept_mask, routes, router, gate_weight, up_weight, down_weight):
    row_count = tokens.shape[0]
    width = tokens.shape[1]
    expert_count = lax.axis_size("expert")
    capacity = max(3 * row_count // 8, 2 * row_count // expert_count)
    logits = jnp.dot(tokens, router, preferred_element_type=jnp.float32)
    columns = lax.broadcasted_iota(jnp.int32, (row_count, expert_count), 1)
    first_hot = (routes[:, 0:1] == columns).astype(jnp.float32)
    second_hot = (routes[:, 1:2] == columns).astype(jnp.float32)
    first_logit = jnp.sum(logits * first_hot, axis=1)
    second_logit = jnp.sum(logits * second_hot, axis=1)
    gate_first = jax.nn.sigmoid(first_logit - second_logit)
    gate_second = jax.nn.sigmoid(second_logit - first_logit)
    keep_rows = kept_mask.astype(jnp.float32)
    chosen = ((first_hot + second_hot) * keep_rows[:, None]).astype(jnp.int32)
    position = jnp.cumsum(chosen, axis=0) - 1
    slot_iota = lax.broadcasted_iota(jnp.int32, (row_count, expert_count, capacity), 2)
    select_mask = (chosen[:, :, None] == 1) & (position[:, :, None] == slot_iota)
    select_bf = select_mask.astype(jnp.bfloat16)
    select_full = select_mask.astype(jnp.float32)
    token_send = jnp.einsum(
        "tec,td->ecd", select_bf, tokens, preferred_element_type=jnp.float32
    ).astype(jnp.bfloat16)
    grad_send = jnp.einsum(
        "tec,td->ecd", select_bf, out_grad, preferred_element_type=jnp.float32
    ).astype(jnp.bfloat16)
    gate_table = first_hot * gate_first[:, None] + second_hot * gate_second[:, None]
    gate_send = jnp.einsum(
        "tec,te->ec", select_full, gate_table, precision=lax.Precision.HIGHEST
    ).astype(jnp.bfloat16)
    token_recv, grad_recv, gate_recv = (
        lax.all_to_all(token_send, "expert", split_axis=0, concat_axis=0, tiled=True),
        lax.all_to_all(grad_send, "expert", split_axis=0, concat_axis=0, tiled=True),
        lax.all_to_all(gate_send, "expert", split_axis=0, concat_axis=0, tiled=True),
    )
    token_all, grad_all, gate_all = (
        lax.all_gather(token_recv, ("seq", "mp"), axis=0, tiled=True),
        lax.all_gather(grad_recv, ("seq", "mp"), axis=0, tiled=True),
        lax.all_gather(gate_recv, ("seq", "mp"), axis=0, tiled=True),
    )
    token_all = token_all.reshape(-1, width)
    grad_all = grad_all.reshape(-1, width)
    gate_all = gate_all.reshape(-1)
    gate_local = gate_weight[0]
    up_local = up_weight[0]
    down_local = down_weight[0]
    pre_gate = jnp.dot(token_all, gate_local, preferred_element_type=jnp.float32)
    pre_up = jnp.dot(token_all, up_local, preferred_element_type=jnp.float32)
    sigma = jax.nn.sigmoid(pre_gate)
    act = pre_gate * sigma
    hidden = act * pre_up
    grad_hidden = jnp.dot(grad_all, down_local.T, preferred_element_type=jnp.float32)
    gate_dot = jnp.sum(grad_hidden * hidden, axis=1)
    scaled = gate_all.astype(jnp.float32)[:, None] * grad_hidden
    grad_gate = (scaled * pre_up * sigma * (1.0 + pre_gate * (1.0 - sigma))).astype(jnp.bfloat16)
    grad_up = (scaled * act).astype(jnp.bfloat16)
    expert_grad = jnp.dot(grad_gate, gate_local.T, preferred_element_type=jnp.float32)
    expert_grad = expert_grad + jnp.dot(grad_up, up_local.T, preferred_element_type=jnp.float32)
    grad_own = lax.psum_scatter(
        expert_grad.astype(jnp.bfloat16), ("seq", "mp"), scatter_dimension=0, tiled=True
    ).astype(jnp.float32)
    dot_own = lax.psum_scatter(gate_dot, ("seq", "mp"), scatter_dimension=0, tiled=True)
    grad_back, dot_back = (
        lax.all_to_all(
            grad_own.reshape(expert_count, capacity, width).astype(jnp.bfloat16),
            "expert",
            split_axis=0,
            concat_axis=0,
            tiled=True,
        ).astype(jnp.float32),
        lax.all_to_all(
            dot_own.reshape(expert_count, capacity).astype(jnp.bfloat16),
            "expert",
            split_axis=0,
            concat_axis=0,
            tiled=True,
        ).astype(jnp.float32),
    )
    expert_sum = jnp.einsum("tec,ecd->td", select_full, grad_back, precision=lax.Precision.HIGHEST)
    dot_table = jnp.einsum("tec,ec->te", select_full, dot_back, precision=lax.Precision.HIGHEST)
    dot_first = jnp.sum(dot_table * first_hot, axis=1)
    dot_second = jnp.sum(dot_table * second_hot, axis=1)
    product = gate_first * gate_second * keep_rows
    grad_first = product * (dot_first - dot_second)
    grad_second = product * (dot_second - dot_first)
    logit_grad = first_hot * grad_first[:, None] + second_hot * grad_second[:, None]
    router_term = jnp.dot(logit_grad, router.astype(jnp.float32).T, precision=lax.Precision.HIGHEST)
    d_tokens = ((expert_sum + router_term) * keep_rows[:, None]).astype(jnp.bfloat16)
    gate_grad = jnp.stack([grad_first, grad_second], axis=1)
    return (d_tokens, gate_grad)

def shift(value, axis, step):
    size = lax.axis_size(axis)
    return lax.ppermute(value, axis, [((i + step) % size, i) for i in range(size)])


def swap(value, axis, bit):
    return lax.ppermute(value, axis, [(i ^ bit, i) for i in range(lax.axis_size(axis))])


def swap_x(value):
    return swap(value, "seq", 1)


def swap_y(value):
    return swap(value, "expert", 2)


def swap_core(value):
    return swap(value, "expert", 1)


def after_others(values, others):
    return lax.optimization_barrier((values, others))[0]


def gather_z(rows):
    return [rows] + [shift(rows, "mp", k) for k in range(1, lax.axis_size("mp"))]


def gather_near(z_rows, cut):
    rows = jnp.concatenate(z_rows, axis=0)
    low, high = rows[:, :cut], rows[:, cut:]
    return [low, swap_x(low)], [high, swap_y(high)]


def gather_far(low, high):
    return swap_y(jnp.concatenate(low, axis=0)), swap_x(jnp.concatenate(high, axis=0))


def gather_core(low, low_far, high, high_far):
    high_far = jnp.split(high_far, 2, axis=0)
    low = jnp.concatenate(low + [low_far], axis=0)
    high = jnp.concatenate([high[0], high_far[0], high[1], high_far[1]], axis=0)
    return tuple(jnp.concatenate([mine, swap_core(mine)], axis=0) for mine in (low, high))


def scatter_core(kept, sent):
    return kept + swap_core(sent).astype(jnp.float32)


def send(value, exchange):
    return exchange(value.astype(jnp.bfloat16)).astype(jnp.float32)


def scatter_far(total, cut):
    low, low_x, low_y, low_both = jnp.split(total[:, :cut], 4, axis=0)
    high, high_x, high_y, high_both = jnp.split(total[:, cut:], 4, axis=0)
    low_far = send(jnp.concatenate([low_y, low_both], axis=0), swap_y)
    high_far = send(jnp.concatenate([high_x, high_both], axis=0), swap_x)
    return jnp.concatenate([low, low_x], axis=0) + low_far, jnp.concatenate([high, high_y], axis=0) + high_far


def scatter_near(low, high):
    low, low_x = jnp.split(low, 2, axis=0)
    high, high_y = jnp.split(high, 2, axis=0)
    return jnp.concatenate([low + send(low_x, swap_x), high + send(high_y, swap_y)], axis=1)


def scatter_z(total):
    size = lax.axis_size("mp")
    rows = total.shape[0] // size
    result = total[:rows]
    for k in range(1, size):
        result = result + send(total[k * rows:(k + 1) * rows], lambda value: shift(value, "mp", size - k))
    return result


def product(a, b, b_dim):
    return lax.dot_general(a, b, (((1,), (b_dim,)), ((), ())), preferred_element_type=jnp.float32)


def part_of(length, wanted):
    return math.gcd(length, wanted)


def in_hbm(value):
    return pltpu.with_memory_space_constraint(value, pltpu.HBM)


def fetch_kernel(first, _, *refs):
    count = (len(refs) - 1) // 2
    sems = refs[-1]
    copies = []
    for index in range(count):
        target = refs[count + index]
        source = refs[index].at[0, pl.ds(first, target.shape[0])]
        copies.append(pltpu.make_async_copy(source, target, sems.at[index]))
    for copy in copies:
        copy.start()
    for copy in copies:
        copy.wait()


def fetch(first, length, earlier, *weights):
    shapes = [(length, value.shape[2]) for value in weights]
    return pl.pallas_call(
        functools.partial(fetch_kernel, first),
        out_shape=tuple(pltpu.VMEM(shape, jnp.bfloat16) for shape in shapes),
        in_specs=[pl.BlockSpec(memory_space=pl.ANY)] * (1 + len(weights)),
        out_specs=(pl.BlockSpec(memory_space=pltpu.VMEM),) * len(weights),
        scratch_shapes=[pltpu.SemaphoreType.DMA((len(weights),))],
        compiler_params=pltpu.CompilerParams(vmem_limit_bytes=TOKEN_VMEM),
        cost_estimate=pl.CostEstimate(
            flops=0, bytes_accessed=sum(2 * rows * hidden for rows, hidden in shapes), transcendentals=0
        ),
    )(earlier, *[in_hbm(value) for value in weights])


def token_kernel(first, tokens, gate, up, *refs):
    pre_gate, pre_up = refs[2:4]
    depth = part_of(tokens.shape[1], TOKEN_PART)
    copies = []
    if first:
        for index in range(2):
            source = refs[index].at[0, pl.ds(first, gate.shape[0])]
            copies.append(pltpu.make_async_copy(source, refs[4 + index], refs[6].at[index]))
    for copy in copies:
        copy.start()
    pre_gate[...] = jnp.zeros_like(pre_gate) if first else refs[0][...]
    pre_up[...] = jnp.zeros_like(pre_up) if first else refs[1][...]

    @pl.loop(0, tokens.shape[1] // depth)
    def _(step):
        rows = pl.ds(pl.multiple_of(step * depth, depth), depth)
        pre_gate[...] += product(tokens[:, rows], gate[rows, :], 0)
        pre_up[...] += product(tokens[:, rows], up[rows, :], 0)

    for copy in copies:
        copy.wait()


def multiply_tokens(tokens, gate, up, first, *others):
    rows, width = tokens.shape
    hidden = gate.shape[1]
    sums = (pltpu.VMEM((rows, hidden), jnp.float32),) * 2
    fetched = (pltpu.VMEM(gate.shape, jnp.bfloat16),) * 2 if first else ()
    if first:
        others = [in_hbm(value) for value in others]
    return pl.pallas_call(
        functools.partial(token_kernel, first),
        out_shape=sums + fetched,
        in_specs=[pl.BlockSpec(memory_space=pltpu.VMEM)] * 3
        + [pl.BlockSpec(memory_space=pl.ANY if first else pltpu.VMEM)] * 2,
        out_specs=(pl.BlockSpec(memory_space=pltpu.VMEM),) * len(sums + fetched),
        scratch_shapes=[pltpu.SemaphoreType.DMA((2,))] if first else [],
        compiler_params=pltpu.CompilerParams(vmem_limit_bytes=TOKEN_VMEM),
        cost_estimate=pl.CostEstimate(
            flops=4 * rows * width * hidden, bytes_accessed=2 * rows * width, transcendentals=0
        ),
    )(tokens, gate, up, *others)


def grad_kernel(
    expert, low, high, pre_gate, pre_up, down, down_weight, grad_gate, grad_up, dots, gate_rows, dot_sums, rest, sems
):
    table = low.shape[1] - high.shape[1]
    half = high.shape[1]
    ready = down.shape[0]
    depth = part_of(ready, HIDDEN_PART)
    steps = ready // depth

    def copy_of(index):
        rows = pl.ds(pl.multiple_of(index * depth, depth), depth)
        source = pl.ds(pl.multiple_of(ready + index * depth, depth), depth)
        return pltpu.make_async_copy(down_weight.at[0, source], rest.at[rows], sems.at[index])

    for index in range(steps):
        copy_of(index).start()

    lanes = lax.broadcasted_iota(jnp.int32, (low.shape[0], table), 1)
    gate_rows[...] = jnp.sum(
        jnp.where(lanes == expert[0], low[:, :table].astype(jnp.float32), 0.0), axis=1, keepdims=True
    )
    dot_sums[...] = jnp.zeros_like(dot_sums)

    def block(weights, first, step):
        rows = pl.ds(pl.multiple_of(step * depth, depth), depth)
        span = pl.ds(pl.multiple_of(first + step * depth, depth), depth)
        grad_hidden = product(low[:, table:], weights[rows, :half], 1) + product(high[...], weights[rows, half:], 1)
        gates = pre_gate[:, span]
        ups = pre_up[:, span]
        sigma = jax.nn.sigmoid(gates)
        act = gates * sigma
        dot_sums[...] += jnp.sum(grad_hidden * (act * ups), axis=1, keepdims=True)
        scaled = gate_rows[...] * grad_hidden
        grad_gate[:, span] = (scaled * ups * sigma * (1.0 + gates * (1.0 - sigma))).astype(jnp.bfloat16)
        grad_up[:, span] = (scaled * act).astype(jnp.bfloat16)

    @pl.loop(0, steps)
    def _(step):
        block(down, 0, step)

    @pl.loop(0, steps)
    def _(step):
        copy_of(step).wait()
        block(rest, ready, step)

    dots[...] = jnp.where(lanes == expert[0], dot_sums[...], 0.0).astype(jnp.bfloat16)


def multiply_grads(expert, low, high, pre_gate, pre_up, down, down_weight):
    rows, hidden = pre_gate.shape
    width = down_weight.shape[2]
    table = low.shape[1] - high.shape[1]
    return pl.pallas_call(
        grad_kernel,
        out_shape=(
            pltpu.VMEM((rows, hidden), jnp.bfloat16),
            pltpu.VMEM((rows, hidden), jnp.bfloat16),
            pltpu.VMEM((rows, table), jnp.bfloat16),
        ),
        in_specs=[pl.BlockSpec(memory_space=pltpu.SMEM)]
        + [pl.BlockSpec(memory_space=pltpu.VMEM)] * 5
        + [pl.BlockSpec(memory_space=pl.ANY)],
        out_specs=(pl.BlockSpec(memory_space=pltpu.VMEM),) * 3,
        scratch_shapes=[
            pltpu.VMEM((rows, 1), jnp.float32),
            pltpu.VMEM((rows, 1), jnp.float32),
            pltpu.VMEM((hidden // 2, width), jnp.bfloat16),
            pltpu.SemaphoreType.DMA((hidden // 2 // part_of(hidden // 2, HIDDEN_PART),)),
        ],
        compiler_params=pltpu.CompilerParams(vmem_limit_bytes=GRAD_VMEM),
        cost_estimate=pl.CostEstimate(
            flops=2 * rows * width * hidden, bytes_accessed=width * hidden, transcendentals=rows * hidden
        ),
    )(expert, low, high, pre_gate, pre_up, down, in_hbm(down_weight))


def output_kernel(grad_gate, grad_up, gate_copy, up_copy, *refs):
    dots, kept, sent = refs if len(refs) == 3 else (None,) + refs
    rows = kept.shape[0]
    columns = kept.shape[1] - (0 if dots is None else dots.shape[1])
    part = part_of(columns, COLUMN_PART)

    @pl.loop(0, columns // part)
    def _(step):
        span = pl.ds(pl.multiple_of(step * part, part), part)
        result = product(grad_gate[...], gate_copy[span, :], 1) + product(grad_up[...], up_copy[span, :], 1)
        kept[:, span] = result[:rows]
        sent[:, span] = result[rows:].astype(jnp.bfloat16)

    if dots is not None:
        kept[:, columns:] = dots[:rows, :].astype(jnp.float32)
        sent[:, columns:] = dots[rows:, :]


def multiply_outputs(grad_gate, grad_up, gate_copy, up_copy, *dots):
    rows, hidden = grad_gate.shape
    columns = gate_copy.shape[0]
    total = columns + sum(value.shape[1] for value in dots)
    return pl.pallas_call(
        output_kernel,
        out_shape=(
            pltpu.VMEM((rows // 2, total), jnp.float32),
            pltpu.VMEM((rows // 2, total), jnp.bfloat16),
        ),
        in_specs=[pl.BlockSpec(memory_space=pltpu.VMEM)] * (4 + len(dots)),
        out_specs=(pl.BlockSpec(memory_space=pltpu.VMEM),) * 2,
        compiler_params=pltpu.CompilerParams(vmem_limit_bytes=OUTPUT_VMEM),
        cost_estimate=pl.CostEstimate(
            flops=4 * rows * columns * hidden, bytes_accessed=4 * rows * columns, transcendentals=0
        ),
    )(grad_gate, grad_up, gate_copy, up_copy, *dots)


def gathered_plan(tokens, out_grad, kept_mask, routes, router, gate_weight, up_weight, down_weight):
    row_count, width = tokens.shape
    expert_count = lax.axis_size("expert")
    columns = lax.broadcasted_iota(jnp.int32, (row_count, expert_count), 1)
    first_hot = (routes[:, 0:1] == columns).astype(jnp.float32)
    second_hot = (routes[:, 1:2] == columns).astype(jnp.float32)
    keep_rows = kept_mask.astype(jnp.float32)
    half = width // 2
    table = 128
    token_z = gather_z(tokens)
    logits = jnp.dot(tokens, router, preferred_element_type=jnp.float32)
    first_logit = jnp.sum(logits * first_hot, axis=1)
    second_logit = jnp.sum(logits * second_hot, axis=1)
    gate_first = jax.nn.sigmoid(first_logit - second_logit)
    gate_second = jax.nn.sigmoid(second_logit - first_logit)
    gate_table = (first_hot * gate_first[:, None] + second_hot * gate_second[:, None]) * keep_rows[:, None]
    gate_table = jnp.pad(gate_table.astype(jnp.bfloat16), ((0, 0), (0, table - expert_count)))
    grad_z = gather_z(after_others(jnp.concatenate([gate_table, out_grad], axis=1), token_z[1]))
    token_near = gather_near(token_z, half)
    gate_low, up_low = fetch(0, half, token_near[0][0], gate_weight, up_weight)
    token_near = after_others(token_near, (gate_low, up_low))
    token_far = gather_far(*token_near)
    grad_near = gather_near(grad_z, half + table)
    (down,) = fetch(0, down_weight.shape[1] // 2, token_near[1][1], down_weight)
    grad_far = gather_far(*after_others(grad_near, token_far))
    token_far = after_others(token_far, down)
    token_low, token_high = gather_core(token_near[0], token_far[0], token_near[1], token_far[1])
    pre_gate, pre_up, gate_high, up_high = multiply_tokens(token_low, gate_low, up_low, half, gate_weight, up_weight)
    pre_gate, pre_up = multiply_tokens(token_high, gate_high, up_high, 0, pre_gate, pre_up)
    grad_far = after_others(grad_far, pre_gate)
    grad_halves = gather_core(grad_near[0], grad_far[0], grad_near[1], grad_far[1])
    expert = lax.axis_index("expert").astype(jnp.int32).reshape(1)
    grad_gate, grad_up, dots = multiply_grads(expert, *grad_halves, pre_gate, pre_up, down, down_weight)
    kept, sent = multiply_outputs(grad_gate, grad_up, gate_low, up_low, dots)
    chunk = scatter_core(kept, sent)
    kept, sent = multiply_outputs(grad_gate, grad_up, gate_high, up_high)
    chunk = scatter_far(after_others(chunk, sent), half // 2)
    later = scatter_core(kept, sent)
    chunk = scatter_near(*after_others(chunk, later))
    later = scatter_far(later, half // 2)
    chunk = scatter_z(after_others(chunk, later))
    later = scatter_z(scatter_near(*later))
    expert_sum = jnp.concatenate([chunk[:, :half], later], axis=1)
    dot_table = chunk[:, half:half + expert_count]
    dot_first = jnp.sum(dot_table * first_hot, axis=1)
    dot_second = jnp.sum(dot_table * second_hot, axis=1)
    product = gate_first * gate_second * keep_rows
    grad_first = product * (dot_first - dot_second)
    grad_second = product * (dot_second - dot_first)
    logit_grad = first_hot * grad_first[:, None] + second_hot * grad_second[:, None]
    router_term = jnp.dot(logit_grad, router.astype(jnp.float32).T, precision=lax.Precision.HIGHEST)
    d_tokens = ((expert_sum + router_term) * keep_rows[:, None]).astype(jnp.bfloat16)
    gate_grad = jnp.stack([grad_first, grad_second], axis=1)
    return (d_tokens, gate_grad)


def solution(mesh):
    gathers = mesh.shape["seq"] == 2 and mesh.shape["expert"] == 4
    return jax.shard_map(
        gathered_plan if gathers else routed_plan,
        mesh=mesh,
        in_specs=(
            P(("seq", "expert", "mp"), None),
            P(("seq", "expert", "mp"), None),
            P(("seq", "expert", "mp")),
            P(("seq", "expert", "mp"), None),
            P(),
            P("expert", None, ("seq", "mp")),
            P("expert", None, ("seq", "mp")),
            P("expert", ("seq", "mp"), None),
        ),
        out_specs=(P(("seq", "expert", "mp"), None), P(("seq", "expert", "mp"), None)),
        check_vma=False,
    )
```

```python
import functools
import math

import jax
import jax.numpy as jnp
from jax import lax
from jax.experimental import pallas as pl
from jax.experimental.pallas import tpu as pltpu
from jax.sharding import PartitionSpec as P

TOKEN_PART = 512
HIDDEN_PART = 512
COLUMN_PART = 1024
TOKEN_VMEM = 6 * 2 ** 20
GRAD_VMEM = 10 * 2 ** 20
OUTPUT_VMEM = 6 * 2 ** 20


def routed_plan(tokens, out_grad, kept_mask, routes, router, gate_weight, up_weight, down_weight):
    row_count = tokens.shape[0]
    width = tokens.shape[1]
    expert_count = lax.axis_size("expert")
    capacity = max(3 * row_count // 8, 2 * row_count // expert_count)
    logits = jnp.dot(tokens, router, preferred_element_type=jnp.float32)
    columns = lax.broadcasted_iota(jnp.int32, (row_count, expert_count), 1)
    first_hot = (routes[:, 0:1] == columns).astype(jnp.float32)
    second_hot = (routes[:, 1:2] == columns).astype(jnp.float32)
    first_logit = jnp.sum(logits * first_hot, axis=1)
    second_logit = jnp.sum(logits * second_hot, axis=1)
    gate_first = jax.nn.sigmoid(first_logit - second_logit)
    gate_second = jax.nn.sigmoid(second_logit - first_logit)
    keep_rows = kept_mask.astype(jnp.float32)
    chosen = ((first_hot + second_hot) * keep_rows[:, None]).astype(jnp.int32)
    position = jnp.cumsum(chosen, axis=0) - 1
    slot_iota = lax.broadcasted_iota(jnp.int32, (row_count, expert_count, capacity), 2)
    select_mask = (chosen[:, :, None] == 1) & (position[:, :, None] == slot_iota)
    select_bf = select_mask.astype(jnp.bfloat16)
    select_full = select_mask.astype(jnp.float32)
    token_send = jnp.einsum(
        "tec,td->ecd", select_bf, tokens, preferred_element_type=jnp.float32
    ).astype(jnp.bfloat16)
    grad_send = jnp.einsum(
        "tec,td->ecd", select_bf, out_grad, preferred_element_type=jnp.float32
    ).astype(jnp.bfloat16)
    gate_table = first_hot * gate_first[:, None] + second_hot * gate_second[:, None]
    gate_send = jnp.einsum(
        "tec,te->ec", select_full, gate_table, precision=lax.Precision.HIGHEST
    ).astype(jnp.bfloat16)
    token_recv, grad_recv, gate_recv = (
        lax.all_to_all(token_send, "expert", split_axis=0, concat_axis=0, tiled=True),
        lax.all_to_all(grad_send, "expert", split_axis=0, concat_axis=0, tiled=True),
        lax.all_to_all(gate_send, "expert", split_axis=0, concat_axis=0, tiled=True),
    )
    token_all, grad_all, gate_all = (
        lax.all_gather(token_recv, ("seq", "mp"), axis=0, tiled=True),
        lax.all_gather(grad_recv, ("seq", "mp"), axis=0, tiled=True),
        lax.all_gather(gate_recv, ("seq", "mp"), axis=0, tiled=True),
    )
    token_all = token_all.reshape(-1, width)
    grad_all = grad_all.reshape(-1, width)
    gate_all = gate_all.reshape(-1)
    gate_local = gate_weight[0]
    up_local = up_weight[0]
    down_local = down_weight[0]
    pre_gate = jnp.dot(token_all, gate_local, preferred_element_type=jnp.float32)
    pre_up = jnp.dot(token_all, up_local, preferred_element_type=jnp.float32)
    sigma = jax.nn.sigmoid(pre_gate)
    act = pre_gate * sigma
    hidden = act * pre_up
    grad_hidden = jnp.dot(grad_all, down_local.T, preferred_element_type=jnp.float32)
    gate_dot = jnp.sum(grad_hidden * hidden, axis=1)
    scaled = gate_all.astype(jnp.float32)[:, None] * grad_hidden
    grad_gate = (scaled * pre_up * sigma * (1.0 + pre_gate * (1.0 - sigma))).astype(jnp.bfloat16)
    grad_up = (scaled * act).astype(jnp.bfloat16)
    expert_grad = jnp.dot(grad_gate, gate_local.T, preferred_element_type=jnp.float32)
    expert_grad = expert_grad + jnp.dot(grad_up, up_local.T, preferred_element_type=jnp.float32)
    grad_own = lax.psum_scatter(
        expert_grad.astype(jnp.bfloat16), ("seq", "mp"), scatter_dimension=0, tiled=True
    ).astype(jnp.float32)
    dot_own = lax.psum_scatter(gate_dot, ("seq", "mp"), scatter_dimension=0, tiled=True)
    grad_back, dot_back = (
        lax.all_to_all(
            grad_own.reshape(expert_count, capacity, width).astype(jnp.bfloat16),
            "expert",
            split_axis=0,
            concat_axis=0,
            tiled=True,
        ).astype(jnp.float32),
        lax.all_to_all(
            dot_own.reshape(expert_count, capacity).astype(jnp.bfloat16),
            "expert",
            split_axis=0,
            concat_axis=0,
            tiled=True,
        ).astype(jnp.float32),
    )
    expert_sum = jnp.einsum("tec,ecd->td", select_full, grad_back, precision=lax.Precision.HIGHEST)
    dot_table = jnp.einsum("tec,ec->te", select_full, dot_back, precision=lax.Precision.HIGHEST)
    dot_first = jnp.sum(dot_table * first_hot, axis=1)
    dot_second = jnp.sum(dot_table * second_hot, axis=1)
    product = gate_first * gate_second * keep_rows
    grad_first = product * (dot_first - dot_second)
    grad_second = product * (dot_second - dot_first)
    logit_grad = first_hot * grad_first[:, None] + second_hot * grad_second[:, None]
    router_term = jnp.dot(logit_grad, router.astype(jnp.float32).T, precision=lax.Precision.HIGHEST)
    d_tokens = ((expert_sum + router_term) * keep_rows[:, None]).astype(jnp.bfloat16)
    gate_grad = jnp.stack([grad_first, grad_second], axis=1)
    return (d_tokens, gate_grad)

def shift(value, axis, step):
    size = lax.axis_size(axis)
    return lax.ppermute(value, axis, [((i + step) % size, i) for i in range(size)])


def swap(value, axis, bit):
    return lax.ppermute(value, axis, [(i ^ bit, i) for i in range(lax.axis_size(axis))])


def swap_x(value):
    return swap(value, "seq", 1)


def swap_y(value):
    return swap(value, "expert", 2)


def swap_core(value):
    return swap(value, "expert", 1)


def after_others(values, others):
    return lax.optimization_barrier((values, others))[0]


def gather_z(rows):
    return [rows] + [shift(rows, "mp", k) for k in range(1, lax.axis_size("mp"))]


def gather_near(z_rows, cut):
    rows = jnp.concatenate(z_rows, axis=0)
    low, high = rows[:, :cut], rows[:, cut:]
    return [low, swap_x(low)], [high, swap_y(high)]


def gather_far(low, high):
    return swap_y(jnp.concatenate(low, axis=0)), swap_x(jnp.concatenate(high, axis=0))


def gather_core(low, low_far, high, high_far):
    high_far = jnp.split(high_far, 2, axis=0)
    low = jnp.concatenate(low + [low_far], axis=0)
    high = jnp.concatenate([high[0], high_far[0], high[1], high_far[1]], axis=0)
    return tuple(jnp.concatenate([mine, swap_core(mine)], axis=0) for mine in (low, high))


def scatter_core(kept, sent):
    return kept + swap_core(sent).astype(jnp.float32)


def send(value, exchange):
    return exchange(value.astype(jnp.bfloat16)).astype(jnp.float32)


def scatter_far(total, cut):
    low, low_x, low_y, low_both = jnp.split(total[:, :cut], 4, axis=0)
    high, high_x, high_y, high_both = jnp.split(total[:, cut:], 4, axis=0)
    low_far = send(jnp.concatenate([low_y, low_both], axis=0), swap_y)
    high_far = send(jnp.concatenate([high_x, high_both], axis=0), swap_x)
    return jnp.concatenate([low, low_x], axis=0) + low_far, jnp.concatenate([high, high_y], axis=0) + high_far


def scatter_near(low, high):
    low, low_x = jnp.split(low, 2, axis=0)
    high, high_y = jnp.split(high, 2, axis=0)
    return jnp.concatenate([low + send(low_x, swap_x), high + send(high_y, swap_y)], axis=1)


def scatter_z(total):
    size = lax.axis_size("mp")
    rows = total.shape[0] // size
    result = total[:rows]
    for k in range(1, size):
        result = result + send(total[k * rows:(k + 1) * rows], lambda value: shift(value, "mp", size - k))
    return result


def product(a, b, b_dim):
    return lax.dot_general(a, b, (((1,), (b_dim,)), ((), ())), preferred_element_type=jnp.float32)


def part_of(length, wanted):
    return math.gcd(length, wanted)


def in_hbm(value):
    return pltpu.with_memory_space_constraint(value, pltpu.HBM)


def fetch_kernel(first, _, *refs):
    count = (len(refs) - 1) // 2
    sems = refs[-1]
    copies = []
    for index in range(count):
        target = refs[count + index]
        source = refs[index].at[0, pl.ds(first, target.shape[0])]
        copies.append(pltpu.make_async_copy(source, target, sems.at[index]))
    for copy in copies:
        copy.start()
    for copy in copies:
        copy.wait()


def fetch(first, length, earlier, *weights):
    shapes = [(length, value.shape[2]) for value in weights]
    return pl.pallas_call(
        functools.partial(fetch_kernel, first),
        out_shape=tuple(pltpu.VMEM(shape, jnp.bfloat16) for shape in shapes),
        in_specs=[pl.BlockSpec(memory_space=pl.ANY)] * (1 + len(weights)),
        out_specs=(pl.BlockSpec(memory_space=pltpu.VMEM),) * len(weights),
        scratch_shapes=[pltpu.SemaphoreType.DMA((len(weights),))],
        compiler_params=pltpu.CompilerParams(vmem_limit_bytes=TOKEN_VMEM),
        cost_estimate=pl.CostEstimate(
            flops=0, bytes_accessed=sum(2 * rows * hidden for rows, hidden in shapes), transcendentals=0
        ),
    )(earlier, *[in_hbm(value) for value in weights])


def token_kernel(first, offset, length, tokens, gate, up, *refs):
    pre_gate, pre_up = refs[2:4]
    depth = part_of(length, TOKEN_PART)
    copies = []
    if first:
        for index in range(2):
            source = refs[index].at[0, pl.ds(first, gate.shape[0])]
            copies.append(pltpu.make_async_copy(source, refs[4 + index], refs[6].at[index]))
    for copy in copies:
        copy.start()
    pre_gate[...] = jnp.zeros_like(pre_gate) if first else refs[0][...]
    pre_up[...] = jnp.zeros_like(pre_up) if first else refs[1][...]

    @pl.loop(0, length // depth)
    def _(step):
        rows = pl.ds(pl.multiple_of(offset + step * depth, depth), depth)
        pre_gate[...] += product(tokens[:, rows], gate[rows, :], 0)
        pre_up[...] += product(tokens[:, rows], up[rows, :], 0)

    for copy in copies:
        copy.wait()


def multiply_tokens(tokens, gate, up, offset, length, first, *others):
    rows, hidden = tokens.shape[0], gate.shape[1]
    sums = (pltpu.VMEM((rows, hidden), jnp.float32),) * 2
    fetched = (pltpu.VMEM(gate.shape, jnp.bfloat16),) * 2 if first else ()
    if first:
        others = [in_hbm(value) for value in others]
    return pl.pallas_call(
        functools.partial(token_kernel, first, offset, length),
        out_shape=sums + fetched,
        in_specs=[pl.BlockSpec(memory_space=pltpu.VMEM)] * 3
        + [pl.BlockSpec(memory_space=pl.ANY if first else pltpu.VMEM)] * 2,
        out_specs=(pl.BlockSpec(memory_space=pltpu.VMEM),) * len(sums + fetched),
        scratch_shapes=[pltpu.SemaphoreType.DMA((2,))] if first else [],
        compiler_params=pltpu.CompilerParams(vmem_limit_bytes=TOKEN_VMEM),
        cost_estimate=pl.CostEstimate(
            flops=4 * rows * length * hidden, bytes_accessed=2 * rows * length, transcendentals=0
        ),
    )(tokens, gate, up, *others)


def grad_kernel(
    expert, low, high, pre_gate, pre_up, down, down_weight, grad_gate, grad_up, dots, gate_rows, dot_sums, rest, sems
):
    table = low.shape[1] - high.shape[1]
    half = high.shape[1]
    ready = down.shape[0]
    depth = part_of(ready, HIDDEN_PART)
    steps = ready // depth

    def copy_of(index):
        rows = pl.ds(pl.multiple_of(index * depth, depth), depth)
        source = pl.ds(pl.multiple_of(ready + index * depth, depth), depth)
        return pltpu.make_async_copy(down_weight.at[0, source], rest.at[rows], sems.at[index])

    for index in range(steps):
        copy_of(index).start()

    lanes = lax.broadcasted_iota(jnp.int32, (low.shape[0], table), 1)
    gate_rows[...] = jnp.sum(
        jnp.where(lanes == expert[0], low[:, :table].astype(jnp.float32), 0.0), axis=1, keepdims=True
    )
    dot_sums[...] = jnp.zeros_like(dot_sums)

    def block(weights, first, step):
        rows = pl.ds(pl.multiple_of(step * depth, depth), depth)
        span = pl.ds(pl.multiple_of(first + step * depth, depth), depth)
        grad_hidden = (product(weights[rows, :half], low[:, table:], 1) + product(weights[rows, half:], high[...], 1)).T
        gates = pre_gate[:, span]
        ups = pre_up[:, span]
        sigma = jax.nn.sigmoid(gates)
        act = gates * sigma
        dot_sums[...] += jnp.sum(grad_hidden * (act * ups), axis=1, keepdims=True)
        scaled = gate_rows[...] * grad_hidden
        grad_gate[:, span] = (scaled * ups * sigma * (1.0 + gates * (1.0 - sigma))).astype(jnp.bfloat16)
        grad_up[:, span] = (scaled * act).astype(jnp.bfloat16)

    @pl.loop(0, steps)
    def _(step):
        block(down, 0, step)

    @pl.loop(0, steps)
    def _(step):
        copy_of(step).wait()
        block(rest, ready, step)

    dots[...] = jnp.where(lanes == expert[0], dot_sums[...], 0.0).astype(jnp.bfloat16)


def multiply_grads(expert, low, high, pre_gate, pre_up, down, down_weight):
    rows, hidden = pre_gate.shape
    width = down_weight.shape[2]
    table = low.shape[1] - high.shape[1]
    return pl.pallas_call(
        grad_kernel,
        out_shape=(
            pltpu.VMEM((rows, hidden), jnp.bfloat16),
            pltpu.VMEM((rows, hidden), jnp.bfloat16),
            pltpu.VMEM((rows, table), jnp.bfloat16),
        ),
        in_specs=[pl.BlockSpec(memory_space=pltpu.SMEM)]
        + [pl.BlockSpec(memory_space=pltpu.VMEM)] * 5
        + [pl.BlockSpec(memory_space=pl.ANY)],
        out_specs=(pl.BlockSpec(memory_space=pltpu.VMEM),) * 3,
        scratch_shapes=[
            pltpu.VMEM((rows, 1), jnp.float32),
            pltpu.VMEM((rows, 1), jnp.float32),
            pltpu.VMEM((hidden // 2, width), jnp.bfloat16),
            pltpu.SemaphoreType.DMA((hidden // 2 // part_of(hidden // 2, HIDDEN_PART),)),
        ],
        compiler_params=pltpu.CompilerParams(vmem_limit_bytes=GRAD_VMEM),
        cost_estimate=pl.CostEstimate(
            flops=2 * rows * width * hidden, bytes_accessed=width * hidden, transcendentals=rows * hidden
        ),
    )(expert, low, high, pre_gate, pre_up, down, in_hbm(down_weight))


def output_kernel(grad_gate, grad_up, gate_copy, up_copy, *refs):
    dots, kept, sent = refs if len(refs) == 3 else (None,) + refs
    rows = kept.shape[0]
    columns = kept.shape[1] - (0 if dots is None else dots.shape[1])
    part = part_of(columns, COLUMN_PART)

    @pl.loop(0, columns // part)
    def _(step):
        span = pl.ds(pl.multiple_of(step * part, part), part)
        result = (product(gate_copy[span, :], grad_gate[...], 1) + product(up_copy[span, :], grad_up[...], 1)).T
        kept[:, span] = result[:rows]
        sent[:, span] = result[rows:].astype(jnp.bfloat16)

    if dots is not None:
        kept[:, columns:] = dots[:rows, :].astype(jnp.float32)
        sent[:, columns:] = dots[rows:, :]


def multiply_outputs(grad_gate, grad_up, gate_copy, up_copy, *dots):
    rows, hidden = grad_gate.shape
    columns = gate_copy.shape[0]
    total = columns + sum(value.shape[1] for value in dots)
    return pl.pallas_call(
        output_kernel,
        out_shape=(
            pltpu.VMEM((rows // 2, total), jnp.float32),
            pltpu.VMEM((rows // 2, total), jnp.bfloat16),
        ),
        in_specs=[pl.BlockSpec(memory_space=pltpu.VMEM)] * (4 + len(dots)),
        out_specs=(pl.BlockSpec(memory_space=pltpu.VMEM),) * 2,
        compiler_params=pltpu.CompilerParams(vmem_limit_bytes=OUTPUT_VMEM),
        cost_estimate=pl.CostEstimate(
            flops=4 * rows * columns * hidden, bytes_accessed=4 * rows * columns, transcendentals=0
        ),
    )(grad_gate, grad_up, gate_copy, up_copy, *dots)


def gathered_plan(tokens, out_grad, kept_mask, routes, router, gate_weight, up_weight, down_weight):
    row_count, width = tokens.shape
    expert_count = lax.axis_size("expert")
    columns = lax.broadcasted_iota(jnp.int32, (row_count, expert_count), 1)
    first_hot = (routes[:, 0:1] == columns).astype(jnp.float32)
    second_hot = (routes[:, 1:2] == columns).astype(jnp.float32)
    keep_rows = kept_mask.astype(jnp.float32)
    half, quarter = width // 2, width // 4
    table = 128
    token_z = gather_z(tokens)
    logits = jnp.dot(tokens, router, preferred_element_type=jnp.float32)
    first_logit = jnp.sum(logits * first_hot, axis=1)
    second_logit = jnp.sum(logits * second_hot, axis=1)
    gate_first = jax.nn.sigmoid(first_logit - second_logit)
    gate_second = jax.nn.sigmoid(second_logit - first_logit)
    gate_table = (first_hot * gate_first[:, None] + second_hot * gate_second[:, None]) * keep_rows[:, None]
    gate_table = jnp.pad(gate_table.astype(jnp.bfloat16), ((0, 0), (0, table - expert_count)))
    grad_z = gather_z(after_others(jnp.concatenate([gate_table, out_grad], axis=1), token_z[1]))
    token_near = gather_near(token_z, half)
    gate_low, up_low = fetch(0, half, token_near[0][0], gate_weight, up_weight)
    token_near = after_others(token_near, (gate_low, up_low))
    token_far = gather_far(*token_near)
    grad_near = gather_near(grad_z, half + table)
    (down,) = fetch(0, down_weight.shape[1] // 2, token_near[1][1], down_weight)
    grad_far = gather_far(*after_others(grad_near, token_far))
    token_far = after_others(token_far, down)
    token_low, token_high = gather_core(token_near[0], token_far[0], token_near[1], token_far[1])
    pre_gate, pre_up, gate_high, up_high = multiply_tokens(
        token_low, gate_low, up_low, 0, half, half, gate_weight, up_weight
    )
    pre_gate, pre_up = multiply_tokens(token_high, gate_high, up_high, 0, quarter, 0, pre_gate, pre_up)
    grad_far = after_others(grad_far, pre_gate)
    pre_gate, pre_up = multiply_tokens(token_high, gate_high, up_high, quarter, quarter, 0, pre_gate, pre_up)
    grad_halves = gather_core(grad_near[0], grad_far[0], grad_near[1], grad_far[1])
    expert = lax.axis_index("expert").astype(jnp.int32).reshape(1)
    grad_gate, grad_up, dots = multiply_grads(expert, *grad_halves, pre_gate, pre_up, down, down_weight)
    kept, sent = multiply_outputs(grad_gate, grad_up, gate_low, up_low, dots)
    chunk = scatter_core(kept, sent)
    kept, sent = multiply_outputs(grad_gate, grad_up, gate_high, up_high)
    chunk = scatter_far(after_others(chunk, sent), half // 2)
    later = scatter_core(kept, sent)
    chunk = scatter_near(*after_others(chunk, later))
    later = scatter_far(later, half // 2)
    chunk = scatter_z(after_others(chunk, later))
    later = scatter_z(scatter_near(*later))
    expert_sum = jnp.concatenate([chunk[:, :half], later], axis=1)
    dot_table = chunk[:, half:half + expert_count]
    dot_first = jnp.sum(dot_table * first_hot, axis=1)
    dot_second = jnp.sum(dot_table * second_hot, axis=1)
    product = gate_first * gate_second * keep_rows
    grad_first = product * (dot_first - dot_second)
    grad_second = product * (dot_second - dot_first)
    logit_grad = first_hot * grad_first[:, None] + second_hot * grad_second[:, None]
    router_term = jnp.dot(logit_grad, router.astype(jnp.float32).T, precision=lax.Precision.HIGHEST)
    d_tokens = ((expert_sum + router_term) * keep_rows[:, None]).astype(jnp.bfloat16)
    gate_grad = jnp.stack([grad_first, grad_second], axis=1)
    return (d_tokens, gate_grad)


def solution(mesh):
    gathers = mesh.shape["seq"] == 2 and mesh.shape["expert"] == 4
    return jax.shard_map(
        gathered_plan if gathers else routed_plan,
        mesh=mesh,
        in_specs=(
            P(("seq", "expert", "mp"), None),
            P(("seq", "expert", "mp"), None),
            P(("seq", "expert", "mp")),
            P(("seq", "expert", "mp"), None),
            P(),
            P("expert", None, ("seq", "mp")),
            P("expert", None, ("seq", "mp")),
            P("expert", ("seq", "mp"), None),
        ),
        out_specs=(P(("seq", "expert", "mp"), None), P(("seq", "expert", "mp"), None)),
        check_vma=False,
    )
```

```python
import functools
import math

import jax
import jax.numpy as jnp
from jax import lax
from jax.experimental import pallas as pl
from jax.experimental.pallas import tpu as pltpu
from jax.sharding import PartitionSpec as P

TOKEN_PART = 512
HIDDEN_PART = 256
COLUMN_PART = 1536
TOKEN_VMEM = 6 * 2 ** 20
GRAD_VMEM = 10 * 2 ** 20
OUTPUT_VMEM = 6 * 2 ** 20


def routed_plan(tokens, out_grad, kept_mask, routes, router, gate_weight, up_weight, down_weight):
    row_count = tokens.shape[0]
    width = tokens.shape[1]
    expert_count = lax.axis_size("expert")
    capacity = max(3 * row_count // 8, 2 * row_count // expert_count)
    logits = jnp.dot(tokens, router, preferred_element_type=jnp.float32)
    columns = lax.broadcasted_iota(jnp.int32, (row_count, expert_count), 1)
    first_hot = (routes[:, 0:1] == columns).astype(jnp.float32)
    second_hot = (routes[:, 1:2] == columns).astype(jnp.float32)
    first_logit = jnp.sum(logits * first_hot, axis=1)
    second_logit = jnp.sum(logits * second_hot, axis=1)
    gate_first = jax.nn.sigmoid(first_logit - second_logit)
    gate_second = jax.nn.sigmoid(second_logit - first_logit)
    keep_rows = kept_mask.astype(jnp.float32)
    chosen = ((first_hot + second_hot) * keep_rows[:, None]).astype(jnp.int32)
    position = jnp.cumsum(chosen, axis=0) - 1
    slot_iota = lax.broadcasted_iota(jnp.int32, (row_count, expert_count, capacity), 2)
    select_mask = (chosen[:, :, None] == 1) & (position[:, :, None] == slot_iota)
    select_bf = select_mask.astype(jnp.bfloat16)
    select_full = select_mask.astype(jnp.float32)
    token_send = jnp.einsum(
        "tec,td->ecd", select_bf, tokens, preferred_element_type=jnp.float32
    ).astype(jnp.bfloat16)
    grad_send = jnp.einsum(
        "tec,td->ecd", select_bf, out_grad, preferred_element_type=jnp.float32
    ).astype(jnp.bfloat16)
    gate_table = first_hot * gate_first[:, None] + second_hot * gate_second[:, None]
    gate_send = jnp.einsum(
        "tec,te->ec", select_full, gate_table, precision=lax.Precision.HIGHEST
    ).astype(jnp.bfloat16)
    token_recv, grad_recv, gate_recv = (
        lax.all_to_all(token_send, "expert", split_axis=0, concat_axis=0, tiled=True),
        lax.all_to_all(grad_send, "expert", split_axis=0, concat_axis=0, tiled=True),
        lax.all_to_all(gate_send, "expert", split_axis=0, concat_axis=0, tiled=True),
    )
    token_all, grad_all, gate_all = (
        lax.all_gather(token_recv, ("seq", "mp"), axis=0, tiled=True),
        lax.all_gather(grad_recv, ("seq", "mp"), axis=0, tiled=True),
        lax.all_gather(gate_recv, ("seq", "mp"), axis=0, tiled=True),
    )
    token_all = token_all.reshape(-1, width)
    grad_all = grad_all.reshape(-1, width)
    gate_all = gate_all.reshape(-1)
    gate_local = gate_weight[0]
    up_local = up_weight[0]
    down_local = down_weight[0]
    pre_gate = jnp.dot(token_all, gate_local, preferred_element_type=jnp.float32)
    pre_up = jnp.dot(token_all, up_local, preferred_element_type=jnp.float32)
    sigma = jax.nn.sigmoid(pre_gate)
    act = pre_gate * sigma
    hidden = act * pre_up
    grad_hidden = jnp.dot(grad_all, down_local.T, preferred_element_type=jnp.float32)
    gate_dot = jnp.sum(grad_hidden * hidden, axis=1)
    scaled = gate_all.astype(jnp.float32)[:, None] * grad_hidden
    grad_gate = (scaled * pre_up * sigma * (1.0 + pre_gate * (1.0 - sigma))).astype(jnp.bfloat16)
    grad_up = (scaled * act).astype(jnp.bfloat16)
    expert_grad = jnp.dot(grad_gate, gate_local.T, preferred_element_type=jnp.float32)
    expert_grad = expert_grad + jnp.dot(grad_up, up_local.T, preferred_element_type=jnp.float32)
    grad_own = lax.psum_scatter(
        expert_grad.astype(jnp.bfloat16), ("seq", "mp"), scatter_dimension=0, tiled=True
    ).astype(jnp.float32)
    dot_own = lax.psum_scatter(gate_dot, ("seq", "mp"), scatter_dimension=0, tiled=True)
    grad_back, dot_back = (
        lax.all_to_all(
            grad_own.reshape(expert_count, capacity, width).astype(jnp.bfloat16),
            "expert",
            split_axis=0,
            concat_axis=0,
            tiled=True,
        ).astype(jnp.float32),
        lax.all_to_all(
            dot_own.reshape(expert_count, capacity).astype(jnp.bfloat16),
            "expert",
            split_axis=0,
            concat_axis=0,
            tiled=True,
        ).astype(jnp.float32),
    )
    expert_sum = jnp.einsum("tec,ecd->td", select_full, grad_back, precision=lax.Precision.HIGHEST)
    dot_table = jnp.einsum("tec,ec->te", select_full, dot_back, precision=lax.Precision.HIGHEST)
    dot_first = jnp.sum(dot_table * first_hot, axis=1)
    dot_second = jnp.sum(dot_table * second_hot, axis=1)
    product = gate_first * gate_second * keep_rows
    grad_first = product * (dot_first - dot_second)
    grad_second = product * (dot_second - dot_first)
    logit_grad = first_hot * grad_first[:, None] + second_hot * grad_second[:, None]
    router_term = jnp.dot(logit_grad, router.astype(jnp.float32).T, precision=lax.Precision.HIGHEST)
    d_tokens = ((expert_sum + router_term) * keep_rows[:, None]).astype(jnp.bfloat16)
    gate_grad = jnp.stack([grad_first, grad_second], axis=1)
    return (d_tokens, gate_grad)

def swap(value, axis, bit):
    return lax.ppermute(value, axis, [(i ^ bit, i) for i in range(lax.axis_size(axis))])


def swap_x(value):
    return swap(value, "seq", 1)


def swap_y(value):
    return swap(value, "expert", 2)


def swap_core(value):
    return swap(value, "expert", 1)


def after_others(values, others):
    return lax.optimization_barrier((values, others))[0]


def gather_z(rows):
    return [rows] + [swap(rows, "mp", k) for k in range(1, lax.axis_size("mp"))]


def gather_near(z_rows, cut):
    rows = jnp.concatenate(z_rows, axis=0)
    low, high = rows[:, :cut], rows[:, cut:]
    return [low, swap_x(low)], [high, swap_y(high)]


def gather_far(low, high):
    return swap_y(jnp.concatenate(low, axis=0)), swap_x(jnp.concatenate(high, axis=0))


def gather_core(low, low_far, high, high_far):
    high_far = jnp.split(high_far, 2, axis=0)
    low = jnp.concatenate(low + [low_far], axis=0)
    high = jnp.concatenate([high[0], high_far[0], high[1], high_far[1]], axis=0)
    return tuple(jnp.concatenate([mine, swap_core(mine)], axis=0) for mine in (low, high))


def scatter_core(kept, sent):
    return kept + swap_core(sent).astype(jnp.float32)


def send(value, exchange):
    return exchange(value.astype(jnp.bfloat16)).astype(jnp.float32)


def scatter_far(total, cut):
    low, low_x, low_y, low_both = jnp.split(total[:, :cut], 4, axis=0)
    high, high_x, high_y, high_both = jnp.split(total[:, cut:], 4, axis=0)
    low_far = send(jnp.concatenate([low_y, low_both], axis=0), swap_y)
    high_far = send(jnp.concatenate([high_x, high_both], axis=0), swap_x)
    return jnp.concatenate([low, low_x], axis=0) + low_far, jnp.concatenate([high, high_y], axis=0) + high_far


def scatter_near(low, high):
    low, low_x = jnp.split(low, 2, axis=0)
    high, high_y = jnp.split(high, 2, axis=0)
    return jnp.concatenate([low + send(low_x, swap_x), high + send(high_y, swap_y)], axis=1)


def scatter_z(total):
    size = lax.axis_size("mp")
    rows = total.shape[0] // size
    result = total[:rows]
    for k in range(1, size):
        result = result + send(total[k * rows:(k + 1) * rows], lambda value: swap(value, "mp", k))
    return result


def product(a, b, b_dim):
    return lax.dot_general(a, b, (((1,), (b_dim,)), ((), ())), preferred_element_type=jnp.float32)


def part_of(length, wanted):
    return math.gcd(length, wanted)


def in_hbm(value):
    return pltpu.with_memory_space_constraint(value, pltpu.HBM)


def fetch_kernel(first, _, *refs):
    count = (len(refs) - 1) // 2
    sems = refs[-1]
    copies = []
    for index in range(count):
        target = refs[count + index]
        source = refs[index].at[0, pl.ds(first, target.shape[0])]
        copies.append(pltpu.make_async_copy(source, target, sems.at[index]))
    for copy in copies:
        copy.start()
    for copy in copies:
        copy.wait()


def fetch(first, length, earlier, *weights):
    shapes = [(length, value.shape[2]) for value in weights]
    return pl.pallas_call(
        functools.partial(fetch_kernel, first),
        out_shape=tuple(pltpu.VMEM(shape, jnp.bfloat16) for shape in shapes),
        in_specs=[pl.BlockSpec(memory_space=pl.ANY)] * (1 + len(weights)),
        out_specs=(pl.BlockSpec(memory_space=pltpu.VMEM),) * len(weights),
        scratch_shapes=[pltpu.SemaphoreType.DMA((len(weights),))],
        compiler_params=pltpu.CompilerParams(vmem_limit_bytes=TOKEN_VMEM),
        cost_estimate=pl.CostEstimate(
            flops=0, bytes_accessed=sum(2 * rows * hidden for rows, hidden in shapes), transcendentals=0
        ),
    )(earlier, *[in_hbm(value) for value in weights])


def token_kernel(first, offset, length, tokens, gate, up, *refs):
    pre_gate, pre_up = refs[2:4]
    depth = part_of(length, TOKEN_PART)
    copies = []
    if first:
        for index in range(2):
            source = refs[index].at[0, pl.ds(first, gate.shape[0])]
            copies.append(pltpu.make_async_copy(source, refs[4 + index], refs[6].at[index]))
    for copy in copies:
        copy.start()
    pre_gate[...] = jnp.zeros_like(pre_gate) if first else refs[0][...]
    pre_up[...] = jnp.zeros_like(pre_up) if first else refs[1][...]

    @pl.loop(0, length // depth)
    def _(step):
        rows = pl.ds(pl.multiple_of(offset + step * depth, depth), depth)
        pre_gate[...] += product(tokens[:, rows], gate[rows, :], 0)
        pre_up[...] += product(tokens[:, rows], up[rows, :], 0)

    for copy in copies:
        copy.wait()


def multiply_tokens(tokens, gate, up, offset, length, first, *others):
    rows, hidden = tokens.shape[0], gate.shape[1]
    sums = (pltpu.VMEM((rows, hidden), jnp.float32),) * 2
    fetched = (pltpu.VMEM(gate.shape, jnp.bfloat16),) * 2 if first else ()
    if first:
        others = [in_hbm(value) for value in others]
    return pl.pallas_call(
        functools.partial(token_kernel, first, offset, length),
        out_shape=sums + fetched,
        in_specs=[pl.BlockSpec(memory_space=pltpu.VMEM)] * 3
        + [pl.BlockSpec(memory_space=pl.ANY if first else pltpu.VMEM)] * 2,
        out_specs=(pl.BlockSpec(memory_space=pltpu.VMEM),) * len(sums + fetched),
        scratch_shapes=[pltpu.SemaphoreType.DMA((2,))] if first else [],
        compiler_params=pltpu.CompilerParams(vmem_limit_bytes=TOKEN_VMEM),
        cost_estimate=pl.CostEstimate(
            flops=4 * rows * length * hidden, bytes_accessed=2 * rows * length, transcendentals=0
        ),
    )(tokens, gate, up, *others)


def grad_kernel(
    expert, low, high, pre_gate, pre_up, down, down_weight, grad_gate, grad_up, dots, gate_rows, dot_sums, rest, sems
):
    table = low.shape[1] - high.shape[1]
    half = high.shape[1]
    ready = down.shape[0]
    depth = part_of(ready, HIDDEN_PART)
    steps = ready // depth

    def copy_of(index):
        rows = pl.ds(pl.multiple_of(index * depth, depth), depth)
        source = pl.ds(pl.multiple_of(ready + index * depth, depth), depth)
        return pltpu.make_async_copy(down_weight.at[0, source], rest.at[rows], sems.at[index])

    for index in range(steps):
        copy_of(index).start()

    lanes = lax.broadcasted_iota(jnp.int32, (low.shape[0], table), 1)
    gate_rows[...] = jnp.sum(
        jnp.where(lanes == expert[0], low[:, :table].astype(jnp.float32), 0.0), axis=1, keepdims=True
    )
    dot_sums[...] = jnp.zeros_like(dot_sums)

    def block(weights, first, step):
        rows = pl.ds(pl.multiple_of(step * depth, depth), depth)
        span = pl.ds(pl.multiple_of(first + step * depth, depth), depth)
        grad_hidden = product(low[:, table:], weights[rows, :half], 1) + product(high[...], weights[rows, half:], 1)
        gates = pre_gate[:, span]
        ups = pre_up[:, span]
        sigma = jax.nn.sigmoid(gates)
        act = gates * sigma
        dot_sums[...] += jnp.sum(grad_hidden * (act * ups), axis=1, keepdims=True)
        scaled = gate_rows[...] * grad_hidden
        grad_gate[:, span] = (scaled * ups * sigma * (1.0 + gates * (1.0 - sigma))).astype(jnp.bfloat16)
        grad_up[:, span] = (scaled * act).astype(jnp.bfloat16)

    @pl.loop(0, steps)
    def _(step):
        block(down, 0, step)

    @pl.loop(0, steps)
    def _(step):
        copy_of(step).wait()
        block(rest, ready, step)

    dots[...] = jnp.where(lanes == expert[0], dot_sums[...], 0.0).astype(jnp.bfloat16)


def multiply_grads(expert, low, high, pre_gate, pre_up, down, down_weight):
    rows, hidden = pre_gate.shape
    width = down_weight.shape[2]
    table = low.shape[1] - high.shape[1]
    return pl.pallas_call(
        grad_kernel,
        out_shape=(
            pltpu.VMEM((rows, hidden), jnp.bfloat16),
            pltpu.VMEM((rows, hidden), jnp.bfloat16),
            pltpu.VMEM((rows, table), jnp.bfloat16),
        ),
        in_specs=[pl.BlockSpec(memory_space=pltpu.SMEM)]
        + [pl.BlockSpec(memory_space=pltpu.VMEM)] * 5
        + [pl.BlockSpec(memory_space=pl.ANY)],
        out_specs=(pl.BlockSpec(memory_space=pltpu.VMEM),) * 3,
        scratch_shapes=[
            pltpu.VMEM((rows, 1), jnp.float32),
            pltpu.VMEM((rows, 1), jnp.float32),
            pltpu.VMEM((hidden // 2, width), jnp.bfloat16),
            pltpu.SemaphoreType.DMA((hidden // 2 // part_of(hidden // 2, HIDDEN_PART),)),
        ],
        compiler_params=pltpu.CompilerParams(vmem_limit_bytes=GRAD_VMEM),
        cost_estimate=pl.CostEstimate(
            flops=2 * rows * width * hidden, bytes_accessed=width * hidden, transcendentals=rows * hidden
        ),
    )(expert, low, high, pre_gate, pre_up, down, in_hbm(down_weight))


def output_kernel(grad_gate, grad_up, gate_copy, up_copy, *refs):
    dots, kept, sent = refs if len(refs) == 3 else (None,) + refs
    rows = kept.shape[0]
    columns = kept.shape[1] - (0 if dots is None else dots.shape[1])
    part = part_of(columns, COLUMN_PART)

    @pl.loop(0, columns // part)
    def _(step):
        span = pl.ds(pl.multiple_of(step * part, part), part)
        result = (product(gate_copy[span, :], grad_gate[...], 1) + product(up_copy[span, :], grad_up[...], 1)).T
        kept[:, span] = result[:rows]
        sent[:, span] = result[rows:].astype(jnp.bfloat16)

    if dots is not None:
        kept[:, columns:] = dots[:rows, :].astype(jnp.float32)
        sent[:, columns:] = dots[rows:, :]


def multiply_outputs(grad_gate, grad_up, gate_copy, up_copy, *dots):
    rows, hidden = grad_gate.shape
    columns = gate_copy.shape[0]
    total = columns + sum(value.shape[1] for value in dots)
    return pl.pallas_call(
        output_kernel,
        out_shape=(
            pltpu.VMEM((rows // 2, total), jnp.float32),
            pltpu.VMEM((rows // 2, total), jnp.bfloat16),
        ),
        in_specs=[pl.BlockSpec(memory_space=pltpu.VMEM)] * (4 + len(dots)),
        out_specs=(pl.BlockSpec(memory_space=pltpu.VMEM),) * 2,
        compiler_params=pltpu.CompilerParams(vmem_limit_bytes=OUTPUT_VMEM),
        cost_estimate=pl.CostEstimate(
            flops=4 * rows * columns * hidden, bytes_accessed=4 * rows * columns, transcendentals=0
        ),
    )(grad_gate, grad_up, gate_copy, up_copy, *dots)


def gathered_plan(tokens, out_grad, kept_mask, routes, router, gate_weight, up_weight, down_weight):
    row_count, width = tokens.shape
    expert_count = lax.axis_size("expert")
    columns = lax.broadcasted_iota(jnp.int32, (row_count, expert_count), 1)
    first_hot = (routes[:, 0:1] == columns).astype(jnp.float32)
    second_hot = (routes[:, 1:2] == columns).astype(jnp.float32)
    keep_rows = kept_mask.astype(jnp.float32)
    half, quarter = width // 2, width // 4
    table = 128
    token_z = gather_z(tokens)
    logits = jnp.dot(tokens, router, preferred_element_type=jnp.float32)
    first_logit = jnp.sum(logits * first_hot, axis=1)
    second_logit = jnp.sum(logits * second_hot, axis=1)
    gate_first = jax.nn.sigmoid(first_logit - second_logit)
    gate_second = jax.nn.sigmoid(second_logit - first_logit)
    gate_table = (first_hot * gate_first[:, None] + second_hot * gate_second[:, None]) * keep_rows[:, None]
    gate_table = jnp.pad(gate_table.astype(jnp.bfloat16), ((0, 0), (0, table - expert_count)))
    grad_z = gather_z(after_others(jnp.concatenate([gate_table, out_grad], axis=1), token_z[1]))
    token_near = gather_near(token_z, half)
    gate_low, up_low = fetch(0, half, token_near[0][0], gate_weight, up_weight)
    token_near = after_others(token_near, (gate_low, up_low))
    token_far = gather_far(*token_near)
    grad_near = gather_near(grad_z, half + table)
    (down,) = fetch(0, down_weight.shape[1] // 2, token_near[1][1], down_weight)
    grad_far = gather_far(*after_others(grad_near, token_far))
    token_far = after_others(token_far, down)
    token_low, token_high = gather_core(token_near[0], token_far[0], token_near[1], token_far[1])
    pre_gate, pre_up, gate_high, up_high = multiply_tokens(
        token_low, gate_low, up_low, 0, half, half, gate_weight, up_weight
    )
    pre_gate, pre_up = multiply_tokens(token_high, gate_high, up_high, 0, quarter, 0, pre_gate, pre_up)
    grad_far = after_others(grad_far, pre_gate)
    pre_gate, pre_up = multiply_tokens(token_high, gate_high, up_high, quarter, quarter, 0, pre_gate, pre_up)
    grad_halves = gather_core(grad_near[0], grad_far[0], grad_near[1], grad_far[1])
    expert = lax.axis_index("expert").astype(jnp.int32).reshape(1)
    grad_gate, grad_up, dots = multiply_grads(expert, *grad_halves, pre_gate, pre_up, down, down_weight)
    kept, sent = multiply_outputs(grad_gate, grad_up, gate_low, up_low, dots)
    chunk = scatter_core(kept, sent)
    kept, sent = multiply_outputs(grad_gate, grad_up, gate_high, up_high)
    chunk = scatter_far(after_others(chunk, sent), half // 2)
    later = scatter_core(kept, sent)
    chunk = scatter_near(*after_others(chunk, later))
    later = scatter_far(later, half // 2)
    chunk = scatter_z(after_others(chunk, later))
    later = scatter_z(scatter_near(*later))
    expert_sum = jnp.concatenate([chunk[:, :half], later], axis=1)
    dot_table = chunk[:, half:half + expert_count]
    dot_first = jnp.sum(dot_table * first_hot, axis=1)
    dot_second = jnp.sum(dot_table * second_hot, axis=1)
    product = gate_first * gate_second * keep_rows
    grad_first = product * (dot_first - dot_second)
    grad_second = product * (dot_second - dot_first)
    logit_grad = first_hot * grad_first[:, None] + second_hot * grad_second[:, None]
    router_term = jnp.dot(logit_grad, router.astype(jnp.float32).T, precision=lax.Precision.HIGHEST)
    d_tokens = ((expert_sum + router_term) * keep_rows[:, None]).astype(jnp.bfloat16)
    gate_grad = jnp.stack([grad_first, grad_second], axis=1)
    return (d_tokens, gate_grad)


def solution(mesh):
    gathers = mesh.shape["seq"] == 2 and mesh.shape["expert"] == 4 and mesh.shape["mp"] in (2, 4)
    return jax.shard_map(
        gathered_plan if gathers else routed_plan,
        mesh=mesh,
        in_specs=(
            P(("seq", "expert", "mp"), None),
            P(("seq", "expert", "mp"), None),
            P(("seq", "expert", "mp")),
            P(("seq", "expert", "mp"), None),
            P(),
            P("expert", None, ("seq", "mp")),
            P("expert", None, ("seq", "mp")),
            P("expert", ("seq", "mp"), None),
        ),
        out_specs=(P(("seq", "expert", "mp"), None), P(("seq", "expert", "mp"), None)),
        check_vma=False,
    )
```

```python
import functools
import math

import jax
import jax.numpy as jnp
from jax import lax
from jax.experimental import pallas as pl
from jax.experimental.pallas import tpu as pltpu
from jax.sharding import PartitionSpec as P

TOKEN_PART = 512
HIDDEN_PART = 256
COLUMN_PART = 1536
TOKEN_VMEM = 6 * 2 ** 20
GRAD_VMEM = 10 * 2 ** 20
OUTPUT_VMEM = 6 * 2 ** 20


def routed_plan(tokens, out_grad, kept_mask, routes, router, gate_weight, up_weight, down_weight):
    row_count = tokens.shape[0]
    width = tokens.shape[1]
    expert_count = lax.axis_size("expert")
    capacity = max(3 * row_count // 8, 2 * row_count // expert_count)
    logits = jnp.dot(tokens, router, preferred_element_type=jnp.float32)
    columns = lax.broadcasted_iota(jnp.int32, (row_count, expert_count), 1)
    first_hot = (routes[:, 0:1] == columns).astype(jnp.float32)
    second_hot = (routes[:, 1:2] == columns).astype(jnp.float32)
    first_logit = jnp.sum(logits * first_hot, axis=1)
    second_logit = jnp.sum(logits * second_hot, axis=1)
    gate_first = jax.nn.sigmoid(first_logit - second_logit)
    gate_second = jax.nn.sigmoid(second_logit - first_logit)
    keep_rows = kept_mask.astype(jnp.float32)
    chosen = ((first_hot + second_hot) * keep_rows[:, None]).astype(jnp.int32)
    position = jnp.cumsum(chosen, axis=0) - 1
    slot_iota = lax.broadcasted_iota(jnp.int32, (row_count, expert_count, capacity), 2)
    select_mask = (chosen[:, :, None] == 1) & (position[:, :, None] == slot_iota)
    select_bf = select_mask.astype(jnp.bfloat16)
    select_full = select_mask.astype(jnp.float32)
    token_send = jnp.einsum(
        "tec,td->ecd", select_bf, tokens, preferred_element_type=jnp.float32
    ).astype(jnp.bfloat16)
    grad_send = jnp.einsum(
        "tec,td->ecd", select_bf, out_grad, preferred_element_type=jnp.float32
    ).astype(jnp.bfloat16)
    gate_table = first_hot * gate_first[:, None] + second_hot * gate_second[:, None]
    gate_send = jnp.einsum(
        "tec,te->ec", select_full, gate_table, precision=lax.Precision.HIGHEST
    ).astype(jnp.bfloat16)
    token_recv, grad_recv, gate_recv = (
        lax.all_to_all(token_send, "expert", split_axis=0, concat_axis=0, tiled=True),
        lax.all_to_all(grad_send, "expert", split_axis=0, concat_axis=0, tiled=True),
        lax.all_to_all(gate_send, "expert", split_axis=0, concat_axis=0, tiled=True),
    )
    token_all, grad_all, gate_all = (
        lax.all_gather(token_recv, ("seq", "mp"), axis=0, tiled=True),
        lax.all_gather(grad_recv, ("seq", "mp"), axis=0, tiled=True),
        lax.all_gather(gate_recv, ("seq", "mp"), axis=0, tiled=True),
    )
    token_all = token_all.reshape(-1, width)
    grad_all = grad_all.reshape(-1, width)
    gate_all = gate_all.reshape(-1)
    gate_local = gate_weight[0]
    up_local = up_weight[0]
    down_local = down_weight[0]
    pre_gate = jnp.dot(token_all, gate_local, preferred_element_type=jnp.float32)
    pre_up = jnp.dot(token_all, up_local, preferred_element_type=jnp.float32)
    sigma = jax.nn.sigmoid(pre_gate)
    act = pre_gate * sigma
    hidden = act * pre_up
    grad_hidden = jnp.dot(grad_all, down_local.T, preferred_element_type=jnp.float32)
    gate_dot = jnp.sum(grad_hidden * hidden, axis=1)
    scaled = gate_all.astype(jnp.float32)[:, None] * grad_hidden
    grad_gate = (scaled * pre_up * sigma * (1.0 + pre_gate * (1.0 - sigma))).astype(jnp.bfloat16)
    grad_up = (scaled * act).astype(jnp.bfloat16)
    expert_grad = jnp.dot(grad_gate, gate_local.T, preferred_element_type=jnp.float32)
    expert_grad = expert_grad + jnp.dot(grad_up, up_local.T, preferred_element_type=jnp.float32)
    grad_own = lax.psum_scatter(
        expert_grad.astype(jnp.bfloat16), ("seq", "mp"), scatter_dimension=0, tiled=True
    ).astype(jnp.float32)
    dot_own = lax.psum_scatter(gate_dot, ("seq", "mp"), scatter_dimension=0, tiled=True)
    grad_back, dot_back = (
        lax.all_to_all(
            grad_own.reshape(expert_count, capacity, width).astype(jnp.bfloat16),
            "expert",
            split_axis=0,
            concat_axis=0,
            tiled=True,
        ).astype(jnp.float32),
        lax.all_to_all(
            dot_own.reshape(expert_count, capacity).astype(jnp.bfloat16),
            "expert",
            split_axis=0,
            concat_axis=0,
            tiled=True,
        ).astype(jnp.float32),
    )
    expert_sum = jnp.einsum("tec,ecd->td", select_full, grad_back, precision=lax.Precision.HIGHEST)
    dot_table = jnp.einsum("tec,ec->te", select_full, dot_back, precision=lax.Precision.HIGHEST)
    dot_first = jnp.sum(dot_table * first_hot, axis=1)
    dot_second = jnp.sum(dot_table * second_hot, axis=1)
    product = gate_first * gate_second * keep_rows
    grad_first = product * (dot_first - dot_second)
    grad_second = product * (dot_second - dot_first)
    logit_grad = first_hot * grad_first[:, None] + second_hot * grad_second[:, None]
    router_term = jnp.dot(logit_grad, router.astype(jnp.float32).T, precision=lax.Precision.HIGHEST)
    d_tokens = ((expert_sum + router_term) * keep_rows[:, None]).astype(jnp.bfloat16)
    gate_grad = jnp.stack([grad_first, grad_second], axis=1)
    return (d_tokens, gate_grad)

def swap(value, axis, bit):
    return lax.ppermute(value, axis, [(i ^ bit, i) for i in range(lax.axis_size(axis))])


def swap_x(value):
    return swap(value, "seq", 1)


def swap_y(value):
    return swap(value, "expert", 2)


def swap_core(value):
    return swap(value, "expert", 1)


def after_others(values, others):
    return lax.optimization_barrier((values, others))[0]


def gather_z(rows):
    return [rows] + [swap(rows, "mp", k) for k in range(1, lax.axis_size("mp"))]


def gather_near(z_rows, cut):
    rows = jnp.concatenate(z_rows, axis=0)
    low, high = rows[:, :cut], rows[:, cut:]
    return [low, swap_x(low)], [high, swap_y(high)]


def gather_far(low, high):
    return swap_y(jnp.concatenate(low, axis=0)), swap_x(jnp.concatenate(high, axis=0))


def gather_core(low, low_far, high, high_far):
    high_far = jnp.split(high_far, 2, axis=0)
    low = jnp.concatenate(low + [low_far], axis=0)
    high = jnp.concatenate([high[0], high_far[0], high[1], high_far[1]], axis=0)
    return tuple(jnp.concatenate([mine, swap_core(mine)], axis=0) for mine in (low, high))


def scatter_core(kept, sent):
    return kept + swap_core(sent).astype(jnp.float32)


def send(value, exchange):
    return exchange(value.astype(jnp.bfloat16)).astype(jnp.float32)


def scatter_far(total, cut):
    low, low_x, low_y, low_both = jnp.split(total[:, :cut], 4, axis=0)
    high, high_x, high_y, high_both = jnp.split(total[:, cut:], 4, axis=0)
    low_far = send(jnp.concatenate([low_y, low_both], axis=0), swap_y)
    high_far = send(jnp.concatenate([high_x, high_both], axis=0), swap_x)
    return jnp.concatenate([low, low_x], axis=0) + low_far, jnp.concatenate([high, high_y], axis=0) + high_far


def scatter_near(low, high):
    low, low_x = jnp.split(low, 2, axis=0)
    high, high_y = jnp.split(high, 2, axis=0)
    return jnp.concatenate([low + send(low_x, swap_x), high + send(high_y, swap_y)], axis=1)


def scatter_z(total):
    size = lax.axis_size("mp")
    rows = total.shape[0] // size
    result = total[:rows]
    for k in range(1, size):
        result = result + send(total[k * rows:(k + 1) * rows], lambda value: swap(value, "mp", k))
    return result


def product(a, b, b_dim):
    return lax.dot_general(a, b, (((1,), (b_dim,)), ((), ())), preferred_element_type=jnp.float32)


def part_of(length, wanted):
    return math.gcd(length, wanted)


def in_hbm(value):
    return pltpu.with_memory_space_constraint(value, pltpu.HBM)


def fetch_kernel(first, _, *refs):
    count = (len(refs) - 1) // 2
    sems = refs[-1]
    copies = []
    for index in range(count):
        target = refs[count + index]
        source = refs[index].at[0, pl.ds(first, target.shape[0])]
        copies.append(pltpu.make_async_copy(source, target, sems.at[index]))
    for copy in copies:
        copy.start()
    for copy in copies:
        copy.wait()


def fetch(first, length, earlier, *weights):
    shapes = [(length, value.shape[2]) for value in weights]
    return pl.pallas_call(
        functools.partial(fetch_kernel, first),
        out_shape=tuple(pltpu.VMEM(shape, jnp.bfloat16) for shape in shapes),
        in_specs=[pl.BlockSpec(memory_space=pl.ANY)] * (1 + len(weights)),
        out_specs=(pl.BlockSpec(memory_space=pltpu.VMEM),) * len(weights),
        scratch_shapes=[pltpu.SemaphoreType.DMA((len(weights),))],
        compiler_params=pltpu.CompilerParams(vmem_limit_bytes=TOKEN_VMEM),
        cost_estimate=pl.CostEstimate(
            flops=0, bytes_accessed=sum(2 * rows * hidden for rows, hidden in shapes), transcendentals=0
        ),
    )(earlier, *[in_hbm(value) for value in weights])


def token_kernel(offset, length, sources, summed, tokens, gate, up, *refs):
    before, refs = refs[:summed], refs[summed:]
    count = len(sources)
    weights, (pre_gate, pre_up), fetched = refs[:count], refs[count:count + 2], refs[count + 2:2 * count + 2]
    depth = part_of(length, TOKEN_PART)
    copies = []
    for index in range(count):
        source = weights[index].at[0, pl.ds(sources[index], fetched[index].shape[0])]
        copies.append(pltpu.make_async_copy(source, fetched[index], refs[-1].at[index]))
    for copy in copies:
        copy.start()
    pre_gate[...] = before[0][...] if summed else jnp.zeros_like(pre_gate)
    pre_up[...] = before[1][...] if summed else jnp.zeros_like(pre_up)

    @pl.loop(0, length // depth)
    def _(step):
        rows = pl.ds(pl.multiple_of(offset + step * depth, depth), depth)
        pre_gate[...] += product(tokens[:, rows], gate[rows, :], 0)
        pre_up[...] += product(tokens[:, rows], up[rows, :], 0)

    for copy in copies:
        copy.wait()


def multiply_tokens(tokens, gate, up, offset, length, sums=(), wanted=()):
    rows, hidden = tokens.shape[0], gate.shape[1]
    shapes = [(count, value.shape[2]) for value, _, count in wanted]
    sources = tuple(first for _, first, _ in wanted)
    out_shape = (pltpu.VMEM((rows, hidden), jnp.float32),) * 2
    out_shape += tuple(pltpu.VMEM(shape, jnp.bfloat16) for shape in shapes)
    return pl.pallas_call(
        functools.partial(token_kernel, offset, length, sources, len(sums)),
        out_shape=out_shape,
        in_specs=[pl.BlockSpec(memory_space=pltpu.VMEM)] * (3 + len(sums))
        + [pl.BlockSpec(memory_space=pl.ANY)] * len(wanted),
        out_specs=(pl.BlockSpec(memory_space=pltpu.VMEM),) * len(out_shape),
        scratch_shapes=[pltpu.SemaphoreType.DMA((len(wanted),))] if wanted else [],
        compiler_params=pltpu.CompilerParams(vmem_limit_bytes=TOKEN_VMEM),
        cost_estimate=pl.CostEstimate(
            flops=4 * rows * length * hidden, bytes_accessed=2 * rows * length, transcendentals=0
        ),
    )(tokens, gate, up, *sums, *[in_hbm(value) for value, _, _ in wanted])


def grad_kernel(
    expert, low, high, pre_gate, pre_up, down, down_weight, grad_gate, grad_up, dots, gate_rows, dot_sums, rest, sems
):
    table = low.shape[1] - high.shape[1]
    half = high.shape[1]
    ready = down.shape[0]
    depth = part_of(ready, HIDDEN_PART)
    steps = ready // depth

    def copy_of(index):
        rows = pl.ds(pl.multiple_of(index * depth, depth), depth)
        source = pl.ds(pl.multiple_of(ready + index * depth, depth), depth)
        return pltpu.make_async_copy(down_weight.at[0, source], rest.at[rows], sems.at[index])

    for index in range(steps):
        copy_of(index).start()

    lanes = lax.broadcasted_iota(jnp.int32, (low.shape[0], table), 1)
    gate_rows[...] = jnp.sum(
        jnp.where(lanes == expert[0], low[:, :table].astype(jnp.float32), 0.0), axis=1, keepdims=True
    )
    dot_sums[...] = jnp.zeros_like(dot_sums)

    def block(weights, first, step):
        rows = pl.ds(pl.multiple_of(step * depth, depth), depth)
        span = pl.ds(pl.multiple_of(first + step * depth, depth), depth)
        grad_hidden = product(low[:, table:], weights[rows, :half], 1) + product(high[...], weights[rows, half:], 1)
        gates = pre_gate[:, span]
        ups = pre_up[:, span]
        sigma = jax.nn.sigmoid(gates)
        act = gates * sigma
        dot_sums[...] += jnp.sum(grad_hidden * (act * ups), axis=1, keepdims=True)
        scaled = gate_rows[...] * grad_hidden
        grad_gate[:, span] = (scaled * ups * sigma * (1.0 + gates * (1.0 - sigma))).astype(jnp.bfloat16)
        grad_up[:, span] = (scaled * act).astype(jnp.bfloat16)

    @pl.loop(0, steps)
    def _(step):
        block(down, 0, step)

    @pl.loop(0, steps)
    def _(step):
        copy_of(step).wait()
        block(rest, ready, step)

    dots[...] = jnp.where(lanes == expert[0], dot_sums[...], 0.0).astype(jnp.bfloat16)


def multiply_grads(expert, low, high, pre_gate, pre_up, down, down_weight):
    rows, hidden = pre_gate.shape
    width = down_weight.shape[2]
    table = low.shape[1] - high.shape[1]
    return pl.pallas_call(
        grad_kernel,
        out_shape=(
            pltpu.VMEM((rows, hidden), jnp.bfloat16),
            pltpu.VMEM((rows, hidden), jnp.bfloat16),
            pltpu.VMEM((rows, table), jnp.bfloat16),
        ),
        in_specs=[pl.BlockSpec(memory_space=pltpu.SMEM)]
        + [pl.BlockSpec(memory_space=pltpu.VMEM)] * 5
        + [pl.BlockSpec(memory_space=pl.ANY)],
        out_specs=(pl.BlockSpec(memory_space=pltpu.VMEM),) * 3,
        scratch_shapes=[
            pltpu.VMEM((rows, 1), jnp.float32),
            pltpu.VMEM((rows, 1), jnp.float32),
            pltpu.VMEM((hidden // 2, width), jnp.bfloat16),
            pltpu.SemaphoreType.DMA((hidden // 2 // part_of(hidden // 2, HIDDEN_PART),)),
        ],
        compiler_params=pltpu.CompilerParams(vmem_limit_bytes=GRAD_VMEM),
        cost_estimate=pl.CostEstimate(
            flops=2 * rows * width * hidden, bytes_accessed=width * hidden, transcendentals=rows * hidden
        ),
    )(expert, low, high, pre_gate, pre_up, down, in_hbm(down_weight))


def output_kernel(grad_gate, grad_up, gate_copy, up_copy, *refs):
    dots, kept, sent = refs if len(refs) == 3 else (None,) + refs
    rows = kept.shape[0]
    columns = kept.shape[1] - (0 if dots is None else dots.shape[1])
    part = part_of(columns, COLUMN_PART)

    @pl.loop(0, columns // part)
    def _(step):
        span = pl.ds(pl.multiple_of(step * part, part), part)
        result = (product(gate_copy[span, :], grad_gate[...], 1) + product(up_copy[span, :], grad_up[...], 1)).T
        kept[:, span] = result[:rows]
        sent[:, span] = result[rows:].astype(jnp.bfloat16)

    if dots is not None:
        kept[:, columns:] = dots[:rows, :].astype(jnp.float32)
        sent[:, columns:] = dots[rows:, :]


def multiply_outputs(grad_gate, grad_up, gate_copy, up_copy, *dots):
    rows, hidden = grad_gate.shape
    columns = gate_copy.shape[0]
    total = columns + sum(value.shape[1] for value in dots)
    return pl.pallas_call(
        output_kernel,
        out_shape=(
            pltpu.VMEM((rows // 2, total), jnp.float32),
            pltpu.VMEM((rows // 2, total), jnp.bfloat16),
        ),
        in_specs=[pl.BlockSpec(memory_space=pltpu.VMEM)] * (4 + len(dots)),
        out_specs=(pl.BlockSpec(memory_space=pltpu.VMEM),) * 2,
        compiler_params=pltpu.CompilerParams(vmem_limit_bytes=OUTPUT_VMEM),
        cost_estimate=pl.CostEstimate(
            flops=4 * rows * columns * hidden, bytes_accessed=4 * rows * columns, transcendentals=0
        ),
    )(grad_gate, grad_up, gate_copy, up_copy, *dots)


def gathered_plan(tokens, out_grad, kept_mask, routes, router, gate_weight, up_weight, down_weight):
    row_count, width = tokens.shape
    expert_count = lax.axis_size("expert")
    columns = lax.broadcasted_iota(jnp.int32, (row_count, expert_count), 1)
    first_hot = (routes[:, 0:1] == columns).astype(jnp.float32)
    second_hot = (routes[:, 1:2] == columns).astype(jnp.float32)
    keep_rows = kept_mask.astype(jnp.float32)
    half, quarter = width // 2, width // 4
    table = 128
    token_z = gather_z(tokens)
    logits = jnp.dot(tokens, router, preferred_element_type=jnp.float32)
    first_logit = jnp.sum(logits * first_hot, axis=1)
    second_logit = jnp.sum(logits * second_hot, axis=1)
    gate_first = jax.nn.sigmoid(first_logit - second_logit)
    gate_second = jax.nn.sigmoid(second_logit - first_logit)
    gate_table = (first_hot * gate_first[:, None] + second_hot * gate_second[:, None]) * keep_rows[:, None]
    gate_table = jnp.pad(gate_table.astype(jnp.bfloat16), ((0, 0), (0, table - expert_count)))
    grad_z = gather_z(after_others(jnp.concatenate([gate_table, out_grad], axis=1), token_z[1]))
    token_near = gather_near(token_z, half)
    (gate_low,) = fetch(0, half, token_near[0][0], gate_weight)
    token_near = after_others(token_near, gate_low)
    token_far = gather_far(*token_near)
    (up_low,) = fetch(0, half, token_near[1][1], up_weight)
    grad_near = gather_near(after_others(grad_z, token_near), half + table)
    grad_far = gather_far(*after_others(grad_near, token_far))
    token_far = after_others(token_far, up_low)
    token_low, token_high = gather_core(token_near[0], token_far[0], token_near[1], token_far[1])
    pre_gate, pre_up, gate_high, up_high = multiply_tokens(
        token_low, gate_low, up_low, 0, half, (), ((gate_weight, half, half), (up_weight, half, half))
    )
    pre_gate, pre_up = multiply_tokens(token_high, gate_high, up_high, 0, quarter, (pre_gate, pre_up))
    grad_far = after_others(grad_far, pre_gate)
    pre_gate, pre_up, down = multiply_tokens(
        token_high, gate_high, up_high, quarter, quarter, (pre_gate, pre_up),
        ((down_weight, 0, down_weight.shape[1] // 2),),
    )
    grad_halves = gather_core(grad_near[0], grad_far[0], grad_near[1], grad_far[1])
    expert = lax.axis_index("expert").astype(jnp.int32).reshape(1)
    grad_gate, grad_up, dots = multiply_grads(expert, *grad_halves, pre_gate, pre_up, down, down_weight)
    kept, sent = multiply_outputs(grad_gate, grad_up, gate_low, up_low, dots)
    chunk = scatter_core(kept, sent)
    kept, sent = multiply_outputs(grad_gate, grad_up, gate_high, up_high)
    chunk = scatter_far(after_others(chunk, sent), half // 2)
    later = scatter_core(kept, sent)
    chunk = scatter_near(*after_others(chunk, later))
    later = scatter_far(later, half // 2)
    chunk = scatter_z(after_others(chunk, later))
    later = scatter_z(scatter_near(*later))
    expert_sum = jnp.concatenate([chunk[:, :half], later], axis=1)
    dot_table = chunk[:, half:half + expert_count]
    dot_first = jnp.sum(dot_table * first_hot, axis=1)
    dot_second = jnp.sum(dot_table * second_hot, axis=1)
    product = gate_first * gate_second * keep_rows
    grad_first = product * (dot_first - dot_second)
    grad_second = product * (dot_second - dot_first)
    logit_grad = first_hot * grad_first[:, None] + second_hot * grad_second[:, None]
    router_term = jnp.dot(logit_grad, router.astype(jnp.float32).T, precision=lax.Precision.HIGHEST)
    d_tokens = ((expert_sum + router_term) * keep_rows[:, None]).astype(jnp.bfloat16)
    gate_grad = jnp.stack([grad_first, grad_second], axis=1)
    return (d_tokens, gate_grad)


def solution(mesh):
    gathers = mesh.shape["seq"] == 2 and mesh.shape["expert"] == 4 and mesh.shape["mp"] in (2, 4)
    return jax.shard_map(
        gathered_plan if gathers else routed_plan,
        mesh=mesh,
        in_specs=(
            P(("seq", "expert", "mp"), None),
            P(("seq", "expert", "mp"), None),
            P(("seq", "expert", "mp")),
            P(("seq", "expert", "mp"), None),
            P(),
            P("expert", None, ("seq", "mp")),
            P("expert", None, ("seq", "mp")),
            P("expert", ("seq", "mp"), None),
        ),
        out_specs=(P(("seq", "expert", "mp"), None), P(("seq", "expert", "mp"), None)),
        check_vma=False,
    )
```

```python
import functools
import math

import jax
import jax.numpy as jnp
from jax import lax
from jax.experimental import pallas as pl
from jax.experimental.pallas import tpu as pltpu
from jax.sharding import PartitionSpec as P

TOKEN_PART = 512
HIDDEN_PART = 256
COLUMN_PART = 1536
TOKEN_VMEM = 6 * 2 ** 20
GRAD_VMEM = 10 * 2 ** 20
OUTPUT_VMEM = 6 * 2 ** 20


def routed_plan(tokens, out_grad, kept_mask, routes, router, gate_weight, up_weight, down_weight):
    row_count = tokens.shape[0]
    width = tokens.shape[1]
    expert_count = lax.axis_size("expert")
    capacity = max(3 * row_count // 8, 2 * row_count // expert_count)
    logits = jnp.dot(tokens, router, preferred_element_type=jnp.float32)
    columns = lax.broadcasted_iota(jnp.int32, (row_count, expert_count), 1)
    first_hot = (routes[:, 0:1] == columns).astype(jnp.float32)
    second_hot = (routes[:, 1:2] == columns).astype(jnp.float32)
    first_logit = jnp.sum(logits * first_hot, axis=1)
    second_logit = jnp.sum(logits * second_hot, axis=1)
    gate_first = jax.nn.sigmoid(first_logit - second_logit)
    gate_second = jax.nn.sigmoid(second_logit - first_logit)
    keep_rows = kept_mask.astype(jnp.float32)
    chosen = ((first_hot + second_hot) * keep_rows[:, None]).astype(jnp.int32)
    position = jnp.cumsum(chosen, axis=0) - 1
    slot_iota = lax.broadcasted_iota(jnp.int32, (row_count, expert_count, capacity), 2)
    select_mask = (chosen[:, :, None] == 1) & (position[:, :, None] == slot_iota)
    select_bf = select_mask.astype(jnp.bfloat16)
    select_full = select_mask.astype(jnp.float32)
    token_send = jnp.einsum(
        "tec,td->ecd", select_bf, tokens, preferred_element_type=jnp.float32
    ).astype(jnp.bfloat16)
    grad_send = jnp.einsum(
        "tec,td->ecd", select_bf, out_grad, preferred_element_type=jnp.float32
    ).astype(jnp.bfloat16)
    gate_table = first_hot * gate_first[:, None] + second_hot * gate_second[:, None]
    gate_send = jnp.einsum(
        "tec,te->ec", select_full, gate_table, precision=lax.Precision.HIGHEST
    ).astype(jnp.bfloat16)
    token_recv, grad_recv, gate_recv = (
        lax.all_to_all(token_send, "expert", split_axis=0, concat_axis=0, tiled=True),
        lax.all_to_all(grad_send, "expert", split_axis=0, concat_axis=0, tiled=True),
        lax.all_to_all(gate_send, "expert", split_axis=0, concat_axis=0, tiled=True),
    )
    token_all, grad_all, gate_all = (
        lax.all_gather(token_recv, ("seq", "mp"), axis=0, tiled=True),
        lax.all_gather(grad_recv, ("seq", "mp"), axis=0, tiled=True),
        lax.all_gather(gate_recv, ("seq", "mp"), axis=0, tiled=True),
    )
    token_all = token_all.reshape(-1, width)
    grad_all = grad_all.reshape(-1, width)
    gate_all = gate_all.reshape(-1)
    gate_local = gate_weight[0]
    up_local = up_weight[0]
    down_local = down_weight[0]
    pre_gate = jnp.dot(token_all, gate_local, preferred_element_type=jnp.float32)
    pre_up = jnp.dot(token_all, up_local, preferred_element_type=jnp.float32)
    sigma = jax.nn.sigmoid(pre_gate)
    act = pre_gate * sigma
    hidden = act * pre_up
    grad_hidden = jnp.dot(grad_all, down_local.T, preferred_element_type=jnp.float32)
    gate_dot = jnp.sum(grad_hidden * hidden, axis=1)
    scaled = gate_all.astype(jnp.float32)[:, None] * grad_hidden
    grad_gate = (scaled * pre_up * sigma * (1.0 + pre_gate * (1.0 - sigma))).astype(jnp.bfloat16)
    grad_up = (scaled * act).astype(jnp.bfloat16)
    expert_grad = jnp.dot(grad_gate, gate_local.T, preferred_element_type=jnp.float32)
    expert_grad = expert_grad + jnp.dot(grad_up, up_local.T, preferred_element_type=jnp.float32)
    grad_own = lax.psum_scatter(
        expert_grad.astype(jnp.bfloat16), ("seq", "mp"), scatter_dimension=0, tiled=True
    ).astype(jnp.float32)
    dot_own = lax.psum_scatter(gate_dot, ("seq", "mp"), scatter_dimension=0, tiled=True)
    grad_back, dot_back = (
        lax.all_to_all(
            grad_own.reshape(expert_count, capacity, width).astype(jnp.bfloat16),
            "expert",
            split_axis=0,
            concat_axis=0,
            tiled=True,
        ).astype(jnp.float32),
        lax.all_to_all(
            dot_own.reshape(expert_count, capacity).astype(jnp.bfloat16),
            "expert",
            split_axis=0,
            concat_axis=0,
            tiled=True,
        ).astype(jnp.float32),
    )
    expert_sum = jnp.einsum("tec,ecd->td", select_full, grad_back, precision=lax.Precision.HIGHEST)
    dot_table = jnp.einsum("tec,ec->te", select_full, dot_back, precision=lax.Precision.HIGHEST)
    dot_first = jnp.sum(dot_table * first_hot, axis=1)
    dot_second = jnp.sum(dot_table * second_hot, axis=1)
    product = gate_first * gate_second * keep_rows
    grad_first = product * (dot_first - dot_second)
    grad_second = product * (dot_second - dot_first)
    logit_grad = first_hot * grad_first[:, None] + second_hot * grad_second[:, None]
    router_term = jnp.dot(logit_grad, router.astype(jnp.float32).T, precision=lax.Precision.HIGHEST)
    d_tokens = ((expert_sum + router_term) * keep_rows[:, None]).astype(jnp.bfloat16)
    gate_grad = jnp.stack([grad_first, grad_second], axis=1)
    return (d_tokens, gate_grad)

def swap(value, axis, bit):
    return lax.ppermute(value, axis, [(i ^ bit, i) for i in range(lax.axis_size(axis))])


def swap_x(value):
    return swap(value, "seq", 1)


def swap_y(value):
    return swap(value, "expert", 2)


def swap_core(value):
    return swap(value, "expert", 1)


def after_others(values, others):
    return lax.optimization_barrier((values, others))[0]


def gather_z(rows):
    return [rows] + [swap(rows, "mp", k) for k in range(1, lax.axis_size("mp"))]


def gather_near(z_rows, cut):
    rows = jnp.concatenate(z_rows, axis=0)
    low, high = rows[:, :cut], rows[:, cut:]
    return [low, swap_x(low)], [high, swap_y(high)]


def gather_far(low, high):
    return swap_y(jnp.concatenate(low, axis=0)), swap_x(jnp.concatenate(high, axis=0))


def gather_core(low, low_far, high, high_far):
    high_far = jnp.split(high_far, 2, axis=0)
    low = jnp.concatenate(low + [low_far], axis=0)
    high = jnp.concatenate([high[0], high_far[0], high[1], high_far[1]], axis=0)
    return tuple(jnp.concatenate([mine, swap_core(mine)], axis=0) for mine in (low, high))


def scatter_core(kept, sent):
    return kept + swap_core(sent).astype(jnp.float32)


def send(value, exchange):
    return exchange(value.astype(jnp.bfloat16)).astype(jnp.float32)


def scatter_far(total, cut):
    low, low_x, low_y, low_both = jnp.split(total[:, :cut], 4, axis=0)
    high, high_x, high_y, high_both = jnp.split(total[:, cut:], 4, axis=0)
    low_far = send(jnp.concatenate([low_y, low_both], axis=0), swap_y)
    high_far = send(jnp.concatenate([high_x, high_both], axis=0), swap_x)
    return jnp.concatenate([low, low_x], axis=0) + low_far, jnp.concatenate([high, high_y], axis=0) + high_far


def scatter_near(low, high):
    low, low_x = jnp.split(low, 2, axis=0)
    high, high_y = jnp.split(high, 2, axis=0)
    return jnp.concatenate([low + send(low_x, swap_x), high + send(high_y, swap_y)], axis=1)


def scatter_z(total):
    size = lax.axis_size("mp")
    rows = total.shape[0] // size
    result = total[:rows]
    for k in range(1, size):
        result = result + send(total[k * rows:(k + 1) * rows], lambda value: swap(value, "mp", k))
    return result


def product(a, b, b_dim):
    return lax.dot_general(a, b, (((1,), (b_dim,)), ((), ())), preferred_element_type=jnp.float32)


def part_of(length, wanted):
    return math.gcd(length, wanted)


def in_hbm(value):
    return pltpu.with_memory_space_constraint(value, pltpu.HBM)


def fetch_kernel(first, _, *refs):
    count = (len(refs) - 1) // 2
    sems = refs[-1]
    copies = []
    for index in range(count):
        target = refs[count + index]
        source = refs[index].at[0, pl.ds(first, target.shape[0])]
        copies.append(pltpu.make_async_copy(source, target, sems.at[index]))
    for copy in copies:
        copy.start()
    for copy in copies:
        copy.wait()


def fetch(first, length, earlier, *weights):
    shapes = [(length, value.shape[2]) for value in weights]
    return pl.pallas_call(
        functools.partial(fetch_kernel, first),
        out_shape=tuple(pltpu.VMEM(shape, jnp.bfloat16) for shape in shapes),
        in_specs=[pl.BlockSpec(memory_space=pl.ANY)] * (1 + len(weights)),
        out_specs=(pl.BlockSpec(memory_space=pltpu.VMEM),) * len(weights),
        scratch_shapes=[pltpu.SemaphoreType.DMA((len(weights),))],
        compiler_params=pltpu.CompilerParams(vmem_limit_bytes=TOKEN_VMEM),
        cost_estimate=pl.CostEstimate(
            flops=0, bytes_accessed=sum(2 * rows * hidden for rows, hidden in shapes), transcendentals=0
        ),
    )(earlier, *[in_hbm(value) for value in weights])


def first_token_kernel(sources, tokens, gate, gate_weight, up_weight, pre_gate, pre_up, up, gate_next, up_next, sems):
    copies = []
    for index, (weight, fetched) in enumerate(((up_weight, up), (gate_weight, gate_next), (up_weight, up_next))):
        source = weight.at[0, pl.ds(sources[index], fetched.shape[0])]
        copies.append(pltpu.make_async_copy(source, fetched, sems.at[index]))
    for copy in copies:
        copy.start()
    depth = part_of(tokens.shape[1], TOKEN_PART)
    for sums, weight in ((pre_gate, gate), (pre_up, up)):
        sums[...] = jnp.zeros_like(sums)
        if weight is up:
            copies[0].wait()

        @pl.loop(0, tokens.shape[1] // depth)
        def _(step):
            rows = pl.ds(pl.multiple_of(step * depth, depth), depth)
            sums[...] += product(tokens[:, rows], weight[rows, :], 0)

    for copy in copies[1:]:
        copy.wait()


def multiply_first_tokens(tokens, gate, gate_weight, up_weight):
    rows, length = tokens.shape
    hidden = gate.shape[1]
    return pl.pallas_call(
        functools.partial(first_token_kernel, (0, length, length)),
        out_shape=(pltpu.VMEM((rows, hidden), jnp.float32),) * 2 + (pltpu.VMEM(gate.shape, jnp.bfloat16),) * 3,
        in_specs=[pl.BlockSpec(memory_space=pltpu.VMEM)] * 2 + [pl.BlockSpec(memory_space=pl.ANY)] * 2,
        out_specs=(pl.BlockSpec(memory_space=pltpu.VMEM),) * 5,
        scratch_shapes=[pltpu.SemaphoreType.DMA((3,))],
        compiler_params=pltpu.CompilerParams(vmem_limit_bytes=TOKEN_VMEM),
        cost_estimate=pl.CostEstimate(
            flops=4 * rows * length * hidden, bytes_accessed=6 * length * hidden, transcendentals=0
        ),
    )(tokens, gate, in_hbm(gate_weight), in_hbm(up_weight))


def token_kernel(offset, length, sources, summed, tokens, gate, up, *refs):
    before, refs = refs[:summed], refs[summed:]
    count = len(sources)
    weights, (pre_gate, pre_up), fetched = refs[:count], refs[count:count + 2], refs[count + 2:2 * count + 2]
    depth = part_of(length, TOKEN_PART)
    copies = []
    for index in range(count):
        source = weights[index].at[0, pl.ds(sources[index], fetched[index].shape[0])]
        copies.append(pltpu.make_async_copy(source, fetched[index], refs[-1].at[index]))
    for copy in copies:
        copy.start()
    pre_gate[...] = before[0][...] if summed else jnp.zeros_like(pre_gate)
    pre_up[...] = before[1][...] if summed else jnp.zeros_like(pre_up)

    @pl.loop(0, length // depth)
    def _(step):
        rows = pl.ds(pl.multiple_of(offset + step * depth, depth), depth)
        pre_gate[...] += product(tokens[:, rows], gate[rows, :], 0)
        pre_up[...] += product(tokens[:, rows], up[rows, :], 0)

    for copy in copies:
        copy.wait()


def multiply_tokens(tokens, gate, up, offset, length, sums=(), wanted=()):
    rows, hidden = tokens.shape[0], gate.shape[1]
    shapes = [(count, value.shape[2]) for value, _, count in wanted]
    sources = tuple(first for _, first, _ in wanted)
    out_shape = (pltpu.VMEM((rows, hidden), jnp.float32),) * 2
    out_shape += tuple(pltpu.VMEM(shape, jnp.bfloat16) for shape in shapes)
    return pl.pallas_call(
        functools.partial(token_kernel, offset, length, sources, len(sums)),
        out_shape=out_shape,
        in_specs=[pl.BlockSpec(memory_space=pltpu.VMEM)] * (3 + len(sums))
        + [pl.BlockSpec(memory_space=pl.ANY)] * len(wanted),
        out_specs=(pl.BlockSpec(memory_space=pltpu.VMEM),) * len(out_shape),
        scratch_shapes=[pltpu.SemaphoreType.DMA((len(wanted),))] if wanted else [],
        compiler_params=pltpu.CompilerParams(vmem_limit_bytes=TOKEN_VMEM),
        cost_estimate=pl.CostEstimate(
            flops=4 * rows * length * hidden, bytes_accessed=2 * rows * length, transcendentals=0
        ),
    )(tokens, gate, up, *sums, *[in_hbm(value) for value, _, _ in wanted])


def grad_kernel(
    expert, low, high, pre_gate, pre_up, down, down_weight, grad_gate, grad_up, dots, gate_rows, dot_sums, rest, sems
):
    table = low.shape[1] - high.shape[1]
    half = high.shape[1]
    ready = down.shape[0]
    depth = part_of(ready, HIDDEN_PART)
    steps = ready // depth

    def copy_of(index):
        rows = pl.ds(pl.multiple_of(index * depth, depth), depth)
        source = pl.ds(pl.multiple_of(ready + index * depth, depth), depth)
        return pltpu.make_async_copy(down_weight.at[0, source], rest.at[rows], sems.at[index])

    for index in range(steps):
        copy_of(index).start()

    lanes = lax.broadcasted_iota(jnp.int32, (low.shape[0], table), 1)
    gate_rows[...] = jnp.sum(
        jnp.where(lanes == expert[0], low[:, :table].astype(jnp.float32), 0.0), axis=1, keepdims=True
    )
    dot_sums[...] = jnp.zeros_like(dot_sums)

    def block(weights, first, step):
        rows = pl.ds(pl.multiple_of(step * depth, depth), depth)
        span = pl.ds(pl.multiple_of(first + step * depth, depth), depth)
        grad_hidden = product(low[:, table:], weights[rows, :half], 1) + product(high[...], weights[rows, half:], 1)
        gates = pre_gate[:, span]
        ups = pre_up[:, span]
        sigma = jax.nn.sigmoid(gates)
        act = gates * sigma
        dot_sums[...] += jnp.sum(grad_hidden * (act * ups), axis=1, keepdims=True)
        scaled = gate_rows[...] * grad_hidden
        grad_gate[:, span] = (scaled * ups * sigma * (1.0 + gates * (1.0 - sigma))).astype(jnp.bfloat16)
        grad_up[:, span] = (scaled * act).astype(jnp.bfloat16)

    @pl.loop(0, steps)
    def _(step):
        block(down, 0, step)

    @pl.loop(0, steps)
    def _(step):
        copy_of(step).wait()
        block(rest, ready, step)

    dots[...] = jnp.where(lanes == expert[0], dot_sums[...], 0.0).astype(jnp.bfloat16)


def multiply_grads(expert, low, high, pre_gate, pre_up, down, down_weight):
    rows, hidden = pre_gate.shape
    width = down_weight.shape[2]
    table = low.shape[1] - high.shape[1]
    return pl.pallas_call(
        grad_kernel,
        out_shape=(
            pltpu.VMEM((rows, hidden), jnp.bfloat16),
            pltpu.VMEM((rows, hidden), jnp.bfloat16),
            pltpu.VMEM((rows, table), jnp.bfloat16),
        ),
        in_specs=[pl.BlockSpec(memory_space=pltpu.SMEM)]
        + [pl.BlockSpec(memory_space=pltpu.VMEM)] * 5
        + [pl.BlockSpec(memory_space=pl.ANY)],
        out_specs=(pl.BlockSpec(memory_space=pltpu.VMEM),) * 3,
        scratch_shapes=[
            pltpu.VMEM((rows, 1), jnp.float32),
            pltpu.VMEM((rows, 1), jnp.float32),
            pltpu.VMEM((hidden // 2, width), jnp.bfloat16),
            pltpu.SemaphoreType.DMA((hidden // 2 // part_of(hidden // 2, HIDDEN_PART),)),
        ],
        compiler_params=pltpu.CompilerParams(vmem_limit_bytes=GRAD_VMEM),
        cost_estimate=pl.CostEstimate(
            flops=2 * rows * width * hidden, bytes_accessed=width * hidden, transcendentals=rows * hidden
        ),
    )(expert, low, high, pre_gate, pre_up, down, in_hbm(down_weight))


def output_kernel(grad_gate, grad_up, gate_copy, up_copy, *refs):
    dots, kept, sent = refs if len(refs) == 3 else (None,) + refs
    rows = kept.shape[0]
    columns = kept.shape[1] - (0 if dots is None else dots.shape[1])
    part = part_of(columns, COLUMN_PART)

    @pl.loop(0, columns // part)
    def _(step):
        span = pl.ds(pl.multiple_of(step * part, part), part)
        result = (product(gate_copy[span, :], grad_gate[...], 1) + product(up_copy[span, :], grad_up[...], 1)).T
        kept[:, span] = result[:rows]
        sent[:, span] = result[rows:].astype(jnp.bfloat16)

    if dots is not None:
        kept[:, columns:] = dots[:rows, :].astype(jnp.float32)
        sent[:, columns:] = dots[rows:, :]


def multiply_outputs(grad_gate, grad_up, gate_copy, up_copy, *dots):
    rows, hidden = grad_gate.shape
    columns = gate_copy.shape[0]
    total = columns + sum(value.shape[1] for value in dots)
    return pl.pallas_call(
        output_kernel,
        out_shape=(
            pltpu.VMEM((rows // 2, total), jnp.float32),
            pltpu.VMEM((rows // 2, total), jnp.bfloat16),
        ),
        in_specs=[pl.BlockSpec(memory_space=pltpu.VMEM)] * (4 + len(dots)),
        out_specs=(pl.BlockSpec(memory_space=pltpu.VMEM),) * 2,
        compiler_params=pltpu.CompilerParams(vmem_limit_bytes=OUTPUT_VMEM),
        cost_estimate=pl.CostEstimate(
            flops=4 * rows * columns * hidden, bytes_accessed=4 * rows * columns, transcendentals=0
        ),
    )(grad_gate, grad_up, gate_copy, up_copy, *dots)


def gathered_plan(tokens, out_grad, kept_mask, routes, router, gate_weight, up_weight, down_weight):
    row_count, width = tokens.shape
    expert_count = lax.axis_size("expert")
    columns = lax.broadcasted_iota(jnp.int32, (row_count, expert_count), 1)
    first_hot = (routes[:, 0:1] == columns).astype(jnp.float32)
    second_hot = (routes[:, 1:2] == columns).astype(jnp.float32)
    keep_rows = kept_mask.astype(jnp.float32)
    half, quarter = width // 2, width // 4
    table = 128
    token_z = gather_z(tokens)
    logits = jnp.dot(tokens, router, preferred_element_type=jnp.float32)
    first_logit = jnp.sum(logits * first_hot, axis=1)
    second_logit = jnp.sum(logits * second_hot, axis=1)
    gate_first = jax.nn.sigmoid(first_logit - second_logit)
    gate_second = jax.nn.sigmoid(second_logit - first_logit)
    gate_table = (first_hot * gate_first[:, None] + second_hot * gate_second[:, None]) * keep_rows[:, None]
    gate_table = jnp.pad(gate_table.astype(jnp.bfloat16), ((0, 0), (0, table - expert_count)))
    grad_rows = jnp.concatenate([gate_table, out_grad], axis=1)
    (gate_low,) = fetch(0, half, grad_rows, gate_weight)
    grad_z = gather_z(after_others(grad_rows, token_z[1]))
    token_near = lax.optimization_barrier(gather_near(after_others(token_z, gate_low), half))
    token_far = gather_far(*token_near)
    grad_near = gather_near(after_others(grad_z, token_near), half + table)
    grad_far = gather_far(*after_others(grad_near, token_far))
    token_low, token_high = gather_core(token_near[0], token_far[0], token_near[1], token_far[1])
    pre_gate, pre_up, up_low, gate_high, up_high = multiply_first_tokens(token_low, gate_low, gate_weight, up_weight)
    pre_gate, pre_up = multiply_tokens(token_high, gate_high, up_high, 0, quarter, (pre_gate, pre_up))
    grad_far = after_others(grad_far, pre_gate)
    pre_gate, pre_up, down = multiply_tokens(
        token_high, gate_high, up_high, quarter, quarter, (pre_gate, pre_up),
        ((down_weight, 0, down_weight.shape[1] // 2),),
    )
    grad_halves = gather_core(grad_near[0], grad_far[0], grad_near[1], grad_far[1])
    expert = lax.axis_index("expert").astype(jnp.int32).reshape(1)
    grad_gate, grad_up, dots = multiply_grads(expert, *grad_halves, pre_gate, pre_up, down, down_weight)
    kept, sent = multiply_outputs(grad_gate, grad_up, gate_low, up_low, dots)
    chunk = scatter_core(kept, sent)
    kept, sent = multiply_outputs(grad_gate, grad_up, gate_high, up_high)
    chunk = scatter_far(after_others(chunk, sent), half // 2)
    later = scatter_core(kept, sent)
    chunk = scatter_near(*after_others(chunk, later))
    later = scatter_far(later, half // 2)
    chunk = scatter_z(after_others(chunk, later))
    later = scatter_z(scatter_near(*later))
    expert_sum = jnp.concatenate([chunk[:, :half], later], axis=1)
    dot_table = chunk[:, half:half + expert_count]
    dot_first = jnp.sum(dot_table * first_hot, axis=1)
    dot_second = jnp.sum(dot_table * second_hot, axis=1)
    product = gate_first * gate_second * keep_rows
    grad_first = product * (dot_first - dot_second)
    grad_second = product * (dot_second - dot_first)
    logit_grad = first_hot * grad_first[:, None] + second_hot * grad_second[:, None]
    router_term = jnp.dot(logit_grad, router.astype(jnp.float32).T, precision=lax.Precision.HIGHEST)
    d_tokens = ((expert_sum + router_term) * keep_rows[:, None]).astype(jnp.bfloat16)
    gate_grad = jnp.stack([grad_first, grad_second], axis=1)
    return (d_tokens, gate_grad)


def solution(mesh):
    gathers = mesh.shape["seq"] == 2 and mesh.shape["expert"] == 4 and mesh.shape["mp"] in (2, 4)
    return jax.shard_map(
        gathered_plan if gathers else routed_plan,
        mesh=mesh,
        in_specs=(
            P(("seq", "expert", "mp"), None),
            P(("seq", "expert", "mp"), None),
            P(("seq", "expert", "mp")),
            P(("seq", "expert", "mp"), None),
            P(),
            P("expert", None, ("seq", "mp")),
            P("expert", None, ("seq", "mp")),
            P("expert", ("seq", "mp"), None),
        ),
        out_specs=(P(("seq", "expert", "mp"), None), P(("seq", "expert", "mp"), None)),
        check_vma=False,
    )
```

```python
import functools
import math

import jax
import jax.numpy as jnp
from jax import lax
from jax.experimental import pallas as pl
from jax.experimental.pallas import tpu as pltpu
from jax.sharding import PartitionSpec as P

TOKEN_PART = 512
HIDDEN_PART = 256
COLUMN_PART = 1536
TOKEN_VMEM = 6 * 2 ** 20
GRAD_VMEM = 10 * 2 ** 20
OUTPUT_VMEM = 6 * 2 ** 20


def routed_plan(tokens, out_grad, kept_mask, routes, router, gate_weight, up_weight, down_weight):
    row_count = tokens.shape[0]
    width = tokens.shape[1]
    expert_count = lax.axis_size("expert")
    capacity = max(3 * row_count // 8, 2 * row_count // expert_count)
    logits = jnp.dot(tokens, router, preferred_element_type=jnp.float32)
    columns = lax.broadcasted_iota(jnp.int32, (row_count, expert_count), 1)
    first_hot = (routes[:, 0:1] == columns).astype(jnp.float32)
    second_hot = (routes[:, 1:2] == columns).astype(jnp.float32)
    first_logit = jnp.sum(logits * first_hot, axis=1)
    second_logit = jnp.sum(logits * second_hot, axis=1)
    gate_first = jax.nn.sigmoid(first_logit - second_logit)
    gate_second = jax.nn.sigmoid(second_logit - first_logit)
    keep_rows = kept_mask.astype(jnp.float32)
    chosen = ((first_hot + second_hot) * keep_rows[:, None]).astype(jnp.int32)
    position = jnp.cumsum(chosen, axis=0) - 1
    slot_iota = lax.broadcasted_iota(jnp.int32, (row_count, expert_count, capacity), 2)
    select_mask = (chosen[:, :, None] == 1) & (position[:, :, None] == slot_iota)
    select_bf = select_mask.astype(jnp.bfloat16)
    select_full = select_mask.astype(jnp.float32)
    token_send = jnp.einsum(
        "tec,td->ecd", select_bf, tokens, preferred_element_type=jnp.float32
    ).astype(jnp.bfloat16)
    grad_send = jnp.einsum(
        "tec,td->ecd", select_bf, out_grad, preferred_element_type=jnp.float32
    ).astype(jnp.bfloat16)
    gate_table = first_hot * gate_first[:, None] + second_hot * gate_second[:, None]
    gate_send = jnp.einsum(
        "tec,te->ec", select_full, gate_table, precision=lax.Precision.HIGHEST
    ).astype(jnp.bfloat16)
    token_recv, grad_recv, gate_recv = (
        lax.all_to_all(token_send, "expert", split_axis=0, concat_axis=0, tiled=True),
        lax.all_to_all(grad_send, "expert", split_axis=0, concat_axis=0, tiled=True),
        lax.all_to_all(gate_send, "expert", split_axis=0, concat_axis=0, tiled=True),
    )
    token_all, grad_all, gate_all = (
        lax.all_gather(token_recv, ("seq", "mp"), axis=0, tiled=True),
        lax.all_gather(grad_recv, ("seq", "mp"), axis=0, tiled=True),
        lax.all_gather(gate_recv, ("seq", "mp"), axis=0, tiled=True),
    )
    token_all = token_all.reshape(-1, width)
    grad_all = grad_all.reshape(-1, width)
    gate_all = gate_all.reshape(-1)
    gate_local = gate_weight[0]
    up_local = up_weight[0]
    down_local = down_weight[0]
    pre_gate = jnp.dot(token_all, gate_local, preferred_element_type=jnp.float32)
    pre_up = jnp.dot(token_all, up_local, preferred_element_type=jnp.float32)
    sigma = jax.nn.sigmoid(pre_gate)
    act = pre_gate * sigma
    hidden = act * pre_up
    grad_hidden = jnp.dot(grad_all, down_local.T, preferred_element_type=jnp.float32)
    gate_dot = jnp.sum(grad_hidden * hidden, axis=1)
    scaled = gate_all.astype(jnp.float32)[:, None] * grad_hidden
    grad_gate = (scaled * pre_up * sigma * (1.0 + pre_gate * (1.0 - sigma))).astype(jnp.bfloat16)
    grad_up = (scaled * act).astype(jnp.bfloat16)
    expert_grad = jnp.dot(grad_gate, gate_local.T, preferred_element_type=jnp.float32)
    expert_grad = expert_grad + jnp.dot(grad_up, up_local.T, preferred_element_type=jnp.float32)
    grad_own = lax.psum_scatter(
        expert_grad.astype(jnp.bfloat16), ("seq", "mp"), scatter_dimension=0, tiled=True
    ).astype(jnp.float32)
    dot_own = lax.psum_scatter(gate_dot, ("seq", "mp"), scatter_dimension=0, tiled=True)
    grad_back, dot_back = (
        lax.all_to_all(
            grad_own.reshape(expert_count, capacity, width).astype(jnp.bfloat16),
            "expert",
            split_axis=0,
            concat_axis=0,
            tiled=True,
        ).astype(jnp.float32),
        lax.all_to_all(
            dot_own.reshape(expert_count, capacity).astype(jnp.bfloat16),
            "expert",
            split_axis=0,
            concat_axis=0,
            tiled=True,
        ).astype(jnp.float32),
    )
    expert_sum = jnp.einsum("tec,ecd->td", select_full, grad_back, precision=lax.Precision.HIGHEST)
    dot_table = jnp.einsum("tec,ec->te", select_full, dot_back, precision=lax.Precision.HIGHEST)
    dot_first = jnp.sum(dot_table * first_hot, axis=1)
    dot_second = jnp.sum(dot_table * second_hot, axis=1)
    product = gate_first * gate_second * keep_rows
    grad_first = product * (dot_first - dot_second)
    grad_second = product * (dot_second - dot_first)
    logit_grad = first_hot * grad_first[:, None] + second_hot * grad_second[:, None]
    router_term = jnp.dot(logit_grad, router.astype(jnp.float32).T, precision=lax.Precision.HIGHEST)
    d_tokens = ((expert_sum + router_term) * keep_rows[:, None]).astype(jnp.bfloat16)
    gate_grad = jnp.stack([grad_first, grad_second], axis=1)
    return (d_tokens, gate_grad)

def swap(value, axis, bit):
    return lax.ppermute(value, axis, [(i ^ bit, i) for i in range(lax.axis_size(axis))])


def swap_x(value):
    return swap(value, "seq", 1)


def swap_y(value):
    return swap(value, "expert", 2)


def swap_core(value):
    return swap(value, "expert", 1)


def after_others(values, others):
    return lax.optimization_barrier((values, others))[0]


def gather_z(rows):
    return [rows] + [swap(rows, "mp", k) for k in range(1, lax.axis_size("mp"))]


def gather_near(z_rows, cut):
    rows = jnp.concatenate(z_rows, axis=0)
    low, high = rows[:, :cut], rows[:, cut:]
    return [low, swap_x(low)], [high, swap_y(high)]


def gather_far(low, high):
    return swap_y(jnp.concatenate(low, axis=0)), swap_x(jnp.concatenate(high, axis=0))


def gather_core(low, low_far, high, high_far):
    high_far = jnp.split(high_far, 2, axis=0)
    low = jnp.concatenate(low + [low_far], axis=0)
    high = jnp.concatenate([high[0], high_far[0], high[1], high_far[1]], axis=0)
    return tuple(jnp.concatenate([mine, swap_core(mine)], axis=0) for mine in (low, high))


def scatter_core(kept, sent):
    return kept + swap_core(sent).astype(jnp.float32)


def send(value, exchange):
    return exchange(value.astype(jnp.bfloat16)).astype(jnp.float32)


def scatter_far(total, cut):
    low, low_x, low_y, low_both = jnp.split(total[:, :cut], 4, axis=0)
    high, high_x, high_y, high_both = jnp.split(total[:, cut:], 4, axis=0)
    low_far = send(jnp.concatenate([low_y, low_both], axis=0), swap_y)
    high_far = send(jnp.concatenate([high_x, high_both], axis=0), swap_x)
    return jnp.concatenate([low, low_x], axis=0) + low_far, jnp.concatenate([high, high_y], axis=0) + high_far


def scatter_near(low, high):
    low, low_x = jnp.split(low, 2, axis=0)
    high, high_y = jnp.split(high, 2, axis=0)
    return jnp.concatenate([low + send(low_x, swap_x), high + send(high_y, swap_y)], axis=1)


def scatter_z(total):
    size = lax.axis_size("mp")
    rows = total.shape[0] // size
    result = total[:rows]
    for k in range(1, size):
        result = result + send(total[k * rows:(k + 1) * rows], lambda value: swap(value, "mp", k))
    return result


def product(a, b, b_dim):
    return lax.dot_general(a, b, (((1,), (b_dim,)), ((), ())), preferred_element_type=jnp.float32)


def part_of(length, wanted):
    return math.gcd(length, wanted)


def in_hbm(value):
    return pltpu.with_memory_space_constraint(value, pltpu.HBM)


def fetch_kernel(first, _, *refs):
    count = (len(refs) - 1) // 2
    sems = refs[-1]
    copies = []
    for index in range(count):
        target = refs[count + index]
        source = refs[index].at[0, pl.ds(first, target.shape[0])]
        copies.append(pltpu.make_async_copy(source, target, sems.at[index]))
    for copy in copies:
        copy.start()
    for copy in copies:
        copy.wait()


def fetch(first, length, earlier, *weights):
    shapes = [(length, value.shape[2]) for value in weights]
    return pl.pallas_call(
        functools.partial(fetch_kernel, first),
        out_shape=tuple(pltpu.VMEM(shape, jnp.bfloat16) for shape in shapes),
        in_specs=[pl.BlockSpec(memory_space=pl.ANY)] * (1 + len(weights)),
        out_specs=(pl.BlockSpec(memory_space=pltpu.VMEM),) * len(weights),
        scratch_shapes=[pltpu.SemaphoreType.DMA((len(weights),))],
        compiler_params=pltpu.CompilerParams(vmem_limit_bytes=TOKEN_VMEM),
        cost_estimate=pl.CostEstimate(
            flops=0, bytes_accessed=sum(2 * rows * hidden for rows, hidden in shapes), transcendentals=0
        ),
    )(earlier, *[in_hbm(value) for value in weights])


def token_kernel(offset, length, sources, summed, tokens, gate, up, *refs):
    before, refs = refs[:summed], refs[summed:]
    count = len(sources)
    weights, (pre_gate, pre_up), fetched = refs[:count], refs[count:count + 2], refs[count + 2:2 * count + 2]
    depth = part_of(length, TOKEN_PART)
    copies = []
    for index in range(count):
        source = weights[index].at[0, pl.ds(sources[index], fetched[index].shape[0])]
        copies.append(pltpu.make_async_copy(source, fetched[index], refs[-1].at[index]))
    for copy in copies:
        copy.start()
    pre_gate[...] = before[0][...] if summed else jnp.zeros_like(pre_gate)
    pre_up[...] = before[1][...] if summed else jnp.zeros_like(pre_up)

    @pl.loop(0, length // depth)
    def _(step):
        rows = pl.ds(pl.multiple_of(offset + step * depth, depth), depth)
        pre_gate[...] += product(tokens[:, rows], gate[rows, :], 0)
        pre_up[...] += product(tokens[:, rows], up[rows, :], 0)

    for copy in copies:
        copy.wait()


def multiply_tokens(tokens, gate, up, offset, length, sums=(), wanted=()):
    rows, hidden = tokens.shape[0], gate.shape[1]
    shapes = [(count, value.shape[2]) for value, _, count in wanted]
    sources = tuple(first for _, first, _ in wanted)
    out_shape = (pltpu.VMEM((rows, hidden), jnp.float32),) * 2
    out_shape += tuple(pltpu.VMEM(shape, jnp.bfloat16) for shape in shapes)
    return pl.pallas_call(
        functools.partial(token_kernel, offset, length, sources, len(sums)),
        out_shape=out_shape,
        in_specs=[pl.BlockSpec(memory_space=pltpu.VMEM)] * (3 + len(sums))
        + [pl.BlockSpec(memory_space=pl.ANY)] * len(wanted),
        out_specs=(pl.BlockSpec(memory_space=pltpu.VMEM),) * len(out_shape),
        scratch_shapes=[pltpu.SemaphoreType.DMA((len(wanted),))] if wanted else [],
        compiler_params=pltpu.CompilerParams(vmem_limit_bytes=TOKEN_VMEM),
        cost_estimate=pl.CostEstimate(
            flops=4 * rows * length * hidden, bytes_accessed=2 * rows * length, transcendentals=0
        ),
    )(tokens, gate, up, *sums, *[in_hbm(value) for value, _, _ in wanted])


def grad_kernel(
    expert, low, high, pre_gate, pre_up, down, down_weight, grad_gate, grad_up, dots, gate_rows, dot_sums, rest, sems
):
    table = low.shape[1] - high.shape[1]
    half = high.shape[1]
    ready = down.shape[0]
    depth = part_of(ready, HIDDEN_PART)
    steps = ready // depth

    def copy_of(index):
        rows = pl.ds(pl.multiple_of(index * depth, depth), depth)
        source = pl.ds(pl.multiple_of(ready + index * depth, depth), depth)
        return pltpu.make_async_copy(down_weight.at[0, source], rest.at[rows], sems.at[index])

    for index in range(steps):
        copy_of(index).start()

    lanes = lax.broadcasted_iota(jnp.int32, (low.shape[0], table), 1)
    gate_rows[...] = jnp.sum(
        jnp.where(lanes == expert[0], low[:, :table].astype(jnp.float32), 0.0), axis=1, keepdims=True
    )
    dot_sums[...] = jnp.zeros_like(dot_sums)

    def block(weights, first, step):
        rows = pl.ds(pl.multiple_of(step * depth, depth), depth)
        span = pl.ds(pl.multiple_of(first + step * depth, depth), depth)
        grad_hidden = product(low[:, table:], weights[rows, :half], 1) + product(high[...], weights[rows, half:], 1)
        gates = pre_gate[:, span]
        ups = pre_up[:, span]
        sigma = jax.nn.sigmoid(gates)
        act = gates * sigma
        dot_sums[...] += jnp.sum(grad_hidden * (act * ups), axis=1, keepdims=True)
        scaled = gate_rows[...] * grad_hidden
        grad_gate[:, span] = (scaled * ups * sigma * (1.0 + gates * (1.0 - sigma))).astype(jnp.bfloat16)
        grad_up[:, span] = (scaled * act).astype(jnp.bfloat16)

    @pl.loop(0, steps)
    def _(step):
        block(down, 0, step)

    @pl.loop(0, steps)
    def _(step):
        copy_of(step).wait()
        block(rest, ready, step)

    dots[...] = jnp.where(lanes == expert[0], dot_sums[...], 0.0).astype(jnp.bfloat16)


def multiply_grads(expert, low, high, pre_gate, pre_up, down, down_weight):
    rows, hidden = pre_gate.shape
    width = down_weight.shape[2]
    table = low.shape[1] - high.shape[1]
    return pl.pallas_call(
        grad_kernel,
        out_shape=(
            pltpu.VMEM((rows, hidden), jnp.bfloat16),
            pltpu.VMEM((rows, hidden), jnp.bfloat16),
            pltpu.VMEM((rows, table), jnp.bfloat16),
        ),
        in_specs=[pl.BlockSpec(memory_space=pltpu.SMEM)]
        + [pl.BlockSpec(memory_space=pltpu.VMEM)] * 5
        + [pl.BlockSpec(memory_space=pl.ANY)],
        out_specs=(pl.BlockSpec(memory_space=pltpu.VMEM),) * 3,
        scratch_shapes=[
            pltpu.VMEM((rows, 1), jnp.float32),
            pltpu.VMEM((rows, 1), jnp.float32),
            pltpu.VMEM((hidden // 2, width), jnp.bfloat16),
            pltpu.SemaphoreType.DMA((hidden // 2 // part_of(hidden // 2, HIDDEN_PART),)),
        ],
        compiler_params=pltpu.CompilerParams(vmem_limit_bytes=GRAD_VMEM),
        cost_estimate=pl.CostEstimate(
            flops=2 * rows * width * hidden, bytes_accessed=width * hidden, transcendentals=rows * hidden
        ),
    )(expert, low, high, pre_gate, pre_up, down, in_hbm(down_weight))


def output_kernel(grad_gate, grad_up, gate_copy, up_copy, *refs):
    dots, kept, sent = refs if len(refs) == 3 else (None,) + refs
    rows = kept.shape[0]
    columns = kept.shape[1] - (0 if dots is None else dots.shape[1])
    part = part_of(columns, COLUMN_PART)

    @pl.loop(0, columns // part)
    def _(step):
        span = pl.ds(pl.multiple_of(step * part, part), part)
        result = (product(gate_copy[span, :], grad_gate[...], 1) + product(up_copy[span, :], grad_up[...], 1)).T
        kept[:, span] = result[:rows]
        sent[:, span] = result[rows:].astype(jnp.bfloat16)

    if dots is not None:
        kept[:, columns:] = dots[:rows, :].astype(jnp.float32)
        sent[:, columns:] = dots[rows:, :]


def multiply_outputs(grad_gate, grad_up, gate_copy, up_copy, *dots):
    rows, hidden = grad_gate.shape
    columns = gate_copy.shape[0]
    total = columns + sum(value.shape[1] for value in dots)
    return pl.pallas_call(
        output_kernel,
        out_shape=(
            pltpu.VMEM((rows // 2, total), jnp.float32),
            pltpu.VMEM((rows // 2, total), jnp.bfloat16),
        ),
        in_specs=[pl.BlockSpec(memory_space=pltpu.VMEM)] * (4 + len(dots)),
        out_specs=(pl.BlockSpec(memory_space=pltpu.VMEM),) * 2,
        compiler_params=pltpu.CompilerParams(vmem_limit_bytes=OUTPUT_VMEM),
        cost_estimate=pl.CostEstimate(
            flops=4 * rows * columns * hidden, bytes_accessed=4 * rows * columns, transcendentals=0
        ),
    )(grad_gate, grad_up, gate_copy, up_copy, *dots)


def gathered_plan(tokens, out_grad, kept_mask, routes, router, gate_weight, up_weight, down_weight):
    row_count, width = tokens.shape
    expert_count = lax.axis_size("expert")
    columns = lax.broadcasted_iota(jnp.int32, (row_count, expert_count), 1)
    first_hot = (routes[:, 0:1] == columns).astype(jnp.float32)
    second_hot = (routes[:, 1:2] == columns).astype(jnp.float32)
    keep_rows = kept_mask.astype(jnp.float32)
    half, quarter = width // 2, width // 4
    table = 128
    token_z = gather_z(tokens)
    logits = jnp.dot(tokens, router, preferred_element_type=jnp.float32)
    first_logit = jnp.sum(logits * first_hot, axis=1)
    second_logit = jnp.sum(logits * second_hot, axis=1)
    gate_first = jax.nn.sigmoid(first_logit - second_logit)
    gate_second = jax.nn.sigmoid(second_logit - first_logit)
    gate_table = (first_hot * gate_first[:, None] + second_hot * gate_second[:, None]) * keep_rows[:, None]
    gate_table = jnp.pad(gate_table.astype(jnp.bfloat16), ((0, 0), (0, table - expert_count)))
    grad_z = gather_z(after_others(jnp.concatenate([gate_table, out_grad], axis=1), token_z[1]))
    token_near = gather_near(token_z, half)
    (gate_low,) = fetch(0, half, token_near[0][0], gate_weight)
    token_near = after_others(token_near, gate_low)
    token_far = gather_far(*token_near)
    (up_low,) = fetch(0, half, token_near[1][1], up_weight)
    grad_near = gather_near(after_others(grad_z, token_near), half + table)
    grad_far = gather_far(*after_others(grad_near, token_far))
    token_far = after_others(token_far, up_low)
    token_low, token_high = gather_core(token_near[0], token_far[0], token_near[1], token_far[1])
    pre_gate, pre_up, gate_high, up_high = multiply_tokens(
        token_low, gate_low, up_low, 0, half, (), ((gate_weight, half, half), (up_weight, half, half))
    )
    pre_gate, pre_up, down = multiply_tokens(
        token_high, gate_high, up_high, 0, quarter, (pre_gate, pre_up),
        ((down_weight, 0, down_weight.shape[1] // 2),),
    )
    grad_far = after_others(grad_far, pre_gate)
    pre_gate, pre_up = multiply_tokens(token_high, gate_high, up_high, quarter, quarter, (pre_gate, pre_up))
    grad_halves = gather_core(grad_near[0], grad_far[0], grad_near[1], grad_far[1])
    expert = lax.axis_index("expert").astype(jnp.int32).reshape(1)
    grad_gate, grad_up, dots = multiply_grads(expert, *grad_halves, pre_gate, pre_up, down, down_weight)
    kept, sent = multiply_outputs(grad_gate, grad_up, gate_low, up_low, dots)
    chunk = scatter_core(kept, sent)
    kept, sent = multiply_outputs(grad_gate, grad_up, gate_high, up_high)
    chunk = scatter_far(after_others(chunk, sent), half // 2)
    later = scatter_core(kept, sent)
    chunk = scatter_near(*after_others(chunk, later))
    later = scatter_far(later, half // 2)
    chunk = scatter_z(after_others(chunk, later))
    later = scatter_z(scatter_near(*later))
    expert_sum = jnp.concatenate([chunk[:, :half], later], axis=1)
    dot_table = chunk[:, half:half + expert_count]
    dot_first = jnp.sum(dot_table * first_hot, axis=1)
    dot_second = jnp.sum(dot_table * second_hot, axis=1)
    product = gate_first * gate_second * keep_rows
    grad_first = product * (dot_first - dot_second)
    grad_second = product * (dot_second - dot_first)
    logit_grad = first_hot * grad_first[:, None] + second_hot * grad_second[:, None]
    router_term = jnp.dot(logit_grad, router.astype(jnp.float32).T, precision=lax.Precision.HIGHEST)
    d_tokens = ((expert_sum + router_term) * keep_rows[:, None]).astype(jnp.bfloat16)
    gate_grad = jnp.stack([grad_first, grad_second], axis=1)
    return (d_tokens, gate_grad)


def solution(mesh):
    gathers = mesh.shape["seq"] == 2 and mesh.shape["expert"] == 4 and mesh.shape["mp"] in (2, 4)
    return jax.shard_map(
        gathered_plan if gathers else routed_plan,
        mesh=mesh,
        in_specs=(
            P(("seq", "expert", "mp"), None),
            P(("seq", "expert", "mp"), None),
            P(("seq", "expert", "mp")),
            P(("seq", "expert", "mp"), None),
            P(),
            P("expert", None, ("seq", "mp")),
            P("expert", None, ("seq", "mp")),
            P("expert", ("seq", "mp"), None),
        ),
        out_specs=(P(("seq", "expert", "mp"), None), P(("seq", "expert", "mp"), None)),
        check_vma=False,
    )
```

```python
import functools
import math

import jax
import jax.numpy as jnp
from jax import lax
from jax.experimental import pallas as pl
from jax.experimental.pallas import tpu as pltpu
from jax.sharding import PartitionSpec as P

TOKEN_PART = 512
HIDDEN_PART = 256
COLUMN_PART = 1536
TOKEN_VMEM = 6 * 2 ** 20
GRAD_VMEM = 10 * 2 ** 20
OUTPUT_VMEM = 6 * 2 ** 20


def routed_plan(tokens, out_grad, kept_mask, routes, router, gate_weight, up_weight, down_weight):
    row_count = tokens.shape[0]
    width = tokens.shape[1]
    expert_count = lax.axis_size("expert")
    capacity = max(3 * row_count // 8, 2 * row_count // expert_count)
    logits = jnp.dot(tokens, router, preferred_element_type=jnp.float32)
    columns = lax.broadcasted_iota(jnp.int32, (row_count, expert_count), 1)
    first_hot = (routes[:, 0:1] == columns).astype(jnp.float32)
    second_hot = (routes[:, 1:2] == columns).astype(jnp.float32)
    first_logit = jnp.sum(logits * first_hot, axis=1)
    second_logit = jnp.sum(logits * second_hot, axis=1)
    gate_first = jax.nn.sigmoid(first_logit - second_logit)
    gate_second = jax.nn.sigmoid(second_logit - first_logit)
    keep_rows = kept_mask.astype(jnp.float32)
    chosen = ((first_hot + second_hot) * keep_rows[:, None]).astype(jnp.int32)
    position = jnp.cumsum(chosen, axis=0) - 1
    slot_iota = lax.broadcasted_iota(jnp.int32, (row_count, expert_count, capacity), 2)
    select_mask = (chosen[:, :, None] == 1) & (position[:, :, None] == slot_iota)
    select_bf = select_mask.astype(jnp.bfloat16)
    select_full = select_mask.astype(jnp.float32)
    token_send = jnp.einsum(
        "tec,td->ecd", select_bf, tokens, preferred_element_type=jnp.float32
    ).astype(jnp.bfloat16)
    grad_send = jnp.einsum(
        "tec,td->ecd", select_bf, out_grad, preferred_element_type=jnp.float32
    ).astype(jnp.bfloat16)
    gate_table = first_hot * gate_first[:, None] + second_hot * gate_second[:, None]
    gate_send = jnp.einsum(
        "tec,te->ec", select_full, gate_table, precision=lax.Precision.HIGHEST
    ).astype(jnp.bfloat16)
    token_recv, grad_recv, gate_recv = (
        lax.all_to_all(token_send, "expert", split_axis=0, concat_axis=0, tiled=True),
        lax.all_to_all(grad_send, "expert", split_axis=0, concat_axis=0, tiled=True),
        lax.all_to_all(gate_send, "expert", split_axis=0, concat_axis=0, tiled=True),
    )
    token_all, grad_all, gate_all = (
        lax.all_gather(token_recv, ("seq", "mp"), axis=0, tiled=True),
        lax.all_gather(grad_recv, ("seq", "mp"), axis=0, tiled=True),
        lax.all_gather(gate_recv, ("seq", "mp"), axis=0, tiled=True),
    )
    token_all = token_all.reshape(-1, width)
    grad_all = grad_all.reshape(-1, width)
    gate_all = gate_all.reshape(-1)
    gate_local = gate_weight[0]
    up_local = up_weight[0]
    down_local = down_weight[0]
    pre_gate = jnp.dot(token_all, gate_local, preferred_element_type=jnp.float32)
    pre_up = jnp.dot(token_all, up_local, preferred_element_type=jnp.float32)
    sigma = jax.nn.sigmoid(pre_gate)
    act = pre_gate * sigma
    hidden = act * pre_up
    grad_hidden = jnp.dot(grad_all, down_local.T, preferred_element_type=jnp.float32)
    gate_dot = jnp.sum(grad_hidden * hidden, axis=1)
    scaled = gate_all.astype(jnp.float32)[:, None] * grad_hidden
    grad_gate = (scaled * pre_up * sigma * (1.0 + pre_gate * (1.0 - sigma))).astype(jnp.bfloat16)
    grad_up = (scaled * act).astype(jnp.bfloat16)
    expert_grad = jnp.dot(grad_gate, gate_local.T, preferred_element_type=jnp.float32)
    expert_grad = expert_grad + jnp.dot(grad_up, up_local.T, preferred_element_type=jnp.float32)
    grad_own = lax.psum_scatter(
        expert_grad.astype(jnp.bfloat16), ("seq", "mp"), scatter_dimension=0, tiled=True
    ).astype(jnp.float32)
    dot_own = lax.psum_scatter(gate_dot, ("seq", "mp"), scatter_dimension=0, tiled=True)
    grad_back, dot_back = (
        lax.all_to_all(
            grad_own.reshape(expert_count, capacity, width).astype(jnp.bfloat16),
            "expert",
            split_axis=0,
            concat_axis=0,
            tiled=True,
        ).astype(jnp.float32),
        lax.all_to_all(
            dot_own.reshape(expert_count, capacity).astype(jnp.bfloat16),
            "expert",
            split_axis=0,
            concat_axis=0,
            tiled=True,
        ).astype(jnp.float32),
    )
    expert_sum = jnp.einsum("tec,ecd->td", select_full, grad_back, precision=lax.Precision.HIGHEST)
    dot_table = jnp.einsum("tec,ec->te", select_full, dot_back, precision=lax.Precision.HIGHEST)
    dot_first = jnp.sum(dot_table * first_hot, axis=1)
    dot_second = jnp.sum(dot_table * second_hot, axis=1)
    product = gate_first * gate_second * keep_rows
    grad_first = product * (dot_first - dot_second)
    grad_second = product * (dot_second - dot_first)
    logit_grad = first_hot * grad_first[:, None] + second_hot * grad_second[:, None]
    router_term = jnp.dot(logit_grad, router.astype(jnp.float32).T, precision=lax.Precision.HIGHEST)
    d_tokens = ((expert_sum + router_term) * keep_rows[:, None]).astype(jnp.bfloat16)
    gate_grad = jnp.stack([grad_first, grad_second], axis=1)
    return (d_tokens, gate_grad)

def swap(value, axis, bit):
    return lax.ppermute(value, axis, [(i ^ bit, i) for i in range(lax.axis_size(axis))])


def swap_x(value):
    return swap(value, "seq", 1)


def swap_y(value):
    return swap(value, "expert", 2)


def swap_core(value):
    return swap(value, "expert", 1)


def after_others(values, others):
    return lax.optimization_barrier((values, others))[0]


def gather_z(rows):
    return [rows] + [swap(rows, "mp", k) for k in range(1, lax.axis_size("mp"))]


def gather_near(z_rows, cut):
    rows = jnp.concatenate(z_rows, axis=0)
    low, high = rows[:, :cut], rows[:, cut:]
    return [low, swap_x(low)], [high, swap_y(high)]


def gather_far(low, high):
    return swap_y(jnp.concatenate(low, axis=0)), swap_x(jnp.concatenate(high, axis=0))


def gather_core(low, low_far, high, high_far):
    high_far = jnp.split(high_far, 2, axis=0)
    low = jnp.concatenate(low + [low_far], axis=0)
    high = jnp.concatenate([high[0], high_far[0], high[1], high_far[1]], axis=0)
    return tuple(jnp.concatenate([mine, swap_core(mine)], axis=0) for mine in (low, high))


def scatter_core(kept, sent):
    return kept + swap_core(sent).astype(jnp.float32)


def send(value, exchange):
    return exchange(value.astype(jnp.bfloat16)).astype(jnp.float32)


def scatter_far(total, cut):
    low, low_x, low_y, low_both = jnp.split(total[:, :cut], 4, axis=0)
    high, high_x, high_y, high_both = jnp.split(total[:, cut:], 4, axis=0)
    low_far = send(jnp.concatenate([low_y, low_both], axis=0), swap_y)
    high_far = send(jnp.concatenate([high_x, high_both], axis=0), swap_x)
    return jnp.concatenate([low, low_x], axis=0) + low_far, jnp.concatenate([high, high_y], axis=0) + high_far


def scatter_near(low, high):
    low, low_x = jnp.split(low, 2, axis=0)
    high, high_y = jnp.split(high, 2, axis=0)
    return jnp.concatenate([low + send(low_x, swap_x), high + send(high_y, swap_y)], axis=1)


def scatter_z(total):
    size = lax.axis_size("mp")
    rows = total.shape[0] // size
    result = total[:rows]
    for k in range(1, size):
        result = result + send(total[k * rows:(k + 1) * rows], lambda value: swap(value, "mp", k))
    return result


def product(a, b, b_dim):
    return lax.dot_general(a, b, (((1,), (b_dim,)), ((), ())), preferred_element_type=jnp.float32)


def part_of(length, wanted):
    return math.gcd(length, wanted)


def in_hbm(value):
    return pltpu.with_memory_space_constraint(value, pltpu.HBM)


def fetch_kernel(first, _, *refs):
    count = (len(refs) - 1) // 2
    sems = refs[-1]
    copies = []
    for index in range(count):
        target = refs[count + index]
        source = refs[index].at[0, pl.ds(first, target.shape[0])]
        copies.append(pltpu.make_async_copy(source, target, sems.at[index]))
    for copy in copies:
        copy.start()
    for copy in copies:
        copy.wait()


def fetch(first, length, earlier, *weights):
    shapes = [(length, value.shape[2]) for value in weights]
    return pl.pallas_call(
        functools.partial(fetch_kernel, first),
        out_shape=tuple(pltpu.VMEM(shape, jnp.bfloat16) for shape in shapes),
        in_specs=[pl.BlockSpec(memory_space=pl.ANY)] * (1 + len(weights)),
        out_specs=(pl.BlockSpec(memory_space=pltpu.VMEM),) * len(weights),
        scratch_shapes=[pltpu.SemaphoreType.DMA((len(weights),))],
        compiler_params=pltpu.CompilerParams(vmem_limit_bytes=TOKEN_VMEM),
        cost_estimate=pl.CostEstimate(
            flops=0, bytes_accessed=sum(2 * rows * hidden for rows, hidden in shapes), transcendentals=0
        ),
    )(earlier, *[in_hbm(value) for value in weights])


def token_kernel(offset, length, sources, summed, tokens, gate, up, *refs):
    before, refs = refs[:summed], refs[summed:]
    count = len(sources)
    weights, (pre_gate, pre_up), fetched = refs[:count], refs[count:count + 2], refs[count + 2:2 * count + 2]
    depth = part_of(length, TOKEN_PART)
    copies = []
    for index in range(count):
        source = weights[index].at[0, pl.ds(sources[index], fetched[index].shape[0])]
        copies.append(pltpu.make_async_copy(source, fetched[index], refs[-1].at[index]))
    for copy in copies:
        copy.start()
    pre_gate[...] = before[0][...] if summed else jnp.zeros_like(pre_gate)
    pre_up[...] = before[1][...] if summed else jnp.zeros_like(pre_up)

    @pl.loop(0, length // depth)
    def _(step):
        rows = pl.ds(pl.multiple_of(offset + step * depth, depth), depth)
        pre_gate[...] += product(tokens[:, rows], gate[rows, :], 0)
        pre_up[...] += product(tokens[:, rows], up[rows, :], 0)

    for copy in copies:
        copy.wait()


def multiply_tokens(tokens, gate, up, offset, length, sums=(), wanted=()):
    rows, hidden = tokens.shape[0], gate.shape[1]
    shapes = [(count, value.shape[2]) for value, _, count in wanted]
    sources = tuple(first for _, first, _ in wanted)
    out_shape = (pltpu.VMEM((rows, hidden), jnp.float32),) * 2
    out_shape += tuple(pltpu.VMEM(shape, jnp.bfloat16) for shape in shapes)
    return pl.pallas_call(
        functools.partial(token_kernel, offset, length, sources, len(sums)),
        out_shape=out_shape,
        in_specs=[pl.BlockSpec(memory_space=pltpu.VMEM)] * (3 + len(sums))
        + [pl.BlockSpec(memory_space=pl.ANY)] * len(wanted),
        out_specs=(pl.BlockSpec(memory_space=pltpu.VMEM),) * len(out_shape),
        scratch_shapes=[pltpu.SemaphoreType.DMA((len(wanted),))] if wanted else [],
        compiler_params=pltpu.CompilerParams(vmem_limit_bytes=TOKEN_VMEM),
        cost_estimate=pl.CostEstimate(
            flops=4 * rows * length * hidden, bytes_accessed=2 * rows * length, transcendentals=0
        ),
    )(tokens, gate, up, *sums, *[in_hbm(value) for value, _, _ in wanted])


def grad_kernel(
    expert, low, high, pre_gate, pre_up, down, down_weight, grad_gate, grad_up, dots, gate_rows, dot_sums, rest, sems
):
    table = low.shape[1] - high.shape[1]
    half = high.shape[1]
    ready = down.shape[0]
    depth = part_of(ready, HIDDEN_PART)
    steps = ready // depth

    def copy_of(index):
        rows = pl.ds(pl.multiple_of(index * depth, depth), depth)
        source = pl.ds(pl.multiple_of(ready + index * depth, depth), depth)
        return pltpu.make_async_copy(down_weight.at[0, source], rest.at[rows], sems.at[index])

    for index in range(steps):
        copy_of(index).start()

    lanes = lax.broadcasted_iota(jnp.int32, (low.shape[0], table), 1)
    gate_rows[...] = jnp.sum(
        jnp.where(lanes == expert[0], low[:, :table].astype(jnp.float32), 0.0), axis=1, keepdims=True
    )
    dot_sums[...] = jnp.zeros_like(dot_sums)

    def block(weights, first, step):
        rows = pl.ds(pl.multiple_of(step * depth, depth), depth)
        span = pl.ds(pl.multiple_of(first + step * depth, depth), depth)
        grad_hidden = product(low[:, table:], weights[rows, :half], 1) + product(high[...], weights[rows, half:], 1)
        gates = pre_gate[:, span]
        ups = pre_up[:, span]
        sigma = jax.nn.sigmoid(gates)
        act = gates * sigma
        dot_sums[...] += jnp.sum(grad_hidden * (act * ups), axis=1, keepdims=True)
        scaled = gate_rows[...] * grad_hidden
        grad_gate[:, span] = (scaled * ups * sigma * (1.0 + gates * (1.0 - sigma))).astype(jnp.bfloat16)
        grad_up[:, span] = (scaled * act).astype(jnp.bfloat16)

    @pl.loop(0, steps)
    def _(step):
        block(down, 0, step)

    @pl.loop(0, steps)
    def _(step):
        copy_of(step).wait()
        block(rest, ready, step)

    dots[...] = jnp.where(lanes == expert[0], dot_sums[...], 0.0).astype(jnp.bfloat16)


def multiply_grads(expert, low, high, pre_gate, pre_up, down, down_weight):
    rows, hidden = pre_gate.shape
    width = down_weight.shape[2]
    table = low.shape[1] - high.shape[1]
    return pl.pallas_call(
        grad_kernel,
        out_shape=(
            pltpu.VMEM((rows, hidden), jnp.bfloat16),
            pltpu.VMEM((rows, hidden), jnp.bfloat16),
            pltpu.VMEM((rows, table), jnp.bfloat16),
        ),
        in_specs=[pl.BlockSpec(memory_space=pltpu.SMEM)]
        + [pl.BlockSpec(memory_space=pltpu.VMEM)] * 5
        + [pl.BlockSpec(memory_space=pl.ANY)],
        out_specs=(pl.BlockSpec(memory_space=pltpu.VMEM),) * 3,
        scratch_shapes=[
            pltpu.VMEM((rows, 1), jnp.float32),
            pltpu.VMEM((rows, 1), jnp.float32),
            pltpu.VMEM((hidden // 2, width), jnp.bfloat16),
            pltpu.SemaphoreType.DMA((hidden // 2 // part_of(hidden // 2, HIDDEN_PART),)),
        ],
        compiler_params=pltpu.CompilerParams(vmem_limit_bytes=GRAD_VMEM),
        cost_estimate=pl.CostEstimate(
            flops=2 * rows * width * hidden, bytes_accessed=width * hidden, transcendentals=rows * hidden
        ),
    )(expert, low, high, pre_gate, pre_up, down, in_hbm(down_weight))


def output_kernel(grad_gate, grad_up, gate_copy, up_copy, *refs):
    dots, kept, sent = refs if len(refs) == 3 else (None,) + refs
    rows = kept.shape[0]
    columns = kept.shape[1] - (0 if dots is None else dots.shape[1])
    part = part_of(columns, COLUMN_PART)

    @pl.loop(0, columns // part)
    def _(step):
        span = pl.ds(pl.multiple_of(step * part, part), part)
        result = (product(gate_copy[span, :], grad_gate[...], 1) + product(up_copy[span, :], grad_up[...], 1)).T
        kept[:, span] = result[:rows]
        sent[:, span] = result[rows:].astype(jnp.bfloat16)

    if dots is not None:
        kept[:, columns:] = dots[:rows, :].astype(jnp.float32)
        sent[:, columns:] = dots[rows:, :]


def multiply_outputs(grad_gate, grad_up, gate_copy, up_copy, *dots):
    rows, hidden = grad_gate.shape
    columns = gate_copy.shape[0]
    total = columns + sum(value.shape[1] for value in dots)
    return pl.pallas_call(
        output_kernel,
        out_shape=(
            pltpu.VMEM((rows // 2, total), jnp.float32),
            pltpu.VMEM((rows // 2, total), jnp.bfloat16),
        ),
        in_specs=[pl.BlockSpec(memory_space=pltpu.VMEM)] * (4 + len(dots)),
        out_specs=(pl.BlockSpec(memory_space=pltpu.VMEM),) * 2,
        compiler_params=pltpu.CompilerParams(vmem_limit_bytes=OUTPUT_VMEM),
        cost_estimate=pl.CostEstimate(
            flops=4 * rows * columns * hidden, bytes_accessed=4 * rows * columns, transcendentals=0
        ),
    )(grad_gate, grad_up, gate_copy, up_copy, *dots)


def gathered_plan(tokens, out_grad, kept_mask, routes, router, gate_weight, up_weight, down_weight):
    row_count, width = tokens.shape
    expert_count = lax.axis_size("expert")
    columns = lax.broadcasted_iota(jnp.int32, (row_count, expert_count), 1)
    first_hot = (routes[:, 0:1] == columns).astype(jnp.float32)
    second_hot = (routes[:, 1:2] == columns).astype(jnp.float32)
    keep_rows = kept_mask.astype(jnp.float32)
    half, quarter = width // 2, width // 4
    table = 128
    token_z = gather_z(tokens)
    logits = jnp.dot(tokens, router, preferred_element_type=jnp.float32)
    first_logit = jnp.sum(logits * first_hot, axis=1)
    second_logit = jnp.sum(logits * second_hot, axis=1)
    gate_first = jax.nn.sigmoid(first_logit - second_logit)
    gate_second = jax.nn.sigmoid(second_logit - first_logit)
    gate_table = (first_hot * gate_first[:, None] + second_hot * gate_second[:, None]) * keep_rows[:, None]
    gate_table = jnp.pad(gate_table.astype(jnp.bfloat16), ((0, 0), (0, table - expert_count)))
    grad_z = gather_z(after_others(jnp.concatenate([gate_table, out_grad], axis=1), token_z[1]))
    token_near = lax.optimization_barrier(gather_near(token_z, half))
    token_far = gather_far(*token_near)
    (gate_low,) = fetch(0, half, token_near[1][1], gate_weight)
    (up_low,) = fetch(0, half, token_near[1][1], up_weight)
    grad_near = gather_near(after_others(grad_z, gate_low), half + table)
    grad_far = gather_far(*after_others(grad_near, token_far))
    token_far = after_others(token_far, (gate_low, up_low))
    token_low, token_high = gather_core(token_near[0], token_far[0], token_near[1], token_far[1])
    pre_gate, pre_up, gate_high, up_high = multiply_tokens(
        token_low, gate_low, up_low, 0, half, (), ((gate_weight, half, half), (up_weight, half, half))
    )
    pre_gate, pre_up = multiply_tokens(token_high, gate_high, up_high, 0, quarter, (pre_gate, pre_up))
    grad_far = after_others(grad_far, pre_gate)
    pre_gate, pre_up, down = multiply_tokens(
        token_high, gate_high, up_high, quarter, quarter, (pre_gate, pre_up),
        ((down_weight, 0, down_weight.shape[1] // 2),),
    )
    grad_halves = gather_core(grad_near[0], grad_far[0], grad_near[1], grad_far[1])
    expert = lax.axis_index("expert").astype(jnp.int32).reshape(1)
    grad_gate, grad_up, dots = multiply_grads(expert, *grad_halves, pre_gate, pre_up, down, down_weight)
    kept, sent = multiply_outputs(grad_gate, grad_up, gate_low, up_low, dots)
    chunk = scatter_core(kept, sent)
    kept, sent = multiply_outputs(grad_gate, grad_up, gate_high, up_high)
    chunk = scatter_far(after_others(chunk, sent), half // 2)
    later = scatter_core(kept, sent)
    chunk = scatter_near(*after_others(chunk, later))
    later = scatter_far(later, half // 2)
    chunk = scatter_z(after_others(chunk, later))
    later = scatter_z(scatter_near(*later))
    expert_sum = jnp.concatenate([chunk[:, :half], later], axis=1)
    dot_table = chunk[:, half:half + expert_count]
    dot_first = jnp.sum(dot_table * first_hot, axis=1)
    dot_second = jnp.sum(dot_table * second_hot, axis=1)
    product = gate_first * gate_second * keep_rows
    grad_first = product * (dot_first - dot_second)
    grad_second = product * (dot_second - dot_first)
    logit_grad = first_hot * grad_first[:, None] + second_hot * grad_second[:, None]
    router_term = jnp.dot(logit_grad, router.astype(jnp.float32).T, precision=lax.Precision.HIGHEST)
    d_tokens = ((expert_sum + router_term) * keep_rows[:, None]).astype(jnp.bfloat16)
    gate_grad = jnp.stack([grad_first, grad_second], axis=1)
    return (d_tokens, gate_grad)


def solution(mesh):
    gathers = mesh.shape["seq"] == 2 and mesh.shape["expert"] == 4 and mesh.shape["mp"] in (2, 4)
    return jax.shard_map(
        gathered_plan if gathers else routed_plan,
        mesh=mesh,
        in_specs=(
            P(("seq", "expert", "mp"), None),
            P(("seq", "expert", "mp"), None),
            P(("seq", "expert", "mp")),
            P(("seq", "expert", "mp"), None),
            P(),
            P("expert", None, ("seq", "mp")),
            P("expert", None, ("seq", "mp")),
            P("expert", ("seq", "mp"), None),
        ),
        out_specs=(P(("seq", "expert", "mp"), None), P(("seq", "expert", "mp"), None)),
        check_vma=False,
    )
```

```python
import functools
import math

import jax
import jax.numpy as jnp
from jax import lax
from jax.experimental import pallas as pl
from jax.experimental.pallas import tpu as pltpu
from jax.sharding import PartitionSpec as P

TOKEN_PART = 512
HIDDEN_PART = 256
COLUMN_PART = 1536
TOKEN_VMEM = 6 * 2 ** 20
GRAD_VMEM = 10 * 2 ** 20
OUTPUT_VMEM = 6 * 2 ** 20


def routed_plan(tokens, out_grad, kept_mask, routes, router, gate_weight, up_weight, down_weight):
    row_count = tokens.shape[0]
    width = tokens.shape[1]
    expert_count = lax.axis_size("expert")
    capacity = max(3 * row_count // 8, 2 * row_count // expert_count)
    logits = jnp.dot(tokens, router, preferred_element_type=jnp.float32)
    columns = lax.broadcasted_iota(jnp.int32, (row_count, expert_count), 1)
    first_hot = (routes[:, 0:1] == columns).astype(jnp.float32)
    second_hot = (routes[:, 1:2] == columns).astype(jnp.float32)
    first_logit = jnp.sum(logits * first_hot, axis=1)
    second_logit = jnp.sum(logits * second_hot, axis=1)
    gate_first = jax.nn.sigmoid(first_logit - second_logit)
    gate_second = jax.nn.sigmoid(second_logit - first_logit)
    keep_rows = kept_mask.astype(jnp.float32)
    chosen = ((first_hot + second_hot) * keep_rows[:, None]).astype(jnp.int32)
    position = jnp.cumsum(chosen, axis=0) - 1
    slot_iota = lax.broadcasted_iota(jnp.int32, (row_count, expert_count, capacity), 2)
    select_mask = (chosen[:, :, None] == 1) & (position[:, :, None] == slot_iota)
    select_bf = select_mask.astype(jnp.bfloat16)
    select_full = select_mask.astype(jnp.float32)
    token_send = jnp.einsum(
        "tec,td->ecd", select_bf, tokens, preferred_element_type=jnp.float32
    ).astype(jnp.bfloat16)
    grad_send = jnp.einsum(
        "tec,td->ecd", select_bf, out_grad, preferred_element_type=jnp.float32
    ).astype(jnp.bfloat16)
    gate_table = first_hot * gate_first[:, None] + second_hot * gate_second[:, None]
    gate_send = jnp.einsum(
        "tec,te->ec", select_full, gate_table, precision=lax.Precision.HIGHEST
    ).astype(jnp.bfloat16)
    token_recv, grad_recv, gate_recv = (
        lax.all_to_all(token_send, "expert", split_axis=0, concat_axis=0, tiled=True),
        lax.all_to_all(grad_send, "expert", split_axis=0, concat_axis=0, tiled=True),
        lax.all_to_all(gate_send, "expert", split_axis=0, concat_axis=0, tiled=True),
    )
    token_all, grad_all, gate_all = (
        lax.all_gather(token_recv, ("seq", "mp"), axis=0, tiled=True),
        lax.all_gather(grad_recv, ("seq", "mp"), axis=0, tiled=True),
        lax.all_gather(gate_recv, ("seq", "mp"), axis=0, tiled=True),
    )
    token_all = token_all.reshape(-1, width)
    grad_all = grad_all.reshape(-1, width)
    gate_all = gate_all.reshape(-1)
    gate_local = gate_weight[0]
    up_local = up_weight[0]
    down_local = down_weight[0]
    pre_gate = jnp.dot(token_all, gate_local, preferred_element_type=jnp.float32)
    pre_up = jnp.dot(token_all, up_local, preferred_element_type=jnp.float32)
    sigma = jax.nn.sigmoid(pre_gate)
    act = pre_gate * sigma
    hidden = act * pre_up
    grad_hidden = jnp.dot(grad_all, down_local.T, preferred_element_type=jnp.float32)
    gate_dot = jnp.sum(grad_hidden * hidden, axis=1)
    scaled = gate_all.astype(jnp.float32)[:, None] * grad_hidden
    grad_gate = (scaled * pre_up * sigma * (1.0 + pre_gate * (1.0 - sigma))).astype(jnp.bfloat16)
    grad_up = (scaled * act).astype(jnp.bfloat16)
    expert_grad = jnp.dot(grad_gate, gate_local.T, preferred_element_type=jnp.float32)
    expert_grad = expert_grad + jnp.dot(grad_up, up_local.T, preferred_element_type=jnp.float32)
    grad_own = lax.psum_scatter(
        expert_grad.astype(jnp.bfloat16), ("seq", "mp"), scatter_dimension=0, tiled=True
    ).astype(jnp.float32)
    dot_own = lax.psum_scatter(gate_dot, ("seq", "mp"), scatter_dimension=0, tiled=True)
    grad_back, dot_back = (
        lax.all_to_all(
            grad_own.reshape(expert_count, capacity, width).astype(jnp.bfloat16),
            "expert",
            split_axis=0,
            concat_axis=0,
            tiled=True,
        ).astype(jnp.float32),
        lax.all_to_all(
            dot_own.reshape(expert_count, capacity).astype(jnp.bfloat16),
            "expert",
            split_axis=0,
            concat_axis=0,
            tiled=True,
        ).astype(jnp.float32),
    )
    expert_sum = jnp.einsum("tec,ecd->td", select_full, grad_back, precision=lax.Precision.HIGHEST)
    dot_table = jnp.einsum("tec,ec->te", select_full, dot_back, precision=lax.Precision.HIGHEST)
    dot_first = jnp.sum(dot_table * first_hot, axis=1)
    dot_second = jnp.sum(dot_table * second_hot, axis=1)
    product = gate_first * gate_second * keep_rows
    grad_first = product * (dot_first - dot_second)
    grad_second = product * (dot_second - dot_first)
    logit_grad = first_hot * grad_first[:, None] + second_hot * grad_second[:, None]
    router_term = jnp.dot(logit_grad, router.astype(jnp.float32).T, precision=lax.Precision.HIGHEST)
    d_tokens = ((expert_sum + router_term) * keep_rows[:, None]).astype(jnp.bfloat16)
    gate_grad = jnp.stack([grad_first, grad_second], axis=1)
    return (d_tokens, gate_grad)

def swap(value, axis, bit):
    return lax.ppermute(value, axis, [(i ^ bit, i) for i in range(lax.axis_size(axis))])


def swap_x(value):
    return swap(value, "seq", 1)


def swap_y(value):
    return swap(value, "expert", 2)


def swap_core(value):
    return swap(value, "expert", 1)


def after_others(values, others):
    return lax.optimization_barrier((values, others))[0]


def gather_z(rows):
    return [rows] + [swap(rows, "mp", k) for k in range(1, lax.axis_size("mp"))]


def gather_near(z_rows, cut):
    rows = jnp.concatenate(z_rows, axis=0)
    low, high = rows[:, :cut], rows[:, cut:]
    return [low, swap_x(low)], [high, swap_y(high)]


def gather_far(low, high):
    return swap_y(jnp.concatenate(low, axis=0)), swap_x(jnp.concatenate(high, axis=0))


def gather_core(low, low_far, high, high_far):
    high_far = jnp.split(high_far, 2, axis=0)
    low = jnp.concatenate(low + [low_far], axis=0)
    high = jnp.concatenate([high[0], high_far[0], high[1], high_far[1]], axis=0)
    return tuple(jnp.concatenate([mine, swap_core(mine)], axis=0) for mine in (low, high))


def scatter_core(kept, sent):
    return kept + swap_core(sent).astype(jnp.float32)


def send(value, exchange):
    return exchange(value.astype(jnp.bfloat16)).astype(jnp.float32)


def scatter_far(total, cut):
    low, low_x, low_y, low_both = jnp.split(total[:, :cut], 4, axis=0)
    high, high_x, high_y, high_both = jnp.split(total[:, cut:], 4, axis=0)
    low_far = send(jnp.concatenate([low_y, low_both], axis=0), swap_y)
    high_far = send(jnp.concatenate([high_x, high_both], axis=0), swap_x)
    return jnp.concatenate([low, low_x], axis=0) + low_far, jnp.concatenate([high, high_y], axis=0) + high_far


def scatter_near(low, high):
    low, low_x = jnp.split(low, 2, axis=0)
    high, high_y = jnp.split(high, 2, axis=0)
    return jnp.concatenate([low + send(low_x, swap_x), high + send(high_y, swap_y)], axis=1)


def scatter_z(total):
    size = lax.axis_size("mp")
    rows = total.shape[0] // size
    result = total[:rows]
    for k in range(1, size):
        result = result + send(total[k * rows:(k + 1) * rows], lambda value: swap(value, "mp", k))
    return result


def product(a, b, b_dim):
    return lax.dot_general(a, b, (((1,), (b_dim,)), ((), ())), preferred_element_type=jnp.float32)


def part_of(length, wanted):
    return math.gcd(length, wanted)


def in_hbm(value):
    return pltpu.with_memory_space_constraint(value, pltpu.HBM)


def fetch_kernel(first, _, *refs):
    count = (len(refs) - 1) // 2
    sems = refs[-1]
    copies = []
    for index in range(count):
        target = refs[count + index]
        source = refs[index].at[0, pl.ds(first, target.shape[0])]
        copies.append(pltpu.make_async_copy(source, target, sems.at[index]))
    for copy in copies:
        copy.start()
    for copy in copies:
        copy.wait()


def fetch(first, length, earlier, *weights):
    shapes = [(length, value.shape[2]) for value in weights]
    return pl.pallas_call(
        functools.partial(fetch_kernel, first),
        out_shape=tuple(pltpu.VMEM(shape, jnp.bfloat16) for shape in shapes),
        in_specs=[pl.BlockSpec(memory_space=pl.ANY)] * (1 + len(weights)),
        out_specs=(pl.BlockSpec(memory_space=pltpu.VMEM),) * len(weights),
        scratch_shapes=[pltpu.SemaphoreType.DMA((len(weights),))],
        compiler_params=pltpu.CompilerParams(vmem_limit_bytes=TOKEN_VMEM),
        cost_estimate=pl.CostEstimate(
            flops=0, bytes_accessed=sum(2 * rows * hidden for rows, hidden in shapes), transcendentals=0
        ),
    )(earlier, *[in_hbm(value) for value in weights])


def token_kernel(offset, length, sources, summed, tokens, gate, up, *refs):
    before, refs = refs[:summed], refs[summed:]
    count = len(sources)
    weights, (pre_gate, pre_up), fetched = refs[:count], refs[count:count + 2], refs[count + 2:2 * count + 2]
    depth = part_of(length, TOKEN_PART)
    copies = []
    for index in range(count):
        source = weights[index].at[0, pl.ds(sources[index], fetched[index].shape[0])]
        copies.append(pltpu.make_async_copy(source, fetched[index], refs[-1].at[index]))
    for copy in copies:
        copy.start()
    pre_gate[...] = before[0][...] if summed else jnp.zeros_like(pre_gate)
    pre_up[...] = before[1][...] if summed else jnp.zeros_like(pre_up)

    @pl.loop(0, length // depth)
    def _(step):
        rows = pl.ds(pl.multiple_of(offset + step * depth, depth), depth)
        pre_gate[...] += product(tokens[:, rows], gate[rows, :], 0)
        pre_up[...] += product(tokens[:, rows], up[rows, :], 0)

    for copy in copies:
        copy.wait()


def multiply_tokens(tokens, gate, up, offset, length, sums=(), wanted=()):
    rows, hidden = tokens.shape[0], gate.shape[1]
    shapes = [(count, value.shape[2]) for value, _, count in wanted]
    sources = tuple(first for _, first, _ in wanted)
    out_shape = (pltpu.VMEM((rows, hidden), jnp.float32),) * 2
    out_shape += tuple(pltpu.VMEM(shape, jnp.bfloat16) for shape in shapes)
    return pl.pallas_call(
        functools.partial(token_kernel, offset, length, sources, len(sums)),
        out_shape=out_shape,
        in_specs=[pl.BlockSpec(memory_space=pltpu.VMEM)] * (3 + len(sums))
        + [pl.BlockSpec(memory_space=pl.ANY)] * len(wanted),
        out_specs=(pl.BlockSpec(memory_space=pltpu.VMEM),) * len(out_shape),
        scratch_shapes=[pltpu.SemaphoreType.DMA((len(wanted),))] if wanted else [],
        compiler_params=pltpu.CompilerParams(vmem_limit_bytes=TOKEN_VMEM),
        cost_estimate=pl.CostEstimate(
            flops=4 * rows * length * hidden, bytes_accessed=2 * rows * length, transcendentals=0
        ),
    )(tokens, gate, up, *sums, *[in_hbm(value) for value, _, _ in wanted])


def grad_kernel(
    expert, low, high, pre_gate, pre_up, down, down_weight, grad_gate, grad_up, dots, gate_rows, dot_sums, rest, sems
):
    table = low.shape[1] - high.shape[1]
    half = high.shape[1]
    ready = down.shape[0]
    depth = part_of(ready, HIDDEN_PART)
    steps = ready // depth

    def copy_of(index):
        rows = pl.ds(pl.multiple_of(index * depth, depth), depth)
        source = pl.ds(pl.multiple_of(ready + index * depth, depth), depth)
        return pltpu.make_async_copy(down_weight.at[0, source], rest.at[rows], sems.at[index])

    for index in range(steps):
        copy_of(index).start()

    lanes = lax.broadcasted_iota(jnp.int32, (low.shape[0], table), 1)
    gate_rows[...] = jnp.sum(
        jnp.where(lanes == expert[0], low[:, :table].astype(jnp.float32), 0.0), axis=1, keepdims=True
    )
    dot_sums[...] = jnp.zeros_like(dot_sums)

    def block(weights, first, step):
        rows = pl.ds(pl.multiple_of(step * depth, depth), depth)
        span = pl.ds(pl.multiple_of(first + step * depth, depth), depth)
        grad_hidden = product(low[:, table:], weights[rows, :half], 1) + product(high[...], weights[rows, half:], 1)
        gates = pre_gate[:, span]
        ups = pre_up[:, span]
        sigma = jax.nn.sigmoid(gates)
        act = gates * sigma
        dot_sums[...] += jnp.sum(grad_hidden * (act * ups), axis=1, keepdims=True)
        scaled = gate_rows[...] * grad_hidden
        grad_gate[:, span] = (scaled * ups * sigma * (1.0 + gates * (1.0 - sigma))).astype(jnp.bfloat16)
        grad_up[:, span] = (scaled * act).astype(jnp.bfloat16)

    @pl.loop(0, steps)
    def _(step):
        block(down, 0, step)

    @pl.loop(0, steps)
    def _(step):
        copy_of(step).wait()
        block(rest, ready, step)

    dots[...] = jnp.where(lanes == expert[0], dot_sums[...], 0.0).astype(jnp.bfloat16)


def multiply_grads(expert, low, high, pre_gate, pre_up, down, down_weight):
    rows, hidden = pre_gate.shape
    width = down_weight.shape[2]
    table = low.shape[1] - high.shape[1]
    return pl.pallas_call(
        grad_kernel,
        out_shape=(
            pltpu.VMEM((rows, hidden), jnp.bfloat16),
            pltpu.VMEM((rows, hidden), jnp.bfloat16),
            pltpu.VMEM((rows, table), jnp.bfloat16),
        ),
        in_specs=[pl.BlockSpec(memory_space=pltpu.SMEM)]
        + [pl.BlockSpec(memory_space=pltpu.VMEM)] * 5
        + [pl.BlockSpec(memory_space=pl.ANY)],
        out_specs=(pl.BlockSpec(memory_space=pltpu.VMEM),) * 3,
        scratch_shapes=[
            pltpu.VMEM((rows, 1), jnp.float32),
            pltpu.VMEM((rows, 1), jnp.float32),
            pltpu.VMEM((hidden // 2, width), jnp.bfloat16),
            pltpu.SemaphoreType.DMA((hidden // 2 // part_of(hidden // 2, HIDDEN_PART),)),
        ],
        compiler_params=pltpu.CompilerParams(vmem_limit_bytes=GRAD_VMEM),
        cost_estimate=pl.CostEstimate(
            flops=2 * rows * width * hidden, bytes_accessed=width * hidden, transcendentals=rows * hidden
        ),
    )(expert, low, high, pre_gate, pre_up, down, in_hbm(down_weight))


def output_kernel(grad_gate, grad_up, gate_copy, up_copy, *refs):
    dots, kept, sent = refs if len(refs) == 3 else (None,) + refs
    rows = kept.shape[0]
    columns = kept.shape[1] - (0 if dots is None else dots.shape[1])
    part = part_of(columns, COLUMN_PART)

    @pl.loop(0, columns // part)
    def _(step):
        span = pl.ds(pl.multiple_of(step * part, part), part)
        result = (product(gate_copy[span, :], grad_gate[...], 1) + product(up_copy[span, :], grad_up[...], 1)).T
        kept[:, span] = result[:rows]
        sent[:, span] = result[rows:].astype(jnp.bfloat16)

    if dots is not None:
        kept[:, columns:] = dots[:rows, :].astype(jnp.float32)
        sent[:, columns:] = dots[rows:, :]


def multiply_outputs(grad_gate, grad_up, gate_copy, up_copy, *dots):
    rows, hidden = grad_gate.shape
    columns = gate_copy.shape[0]
    total = columns + sum(value.shape[1] for value in dots)
    return pl.pallas_call(
        output_kernel,
        out_shape=(
            pltpu.VMEM((rows // 2, total), jnp.float32),
            pltpu.VMEM((rows // 2, total), jnp.bfloat16),
        ),
        in_specs=[pl.BlockSpec(memory_space=pltpu.VMEM)] * (4 + len(dots)),
        out_specs=(pl.BlockSpec(memory_space=pltpu.VMEM),) * 2,
        compiler_params=pltpu.CompilerParams(vmem_limit_bytes=OUTPUT_VMEM),
        cost_estimate=pl.CostEstimate(
            flops=4 * rows * columns * hidden, bytes_accessed=4 * rows * columns, transcendentals=0
        ),
    )(grad_gate, grad_up, gate_copy, up_copy, *dots)


def gathered_plan(tokens, out_grad, kept_mask, routes, router, gate_weight, up_weight, down_weight):
    row_count, width = tokens.shape
    expert_count = lax.axis_size("expert")
    columns = lax.broadcasted_iota(jnp.int32, (row_count, expert_count), 1)
    first_hot = (routes[:, 0:1] == columns).astype(jnp.float32)
    second_hot = (routes[:, 1:2] == columns).astype(jnp.float32)
    keep_rows = kept_mask.astype(jnp.float32)
    half, quarter = width // 2, width // 4
    table = 128
    token_z = gather_z(tokens)
    logits = jnp.dot(tokens, router, preferred_element_type=jnp.float32)
    first_logit = jnp.sum(logits * first_hot, axis=1)
    second_logit = jnp.sum(logits * second_hot, axis=1)
    gate_first = jax.nn.sigmoid(first_logit - second_logit)
    gate_second = jax.nn.sigmoid(second_logit - first_logit)
    gate_table = (first_hot * gate_first[:, None] + second_hot * gate_second[:, None]) * keep_rows[:, None]
    gate_table = jnp.pad(gate_table.astype(jnp.bfloat16), ((0, 0), (0, table - expert_count)))
    grad_z = gather_z(after_others(jnp.concatenate([gate_table, out_grad], axis=1), token_z[1]))
    token_near = lax.optimization_barrier(gather_near(token_z, half))
    token_far = gather_far(*token_near)
    (gate_low,) = fetch(0, half, token_near[1][1], gate_weight)
    (up_low,) = fetch(0, half, token_near[1][1], up_weight)
    grad_near = gather_near(after_others(grad_z, gate_low), half + table)
    grad_far = gather_far(*after_others(grad_near, token_far))
    token_far = after_others(token_far, (gate_low, up_low))
    token_low, token_high = gather_core(token_near[0], token_far[0], token_near[1], token_far[1])
    pre_gate, pre_up, gate_high, up_high = multiply_tokens(
        token_low, gate_low, up_low, 0, half, (), ((gate_weight, half, half), (up_weight, half, half))
    )
    pre_gate, pre_up, down = multiply_tokens(
        token_high, gate_high, up_high, 0, quarter, (pre_gate, pre_up),
        ((down_weight, 0, down_weight.shape[1] // 2),),
    )
    grad_far = after_others(grad_far, pre_gate)
    pre_gate, pre_up = multiply_tokens(token_high, gate_high, up_high, quarter, quarter, (pre_gate, pre_up))
    grad_halves = gather_core(grad_near[0], grad_far[0], grad_near[1], grad_far[1])
    expert = lax.axis_index("expert").astype(jnp.int32).reshape(1)
    grad_gate, grad_up, dots = multiply_grads(expert, *grad_halves, pre_gate, pre_up, down, down_weight)
    kept, sent = multiply_outputs(grad_gate, grad_up, gate_low, up_low, dots)
    chunk = scatter_core(kept, sent)
    kept, sent = multiply_outputs(grad_gate, grad_up, gate_high, up_high)
    chunk = scatter_far(after_others(chunk, sent), half // 2)
    later = scatter_core(kept, sent)
    chunk = scatter_near(*after_others(chunk, later))
    later = scatter_far(later, half // 2)
    chunk = scatter_z(after_others(chunk, later))
    later = scatter_z(scatter_near(*later))
    expert_sum = jnp.concatenate([chunk[:, :half], later], axis=1)
    dot_table = chunk[:, half:half + expert_count]
    dot_first = jnp.sum(dot_table * first_hot, axis=1)
    dot_second = jnp.sum(dot_table * second_hot, axis=1)
    product = gate_first * gate_second * keep_rows
    grad_first = product * (dot_first - dot_second)
    grad_second = product * (dot_second - dot_first)
    logit_grad = first_hot * grad_first[:, None] + second_hot * grad_second[:, None]
    router_term = jnp.dot(logit_grad, router.astype(jnp.float32).T, precision=lax.Precision.HIGHEST)
    d_tokens = ((expert_sum + router_term) * keep_rows[:, None]).astype(jnp.bfloat16)
    gate_grad = jnp.stack([grad_first, grad_second], axis=1)
    return (d_tokens, gate_grad)


def solution(mesh):
    gathers = mesh.shape["seq"] == 2 and mesh.shape["expert"] == 4 and mesh.shape["mp"] in (2, 4)
    return jax.shard_map(
        gathered_plan if gathers else routed_plan,
        mesh=mesh,
        in_specs=(
            P(("seq", "expert", "mp"), None),
            P(("seq", "expert", "mp"), None),
            P(("seq", "expert", "mp")),
            P(("seq", "expert", "mp"), None),
            P(),
            P("expert", None, ("seq", "mp")),
            P("expert", None, ("seq", "mp")),
            P("expert", ("seq", "mp"), None),
        ),
        out_specs=(P(("seq", "expert", "mp"), None), P(("seq", "expert", "mp"), None)),
        check_vma=False,
    )
```
